32 devices in a mesh: dp: 8 (over z, x), fsdp: 4 (over y, core).
Axes of the slice: x: 2, y: 2, z: 4, core: 2. Of those that a mesh axis runs over, the one named last changes fastest.
Arguments:
- features: float32 [64, 512, 192], P(('dp', 'fsdp')), may hold values from -6 to 6
- widths: int32 [64], P(('dp', 'fsdp')), may hold values from 5 to 512, as said below
- params_one: float32 [296576], P(('dp', 'fsdp')), as said below
- params_two: float32 [296960], P(('dp', 'fsdp')), as said below
- out_grad: float32 [64, 512, 192], P(('dp', 'fsdp')), may hold values from -6 to 6
Outputs:
- activations: float32 [64, 512, 192], P(('dp', 'fsdp'))
- grad_features: float32 [64, 512, 192], P(('dp', 'fsdp'))
- grad_one: float32 [296576], P(('dp', 'fsdp'))
- grad_two: float32 [296960], P(('dp', 'fsdp'))
The draws below stay inside these ranges and needn't reach their ends.
Inputs may be any that keep to these rules, and one draw needn't show every extreme that they name: `widths`: some row has all 512 slots live and some row has 5. `params_one`: laid out as the first step says; the padding entries are zero. `params_two`: laid out as the first step says; the padding entries are zero.
All inputs are finite; a program needn't handle non-finite values.
Results may differ from the reference program's by a relative error of at most 0.014.
The reference program's roundings to bfloat16 on the way count: a program that leaves them out, or rounds other values in their place, can miss the bound.
Values may be sent and summed in bfloat16 or wider, within the bound.
A program may use at most 64 MiB of HBM per device.

```python
import math
import jax
import jax.numpy as jnp
from jax import lax

D = 192
HEADS = 8
FF = 256
HEAD_DIM = 24
SEQ = 512
ROWS = 64
FLAT_ONE = 296576
FLAT_TWO = 296960


def layout_drawn(leading):
    entries = [('w_query', (D, D)), ('w_key', (D, D)), ('w_value', (D, D)), ('w_output', (D, D)), ('b_query', (D,)), ('b_value', (D,)), ('b_output', (D,))]
    if not leading:
        entries = entries + [('gain_attn', (D,)), ('bias_attn', (D,))]
    return entries + [('gain_ffn', (D,)), ('bias_ffn', (D,)), ('w_inner', (D, 2 * FF)), ('b_inner', (2 * FF,)), ('w_outer', (FF, D)), ('b_outer', (D,))]


def entry_law(entry_name):
    if entry_name in ('w_query', 'w_key', 'w_value', 'w_inner'):
        return (D ** (-0.5), 0.0)
    if entry_name == 'w_output':
        return (4.0 * D ** (-0.5), 0.0)
    if entry_name == 'w_outer':
        return (1.5 * FF ** (-0.5), 0.0)
    if entry_name in ('gain_attn', 'gain_ffn'):
        return (0.25, 1.0)
    return (0.3, 0.0)


def shaped_params(noise, leading):
    scales = []
    shifts = []
    used_total = 0
    for entry_name, entry_shape in layout_drawn(leading):
        length = math.prod(entry_shape)
        spread, center = entry_law(entry_name)
        scales.append(jnp.full((length,), spread, jnp.float32))
        shifts.append(jnp.full((length,), center, jnp.float32))
        used_total = used_total + length
    padding = noise.shape[0] - used_total
    scales.append(jnp.zeros((padding,), jnp.float32))
    shifts.append(jnp.zeros((padding,), jnp.float32))
    return noise * jnp.concatenate(scales) + jnp.concatenate(shifts)


def draw_params_one(key, part):
    key = jax.random.fold_in(key, 11)
    noise = jax.random.normal(key, (FLAT_ONE,), jnp.float32)
    return shaped_params(noise, True)


def draw_params_two(key, part):
    key = jax.random.fold_in(key, 23)
    noise = jax.random.normal(key, (FLAT_TWO,), jnp.float32)
    return shaped_params(noise, False)


def draw_widths(key, part):
    key = jax.random.fold_in(key, 5)
    first_key, second_key = jax.random.split(key)
    counts = jax.random.randint(first_key, (ROWS,), 5, SEQ + 1, jnp.int32)
    chosen = jax.random.randint(second_key, (), 0, ROWS, jnp.int32)
    counts = counts.at[chosen].set(SEQ)
    return counts.at[(chosen + 1) % ROWS].set(5)


def block_scale(key, extent, cuts, least, top_value):
    level = 1.0
    for position, parts in cuts:
        steps = jax.random.uniform(jax.random.fold_in(jax.random.fold_in(key, 6), position), (parts,), jnp.float32, least / len(cuts), top_value / len(cuts))
        level = level * jnp.repeat(jnp.exp(steps), extent[position] // parts).reshape((-1,) + (1,) * (len(extent) - 1 - position))
    return level


def centred(key, dims, deviation, bound, shards=(), kind=jnp.bfloat16):
    level = block_scale(key, dims, shards, -0.22, 0.18) if shards else 1.0
    array = jax.random.normal(key, dims, jnp.float32) * deviation * level
    return jnp.minimum(jnp.maximum(array, -bound), bound).astype(kind)


def setup_inputs(seed: int = 0) -> dict:
    keys = jax.random.split(jax.random.key(seed), 6)
    features = centred(keys[0], (ROWS, SEQ, D), 1.0, 6.0, ((0, 32),), jnp.float32)
    widths = draw_widths(jax.random.fold_in(keys[5], 71), 0)
    params_one = draw_params_one(jax.random.fold_in(keys[5], 71), 0)
    params_two = draw_params_two(jax.random.fold_in(keys[5], 71), 0)
    out_grad = centred(keys[4], (ROWS, SEQ, D), 1.0, 6.0, ((0, 32),), jnp.float32)
    return {"features": features, "widths": widths, "params_one": params_one, "params_two": params_two, "out_grad": out_grad}


@jax.custom_vjp
def low(v):
    return lax.optimization_barrier(v.astype(jnp.bfloat16)).astype(jnp.float32)

@jax.custom_vjp
def low_back(v):
    return v

def low_keep(v):
    return (low(v), None)

def low_pass(kept, grad):
    return (grad,)

def back_keep(v):
    return (v, None)

def back_low(kept, grad):
    return (low(grad),)
low.defvjp(low_keep, low_pass)
low_back.defvjp(back_keep, back_low)
epsilon = 1e-05
masked_score = -1e+30

def layout(leading):
    entries = [('w_query', (D, D)), ('w_key', (D, D)), ('w_value', (D, D)), ('w_output', (D, D)), ('b_query', (D,)), ('b_value', (D,)), ('b_output', (D,))]
    if not leading:
        entries = entries + [('gain_attn', (D,)), ('bias_attn', (D,))]
    return entries + [('gain_ffn', (D,)), ('bias_ffn', (D,)), ('w_inner', (D, 2 * FF)), ('b_inner', (2 * FF,)), ('w_outer', (FF, D)), ('b_outer', (D,))]

def unpack(flat_vec, leading):
    params = {}
    offset = 0
    for entry_name, entry_shape in layout(leading):
        length = math.prod(entry_shape)
        params[entry_name] = flat_vec[offset:offset + length].reshape(entry_shape)
        offset = offset + length
    return params

def matmul(left, right):
    return jnp.dot(left, right, precision=lax.Precision.HIGHEST, preferred_element_type=jnp.float32)

def layer_norm(values, gain, bias):
    center = values - lax.optimization_barrier(jnp.mean(values, axis=-1, keepdims=True))
    inverse = lax.rsqrt(lax.optimization_barrier(jnp.mean(center * center, axis=-1, keepdims=True)) + epsilon)
    return center * inverse * gain + bias

def attend_row(packed):
    query_row, key_row, value_row, row_width = packed
    raw_scores = jnp.einsum('qhd,khd->hqk', query_row, key_row, precision=lax.Precision.HIGHEST) * HEAD_DIM ** (-0.5)
    positions = lax.broadcasted_iota(jnp.int32, (1, 1, SEQ), 2)
    scores = low_back(jnp.where(positions < row_width, raw_scores, masked_score))
    soft_low = low(jax.nn.softmax(scores, axis=-1))
    return jnp.einsum('hqk,khd->qhd', soft_low, value_row, precision=lax.Precision.HIGHEST)

def block(inputs, params, widths, leading):
    flat_in = inputs.reshape(ROWS * SEQ, D)
    if leading:
        attn_in = flat_in
    else:
        attn_in = layer_norm(flat_in, params['gain_attn'], params['bias_attn'])
    attn_low = low(attn_in)
    query_all = low(low_back(matmul(attn_low, params['w_query']) + params['b_query']))
    key_all = low(low_back(matmul(attn_low, params['w_key'])))
    value_all = low(low_back(matmul(attn_low, params['w_value']) + params['b_value']))
    split_shape = (ROWS, SEQ, HEADS, HEAD_DIM)
    mixed = lax.map(jax.checkpoint(attend_row), (query_all.reshape(split_shape), key_all.reshape(split_shape), value_all.reshape(split_shape), widths))
    mixed_low = low(low_back(mixed.reshape(ROWS * SEQ, D)))
    middle = flat_in + low_back(matmul(mixed_low, params['w_output']) + params['b_output'])
    ffn_low = low(layer_norm(middle, params['gain_ffn'], params['bias_ffn']))
    inner = low_back(matmul(ffn_low, params['w_inner']) + params['b_inner'])
    hidden_low = low(inner[:, :FF] * jax.nn.silu(inner[:, FF:]))
    output = middle + low_back(matmul(hidden_low, params['w_outer']) + params['b_outer'])
    return output.reshape(inputs.shape)

def forward(features, params_one, params_two, widths):
    middle = block(features, unpack(low(params_one), True), widths, True)
    return block(middle, unpack(low(params_two), False), widths, False)

def reference(features, widths, params_one, params_two, out_grad):

    def apply_net(inputs, flat_one, flat_two):
        return forward(inputs, flat_one, flat_two, widths)
    activations, pullback = jax.vjp(apply_net, features, params_one, params_two)
    grad_features, grad_one, grad_two = pullback(out_grad)
    return (activations, grad_features, grad_one, grad_two)
```

```python
import functools
import math

import jax
import jax.numpy as jnp
from jax import lax
from jax.experimental import pallas as pl
from jax.experimental.pallas import tpu as pltpu
from jax.sharding import PartitionSpec as P

D = 192
HEADS = 8
FF = 256
HEAD_DIM = 24
PAD = 32
AUG = 208
HID = 272
CHUNK = 256
EPS = 1e-5
MASK = -4e30
SCALE = HEAD_DIM**-0.5
LOG2E = math.log2(math.e)
MATS = 1152
BF = jnp.bfloat16
F32 = jnp.float32


def nn(left, right):
    return lax.dot_general(left, right, (((1,), (0,)), ((), ())), preferred_element_type=F32)


def nt(left, right):
    return lax.dot_general(left, right, (((1,), (1,)), ((), ())), preferred_element_type=F32)


def tn(left, right):
    return lax.dot_general(left, right, (((0,), (0,)), ((), ())), preferred_element_type=F32)


def lanes_low(rows):
    return lax.broadcasted_iota(jnp.int32, (rows, 128), 1) < 64


def half_turn(values):
    return pltpu.roll(values, 64, 1)


def read_wide(flat, start, rows, pair):
    count = rows // 2
    first = flat[pl.ds(start, count, stride=3), :]
    second = flat[pl.ds(start + 1, count, stride=3), :]
    third = half_turn(flat[pl.ds(start + 2, count, stride=3), :])
    pair[0, pl.ds(0, count, stride=2), :] = first
    pair[1, pl.ds(0, count, stride=2), :] = second
    pair[0, pl.ds(1, count, stride=2), :] = jnp.where(lanes_low(count), half_turn(second), third)
    pair[1, pl.ds(1, count, stride=2), :] = third
    return jnp.concatenate([pair[0, :rows, :], pair[1, :rows, :64]], axis=1)


def write_wide(flat, start, values, pair):
    rows = values.shape[0]
    count = rows // 2
    pair[0, :rows, :] = values[:, :128]
    pair[1, :rows, :64] = values[:, 128:]
    low = lanes_low(count)
    even_low = pair[0, pl.ds(0, count, stride=2), :]
    even_high = pair[1, pl.ds(0, count, stride=2), :]
    odd_low = half_turn(pair[0, pl.ds(1, count, stride=2), :])
    odd_high = half_turn(pair[1, pl.ds(1, count, stride=2), :])
    flat[pl.ds(start, count, stride=3), :] = even_low
    flat[pl.ds(start + 1, count, stride=3), :] = jnp.where(low, even_high, odd_low)
    flat[pl.ds(start + 2, count, stride=3), :] = jnp.where(low, odd_low, odd_high)


def vector_names(leading):
    names = ["b_query", "b_value", "b_output"]
    if not leading:
        names = names + ["gain_attn", "bias_attn"]
    return names + ["gain_ffn", "bias_ffn"]


def spread(leading):
    row = lax.broadcasted_iota(jnp.int32, (HEADS * PAD, D), 0)
    col = lax.broadcasted_iota(jnp.int32, (HEADS * PAD, D), 1)
    inside = (row & (PAD - 1)) < HEAD_DIM
    source = (row >> 5) * HEAD_DIM + (row & (PAD - 1))
    return jnp.where(inside & (source == col), 1.0, 0.0).astype(BF)


def identity(size):
    row = lax.broadcasted_iota(jnp.int32, (size, size), 0)
    col = lax.broadcasted_iota(jnp.int32, (size, size), 1)
    return jnp.where(row == col, 1.0, 0.0).astype(BF)


def unit_entry(column):
    row = lax.broadcasted_iota(jnp.int32, (HEADS * PAD, AUG), 0)
    col = lax.broadcasted_iota(jnp.int32, (HEADS * PAD, AUG), 1)
    return jnp.where(((row & (PAD - 1)) == HEAD_DIM) & (col == column), 1.0, 0.0)


def column(row_vec):
    return jnp.broadcast_to(row_vec, (128, D)).T


def augment(matrix, bias):
    width = matrix.shape[1]
    return jnp.concatenate([matrix, bias, jnp.zeros((AUG - D - 1, width), F32)], axis=0).astype(BF)


def unpack(flat, w, leading, pair, tail):
    names = vector_names(leading)
    vecs = read_wide(flat, MATS, len(names) + 1, pair)
    vec = {name: vecs[i : i + 1, :] for i, name in enumerate(names)}
    put = spread(leading)
    zero_row = jnp.zeros((1, D), F32)
    for i, (bias, spare) in enumerate((("b_query", D), (None, D + 1), ("b_value", D))):
        mat = read_wide(flat, 288 * i, D, pair)
        aug = augment(mat, vec[bias] if bias else zero_row)
        w.qkv[i] = aug[:D]
        w.qkv_t[i] = (nt(put, aug) + unit_entry(spare)).astype(BF)
    aug = augment(read_wide(flat, 864, D, pair), vec["b_output"])
    w.out_t[...] = nt(identity(D), aug).astype(BF)
    w.out_pad[...] = nn(put, aug[:D]).astype(BF)
    start = MATS + len(names) * 3 // 2
    count = 1160
    turned = half_turn(flat[pl.ds(start, count + 8), :])
    tail[:count, :] = jnp.where(lanes_low(count), turned[:count], turned[1 : count + 1])
    aug = augment(
        jnp.concatenate([tail[pl.ds(j, D, stride=4), :] for j in range(4)], axis=1),
        jnp.concatenate([tail[768 + j : 769 + j, :] for j in range(4)], axis=1),
    )
    w.inner[...] = aug[:D]
    for half in range(2):
        cols = slice(half * FF, (half + 1) * FF)
        w.inner_t[cols, :] = nt(identity(FF), aug[:, cols]).astype(BF)
    outer = read_wide(tail, 772, FF, pair).astype(BF)
    w.outer[...] = outer
    w.outer_t[...] = nt(identity(D), outer).astype(BF)
    b_outer = jnp.concatenate([tail[1156:1157, :], tail[1157:1158, :64]], axis=1)
    w.cols[0] = column(b_outer)
    w.cols[1] = column(vec["gain_ffn"])
    w.cols[2] = column(vec["bias_ffn"])
    if not leading:
        w.cols[3] = column(vec["gain_attn"])
        w.cols[4] = column(vec["bias_attn"])


class Group:
    def __init__(self, **refs):
        self.__dict__.update(refs)


def wide(col):
    return jnp.concatenate([col] * (CHUNK // 128), axis=1)


def norm(values):
    center = values - jnp.sum(values, axis=0, keepdims=True) * (1.0 / D)
    inverse = lax.rsqrt(jnp.sum(center * center, axis=0, keepdims=True) * (1.0 / D) + EPS)
    return center * inverse, inverse


def norm_back(grad, normed, inverse, gain):
    scaled = grad * gain
    mean = jnp.sum(scaled, axis=0, keepdims=True) * (1.0 / D)
    cross = jnp.sum(scaled * normed, axis=0, keepdims=True) * (1.0 / D)
    return inverse * (scaled - mean - normed * cross)


def chunks(tokens, body, unroll=True):
    count = tokens // CHUNK

    def step(i, carry):
        body(pl.ds(pl.multiple_of(i * CHUNK, CHUNK), CHUNK))
        return carry

    if unroll is True:
        for i in range(count):
            body(pl.ds(i * CHUNK, CHUNK))
    else:
        lax.fori_loop(0, count, step, 0, unroll=unroll)


def attend_forward(s, a, seq, row_count):
    units = row_count * HEADS

    def place(u):
        row = u // HEADS if isinstance(u, int) else lax.div(u, HEADS)
        head = u - row * HEADS
        if isinstance(u, int):
            return head, pl.ds(head * PAD, PAD), pl.ds(row * seq, seq)
        return (
            head,
            pl.ds(pl.multiple_of(head * PAD, PAD), PAD),
            pl.ds(pl.multiple_of(row * seq, seq), seq),
        )

    def score(u, slot):
        _, rows, cols = place(u)
        key = a.key[rows, cols]
        keys = jnp.concatenate([key, key], axis=0)
        query = jnp.concatenate([a.query_hi[rows, cols], a.query_lo[rows, cols]], axis=0)
        scores = tn(keys, query)
        s.scores[slot] = scores
        s.top[slot] = jnp.max(scores, axis=0, keepdims=True)

    def expo(u, slot):
        a.expo[u] = jnp.exp2(s.scores[slot] - s.top[slot]).astype(BF)

    def mix(u):
        head, rows, cols = place(u)
        total = nn(a.value[rows, cols], a.expo[u])
        inverse = 1.0 / total[HEAD_DIM : HEAD_DIM + 1]
        mixed = total * inverse
        a.mixed[rows, cols] = mixed
        a.total[pl.ds(head, 1), cols] = inverse
        start = head * HEAD_DIM
        if not isinstance(u, int):
            start = pl.multiple_of(start, 8)
        s.compact[0, pl.ds(start, HEAD_DIM), cols] = mixed[:HEAD_DIM]

    def step(i, carry):
        mix(i - 2)
        expo(i - 1, (i - 1) & 1)
        score(i, i & 1)
        return carry

    score(0, 0)
    expo(0, 0)
    score(1, 1)
    lax.fori_loop(2, units, step, 0, unroll=2)
    mix(units - 2)
    expo(units - 1, (units - 1) % 2)
    mix(units - 1)


def attend_backward(s, a, seq, row_count):
    units = row_count * HEADS

    def step(u, carry):
        row = lax.div(u, HEADS)
        head = u - row * HEADS
        rows = pl.ds(pl.multiple_of(head * PAD, PAD), PAD)
        cols = pl.ds(pl.multiple_of(row * seq, seq), seq)
        value = a.value[rows, cols]
        grad_hi = s.grad_hi[rows, cols]
        values = jnp.concatenate([value, value], axis=0)
        grads = jnp.concatenate([grad_hi, s.grad_lo[rows, cols]], axis=0)
        expo = a.expo[u]
        grad_soft = tn(values, grads)
        grad_scores = (grad_soft * expo.astype(F32)).astype(BF)
        compact = pl.ds(pl.multiple_of(head * HEAD_DIM, 8), HEAD_DIM)
        s.compact[2, compact, cols] = nt(grad_hi, expo)[:HEAD_DIM]
        s.compact[1, compact, cols] = nt(a.query[rows, cols], grad_scores)[:HEAD_DIM] * SCALE
        s.compact[0, compact, cols] = nn(a.key[rows, cols], grad_scores)[:HEAD_DIM] * SCALE
        return carry

    lax.fori_loop(0, units, step, 0, unroll=4)


def block_forward(s, a, w, source, target, leading, seq, row_count):
    tokens = seq * row_count

    def project(cols):
        x = source[:, cols]
        if not leading:
            normed, inverse = norm(x)
            a.normed_attn[:, cols] = normed
            a.inverse_attn[:, cols] = inverse
            x = normed * wide(w.cols[3]) + wide(w.cols[4])
        a.attn_low[:D, cols] = x.astype(BF)
        low = a.attn_low[:, cols]
        query = nn(w.qkv_t[0], low).astype(BF)
        a.query[:, cols] = query
        scaled = query.astype(F32) * (SCALE * LOG2E)
        high = scaled.astype(BF)
        a.query_hi[:, cols] = high
        a.query_lo[:, cols] = (scaled - high.astype(F32)).astype(BF)
        a.key[:, cols] = nn(w.qkv_t[1], low).astype(BF)
        a.value[:, cols] = nn(w.qkv_t[2], low).astype(BF)

    chunks(tokens, project)
    attend_forward(s, a, seq, row_count)

    def feed(cols):
        a.mixed_low[:D, cols] = s.compact[0, :, cols].astype(BF)
        middle = source[:, cols] + nn(w.out_t[...], a.mixed_low[:, cols])
        normed, inverse = norm(middle)
        a.normed_ffn[:, cols] = normed
        a.inverse_ffn[:, cols] = inverse
        a.ffn_low[:D, cols] = (normed * wide(w.cols[1]) + wide(w.cols[2])).astype(BF)
        low = a.ffn_low[:, cols]
        linear = nn(w.inner_t[:FF, :], low)
        gate = nn(w.inner_t[FF:, :], low)
        sigmoid = 1.0 / (1.0 + jnp.exp2(gate * (-LOG2E)))
        silu = gate * sigmoid
        a.silu[:, cols] = silu
        a.slope[:, cols] = linear * sigmoid * (1.0 + gate * (1.0 - sigmoid))
        hidden = (linear * silu).astype(BF)
        a.hidden[:FF, cols] = hidden
        target(cols, middle + nn(w.outer_t[...], hidden) + wide(w.cols[0]))

    chunks(tokens, feed)


def block_backward(s, a, w, grad, target, leading, seq, row_count, flat, pair, tail):
    tokens = seq * row_count
    s.sums[...] = jnp.zeros_like(s.sums)

    def feed(cols):
        g = grad[:, cols]
        low = g.astype(BF)
        s.grad_branch[:, cols] = low
        grad_hidden = nn(w.outer[...], low)
        grad_linear = (grad_hidden * a.silu[:, cols]).astype(BF)
        grad_gate = (grad_hidden * a.slope[:, cols]).astype(BF)
        s.grad_inner[:FF, cols] = grad_linear
        s.grad_inner[FF:, cols] = grad_gate
        u = nn(w.inner[:, :FF], grad_linear) + nn(w.inner[:, FF:], grad_gate)
        normed = a.normed_ffn[:, cols]
        s.sums[0] += u * normed
        s.sums[1] += u
        middle = g + norm_back(u, normed, a.inverse_ffn[:, cols], wide(w.cols[1]))
        s.grad_middle[:, cols] = middle
        low = middle.astype(BF)
        s.grad_attn[:, cols] = low
        grad_mixed = nn(w.out_pad[...], low).astype(BF).astype(F32)
        for head in range(HEADS):
            rows = slice(head * PAD, (head + 1) * PAD)
            part = grad_mixed[rows]
            dot = jnp.sum(part * a.mixed[rows, cols], axis=0, keepdims=True)
            spare = lax.broadcasted_iota(jnp.int32, (PAD, CHUNK), 0) == HEAD_DIM
            part = jnp.where(spare, -dot, part) * a.total[head : head + 1, cols]
            high = part.astype(BF)
            s.grad_hi[rows, cols] = high
            s.grad_lo[rows, cols] = (part - high.astype(F32)).astype(BF)

    chunks(tokens, feed)
    names = vector_names(leading)
    vecs = {}
    grads = nt(a.hidden[...], s.grad_branch[...])
    write_wide(tail, 8 + 772, grads[:FF], pair)
    tail[8 + 1156 : 8 + 1157, :] = grads[FF : FF + 1, :128]
    tail[8 + 1157 : 8 + 1158, :64] = grads[FF : FF + 1, 128:]
    tail[8 + 1157 : 8 + 1158, 64:] = jnp.zeros((1, 64), F32)
    tail[8 + 1158 :, :] = jnp.zeros_like(tail[8 + 1158 :, :])
    grads = nt(a.ffn_low[...], s.grad_inner[...])
    for j in range(4):
        cols = slice(128 * j, 128 * j + 128)
        tail[pl.ds(8 + j, D, stride=4), :] = grads[:D, cols]
        tail[8 + 768 + j : 8 + 769 + j, :] = grads[D : D + 1, cols]
    vecs["gain_ffn"] = sum_lanes(s.sums[0])
    vecs["bias_ffn"] = sum_lanes(s.sums[1])
    tail[7:8, 64:] = vecs["bias_ffn"][:, 128:]
    start = MATS + len(names) * 3 // 2
    count = flat.shape[0] - start
    turned = half_turn(tail[pl.ds(0, count + 8), :])
    flat[pl.ds(start, count), :] = jnp.where(
        lanes_low(count), turned[7 : 7 + count], turned[8 : 8 + count]
    )
    grads = nt(a.mixed_low[...], s.grad_attn[...])
    write_wide(flat, 864, grads[:D], pair)
    vecs["b_output"] = grads[D : D + 1]
    attend_backward(s, a, seq, row_count)

    s.sums[...] = jnp.zeros_like(s.sums)

    def project(cols):
        total = None
        for i in range(3):
            low = s.compact[i, :, cols].astype(BF)
            s.grad_qkv[i, :, cols] = low
            term = nn(w.qkv[i], low)
            total = term if total is None else total + term
        if leading:
            target(cols, s.grad_middle[:, cols] + total)
        else:
            normed = a.normed_attn[:, cols]
            s.sums[0] += total * normed
            s.sums[1] += total
            back = norm_back(total, normed, a.inverse_attn[:, cols], wide(w.cols[3]))
            target(cols, s.grad_middle[:, cols] + back)

    chunks(tokens, project)
    for i, bias in enumerate(("b_query", None, "b_value")):
        grads = nt(a.attn_low[...], s.grad_qkv[i])
        write_wide(flat, 288 * i, grads[:D], pair)
        if bias:
            vecs[bias] = grads[D : D + 1]
    if not leading:
        vecs["gain_attn"] = sum_lanes(s.sums[0])
        vecs["bias_attn"] = sum_lanes(s.sums[1])
    last = MATS + len(names) * 3 // 2
    keep = flat[last : last + 8, :]
    stack = jnp.concatenate([vecs[name] for name in names] + [jnp.zeros((1, D), F32)], axis=0)
    write_wide(flat, MATS, stack, pair)
    flat[last : last + 8, :] = keep


def sum_lanes(values):
    total = values[:, :128]
    for start in range(128, values.shape[1], 128):
        total = total + values[:, start : start + 128]
    return jnp.sum(total.T, axis=0, keepdims=True)


def weight_shapes():
    return dict(
        qkv=((3, D, D), BF),
        qkv_t=((3, HEADS * PAD, AUG), BF),
        out_t=((D, AUG), BF),
        out_pad=((HEADS * PAD, D), BF),
        inner=((D, 2 * FF), BF),
        inner_t=((2 * FF, AUG), BF),
        outer=((FF, D), BF),
        outer_t=((D, FF), BF),
        cols=((5, D, 128), F32),
    )


def kept_shapes(tokens, seq, row_count):
    return dict(
        attn_low=((AUG, tokens), BF),
        query=((HEADS * PAD, tokens), BF),
        query_hi=((HEADS * PAD, tokens), BF),
        query_lo=((HEADS * PAD, tokens), BF),
        key=((HEADS * PAD, tokens), BF),
        value=((HEADS * PAD, tokens), BF),
        expo=((row_count * HEADS, seq, seq), BF),
        mixed=((HEADS * PAD, tokens), F32),
        total=((HEADS, tokens), F32),
        mixed_low=((AUG, tokens), BF),
        normed_ffn=((D, tokens), F32),
        inverse_ffn=((1, tokens), F32),
        ffn_low=((AUG, tokens), BF),
        silu=((FF, tokens), F32),
        slope=((FF, tokens), F32),
        hidden=((HID, tokens), BF),
    )


def norm_shapes(tokens):
    return dict(normed_attn=((D, tokens), F32), inverse_attn=((1, tokens), F32))


def shared_shapes(tokens, seq):
    return dict(
        scores=((2, seq, seq), F32),
        top=((2, 1, seq), F32),
        compact=((3, D, tokens), F32),
        grad_hi=((HEADS * PAD, tokens), BF),
        grad_lo=((HEADS * PAD, tokens), BF),
        grad_branch=((D, tokens), BF),
        grad_inner=((2 * FF, tokens), BF),
        grad_middle=((D, tokens), F32),
        grad_attn=((D, tokens), BF),
        grad_qkv=((3, D, tokens), BF),
        sums=((2, D, CHUNK), F32),
        grad_next=((D, tokens), F32),
        input_one=((D, tokens), F32),
        input_two=((D, tokens), F32),
        pair=((2, FF, 128), F32),
        tail=((1176, 128), F32),
    )


def fill_spare(group, widths, seq, row_count):
    tokens = seq * row_count
    row = lax.broadcasted_iota(jnp.int32, (AUG - D, tokens), 0)
    ones = jnp.where(row == 0, 1.0, 0.0)
    slot = lax.broadcasted_iota(jnp.int32, (AUG - D, seq), 1)
    masks = [jnp.where(slot < widths[r], 0.0, MASK) for r in range(row_count)]
    mask = jnp.where(row == 1, jnp.concatenate(masks, axis=1), 0.0)
    group.attn_low[D:, :] = (ones + mask).astype(BF)
    group.mixed_low[D:, :] = ones.astype(BF)
    group.ffn_low[D:, :] = ones.astype(BF)
    group.hidden[FF:, :] = ones.astype(BF)
MESH_ID = pl.DeviceIdType.MESH


class Plan:
    def __init__(self, mesh_shape):
        self.dp, self.fs = mesh_shape["dp"], mesh_shape["fsdp"]
        self.line = 2 ** ((self.dp.bit_length()) // 2)
        self.low = self.dp // self.line
        self.peers = self.low * self.fs // 2
        self.count = self.dp * self.fs

    def here(self):
        dp, fs = lax.axis_index("dp"), lax.axis_index("fsdp")
        half = self.fs // 2
        return dp // self.low, (dp % self.low) * half + fs // 2, fs % 2

    def device(self, hi, q, c):
        half = self.fs // 2
        return (hi * self.low + q // half, (q % half) * 2 + c)

    def shard(self, hi, q, c):
        return (hi * self.peers + q) * 2 + c

    def partners(self):
        hi, q, c = self.here()
        return (
            [self.device((hi + d) % self.line, q, c) for d in range(1, self.line)]
            + [self.device(hi, (q + d) % self.peers, c) for d in range(1, self.peers)]
            + [self.device(hi, q, 1 - c)]
        )

    def greet(self):
        barrier = pltpu.get_barrier_semaphore()
        others = self.partners()
        for other in others:
            pl.semaphore_signal(barrier, 1, device_id=other, device_id_type=MESH_ID)
        pl.semaphore_wait(barrier, len(others))


def piece_rows(length):
    return -(-(length + 127) // 2048) * 16


def send(source, target, sems, index, device):
    copy = pltpu.make_async_remote_copy(
        source, target, sems.at[0, index], sems.at[1, index], device_id=device, device_id_type=MESH_ID
    )
    copy.start()
    return copy


def place_shard(x, offset):
    turned = pltpu.roll(x, offset, 1)
    before = jnp.concatenate([jnp.zeros((1, 128), x.dtype), turned[:-1]], axis=0)
    lane = lax.broadcasted_iota(jnp.int32, x.shape, 1)
    return jnp.where(lane >= offset, turned, before)


def lift_shard(x, offset):
    turned = pltpu.roll(x, lax.rem(128 - offset, 128), 1)
    after = jnp.concatenate([turned[1:], turned[:1]], axis=0)
    lane = lax.broadcasted_iota(jnp.int32, x.shape, 1)
    return jnp.where(lane < 128 - offset, turned, after)


class Gather:
    def __init__(self, plan, sems, held, length):
        self.plan, self.sems, self.held, self.length = plan, sems, held, length

    def begin(self, shard):
        p = self.plan
        hi, q, c = p.here()
        offset = lax.rem(p.shard(hi, q, c) * self.length, 128)
        self.held[c, q, hi] = place_shard(shard, offset).astype(BF)
        mine = self.held.at[c, q, hi]
        self.along = [
            send(mine, mine, self.sems, d, p.device((hi + d) % p.line, q, c)) for d in range(1, p.line)
        ]

    def spread(self):
        p = self.plan
        hi, q, c = p.here()
        for copy in self.along:
            copy.wait_recv()
        mine = self.held.at[c, q]
        base = p.line
        self.across = [
            send(mine, mine, self.sems, base + d, p.device(hi, (q + d) % p.peers, c))
            for d in range(1, p.peers)
        ]
        self.pair = [send(mine, mine, self.sems, base + p.peers, p.device(hi, q, 1 - c))]

    def mirror(self):
        p = self.plan
        hi, q, c = p.here()
        base = p.line + p.peers
        for d, copy in enumerate(self.across, 1):
            copy.wait_recv()
            piece = self.held.at[c, (q - d + p.peers) % p.peers]
            self.pair.append(send(piece, piece, self.sems, base + d, p.device(hi, q, 1 - c)))

    def finish(self):
        for copy in self.pair:
            copy.wait_recv()
        for copy in self.along + self.across + self.pair:
            copy.wait_send()

    def flatten(self, flat):
        p = self.plan
        rows = self.held.shape[3]
        flat[0:8, :] = jnp.zeros((8, 128), F32)
        for hi in range(p.line):
            for q in range(p.peers):
                for c in range(2):
                    start = p.shard(hi, q, c) * self.length // 128
                    piece = self.held[c, q, hi].astype(F32)
                    flat[start : start + 1, :] += piece[:1]
                    flat[start + 1 : start + rows, :] = piece[1:]


def gather_sems(plan):
    return pltpu.SemaphoreType.DMA((2, plan.line + 2 * plan.peers))


class Reduce:
    def __init__(self, plan, sems, refs, length):
        self.plan, self.sems, self.r, self.length = plan, sems, refs, length
        self.sent = []

    def pack(self, flat):
        p, r = self.plan, self.r
        rows = r.mine.shape[3]
        for hi in range(p.line):
            for q in range(p.peers):
                for c in range(2):
                    start = p.shard(hi, q, c) * self.length // 128
                    r.mine[c, q, hi] = flat[start : start + rows, :].astype(BF)

    def begin(self):
        p, r = self.plan, self.r
        hi, q, c = p.here()
        self.pair = send(r.mine.at[1 - c], r.pair, self.sems, 0, p.device(hi, q, 1 - c))
        self.sent.append(self.pair)

    def across(self):
        p, r = self.plan, self.r
        hi, q, c = p.here()
        self.pair.wait_recv()
        r.both[...] = (r.mine[c].astype(F32) + r.pair[...].astype(F32)).astype(BF)
        self.peers = [
            send(
                r.both.at[(q + d) % p.peers], r.peers.at[d], self.sems, d, p.device(hi, (q + d) % p.peers, c)
            )
            for d in range(1, p.peers)
        ]
        self.sent += self.peers

    def along(self):
        p, r = self.plan, self.r
        hi, q, c = p.here()
        total = r.both[q].astype(F32)
        for d, copy in enumerate(self.peers, 1):
            copy.wait_recv()
            total = total + r.peers[d].astype(F32)
        r.plane[...] = total.astype(BF)
        self.lines = [
            send(
                r.plane.at[(hi + d) % p.line],
                r.line.at[d],
                self.sems,
                p.peers + d,
                p.device((hi + d) % p.line, q, c),
            )
            for d in range(1, p.line)
        ]
        self.sent += self.lines

    def finish(self):
        p, r = self.plan, self.r
        hi, q, c = p.here()
        total = r.plane[hi].astype(F32)
        for d, copy in enumerate(self.lines, 1):
            copy.wait_recv()
            total = total + r.line[d].astype(F32)
        for copy in self.sent:
            copy.wait_send()
        offset = lax.rem(p.shard(hi, q, c) * self.length, 128)
        return lift_shard(total, offset)


def reduce_shapes(plan, rows):
    return dict(
        mine=((2, plan.peers, plan.line, rows, 128), BF),
        pair=((plan.peers, plan.line, rows, 128), BF),
        both=((plan.peers, plan.line, rows, 128), BF),
        peers=((plan.peers, plan.line, rows, 128), BF),
        plane=((plan.line, rows, 128), BF),
        line=((plan.line, rows, 128), BF),
    )


def reduce_sems(plan):
    return pltpu.SemaphoreType.DMA((2, plan.line + plan.peers))
def vmem():
    return pl.BlockSpec(memory_space=pltpu.VMEM)


def scratch(*dicts):
    shapes, names = [], []
    for entry in dicts:
        names.append(list(entry))
        shapes += [pltpu.VMEM(*entry[name]) for name in entry]
    return shapes, names


def grouped(names, refs):
    it = iter(refs)
    return [Group(**{name: next(it) for name in entry}) for entry in names]


def gather_kernel(plan, lengths, names, one, two, flat_one, flat_two, sem_one, sem_two, held_one, held_two):
    plan.greet()
    gathers = [
        Gather(plan, sem_one, held_one, lengths[0]),
        Gather(plan, sem_two, held_two, lengths[1]),
    ]
    for g, shard in zip(gathers, (one, two)):
        g.begin(shard[...])
    for g in gathers:
        g.spread()
    for g in gathers:
        g.mirror()
    for g, flat in zip(gathers, (flat_one, flat_two)):
        g.finish()
        g.flatten(flat)


def core_kernel(seq, row_count, names, widths, features, out_grad, flat_one, flat_two, *refs):
    activations, grad_features, grad_one, grad_two = refs[:4]
    w_one, w_two, a_one, a_two, s = grouped(names, refs[4:])
    tokens = seq * row_count
    unpack(flat_one, w_one, True, s.pair, s.tail)
    unpack(flat_two, w_two, False, s.pair, s.tail)
    live = [widths[r] for r in range(row_count)]
    for a in (a_one, a_two):
        fill_spare(a, live, seq, row_count)

    def load(cols):
        s.input_one[:, cols] = features[cols, :].T
        s.grad_next[:, cols] = out_grad[cols, :].T

    chunks(tokens, load)

    def to_two(cols, values):
        s.input_two[:, cols] = values

    def to_activations(cols, values):
        activations[cols, :] = values.T

    def to_next(cols, values):
        s.grad_next[:, cols] = values

    def to_features(cols, values):
        grad_features[cols, :] = values.T

    block_forward(s, a_one, w_one, s.input_one, to_two, True, seq, row_count)
    block_forward(s, a_two, w_two, s.input_two, to_activations, False, seq, row_count)
    back = (seq, row_count)
    block_backward(s, a_two, w_two, s.grad_next, to_next, False, *back, grad_two, s.pair, s.tail)
    block_backward(s, a_one, w_one, s.grad_next, to_features, True, *back, grad_one, s.pair, s.tail)


def reduce_kernel(plan, lengths, names, flat_one, flat_two, one, two, sem_one, sem_two, *refs):
    r_one, r_two = grouped(names, refs)
    plan.greet()
    reduces = [Reduce(plan, sem_two, r_two, lengths[1]), Reduce(plan, sem_one, r_one, lengths[0])]
    for r, flat in zip(reduces, (flat_two, flat_one)):
        r.pack(flat)
        r.begin()
    for r in reduces:
        r.across()
    for r in reduces:
        r.along()
    for r, out in zip(reduces, (two, one)):
        out[...] = r.finish()


def params(**more):
    return pltpu.CompilerParams(vmem_limit_bytes=62 * 2**20, **more)


def on_device(plan, features, widths, params_one, params_two, out_grad):
    row_count, seq, _ = features.shape
    tokens = row_count * seq
    lengths = [params_one.shape[0], params_two.shape[0]]
    rows = [piece_rows(length) for length in lengths]
    flat_rows = [plan.count * length // 128 for length in lengths]
    room = max(2360, max(flat_rows) + max(rows) + 16) // 8 * 8
    padded = [
        jnp.pad(shard, (0, r * 128 - shard.shape[0])).reshape(r, 128)
        for shard, r in zip((params_one, params_two), rows)
    ]
    held = [pltpu.VMEM((2, plan.peers, plan.line, r, 128), BF) for r in rows]
    flats = pl.pallas_call(
        functools.partial(gather_kernel, plan, lengths, None),
        out_shape=[jax.ShapeDtypeStruct((room, 128), F32)] * 2,
        in_specs=[vmem()] * 2,
        out_specs=[vmem()] * 2,
        scratch_shapes=[gather_sems(plan)] * 2 + held,
        compiler_params=params(collective_id=0, has_side_effects=True),
        name="gather",
    )(*padded)
    kept = kept_shapes(tokens, seq, row_count)
    shapes, names = scratch(
        weight_shapes(),
        weight_shapes(),
        kept,
        {**kept, **norm_shapes(tokens)},
        shared_shapes(tokens, seq),
    )
    flat = jax.ShapeDtypeStruct((tokens, D), F32)
    activations, grad_features, grad_one, grad_two = pl.pallas_call(
        functools.partial(core_kernel, seq, row_count, names),
        out_shape=[flat, flat] + [jax.ShapeDtypeStruct((r, 128), F32) for r in flat_rows],
        in_specs=[pl.BlockSpec(memory_space=pltpu.SMEM)] + [vmem()] * 4,
        out_specs=[vmem()] * 4,
        scratch_shapes=shapes,
        compiler_params=params(),
        name="core",
    )(widths, features.reshape(tokens, D), out_grad.reshape(tokens, D), *flats)
    grads = [jnp.pad(g, ((0, room - g.shape[0]), (0, 0))) for g in (grad_one, grad_two)]
    shapes, names = scratch(*[reduce_shapes(plan, r) for r in rows])
    shards = pl.pallas_call(
        functools.partial(reduce_kernel, plan, lengths, names),
        out_shape=[jax.ShapeDtypeStruct((r, 128), F32) for r in rows],
        in_specs=[vmem()] * 2,
        out_specs=[vmem()] * 2,
        scratch_shapes=[reduce_sems(plan)] * 2 + shapes,
        compiler_params=params(collective_id=1, has_side_effects=True),
        name="reduce",
    )(*grads)
    shards = [g.reshape(-1)[:length] for g, length in zip(shards, lengths)]
    back = features.shape
    return (activations.reshape(back), grad_features.reshape(back), *shards)


def solution(mesh):
    plan = Plan(dict(mesh.shape))
    rows = P(("dp", "fsdp"), None, None)
    flat = P(("dp", "fsdp"))
    return jax.shard_map(
        functools.partial(on_device, plan),
        mesh=mesh,
        in_specs=(rows, flat, flat, flat, rows),
        out_specs=(rows, rows, flat, flat),
        check_vma=False,
    )
```

```python
import functools
import math

import jax
import jax.numpy as jnp
from jax import lax
from jax.experimental import pallas as pl
from jax.experimental.pallas import tpu as pltpu
from jax.sharding import PartitionSpec as P

D = 192
HEADS = 8
FF = 256
HEAD_DIM = 24
PAD = 32
AUG = 208
HID = 272
CHUNK = 256
EPS = 1e-5
MASK = -4e30
SCALE = HEAD_DIM**-0.5
LOG2E = math.log2(math.e)
MATS = 1152
BF = jnp.bfloat16
F32 = jnp.float32


def nn(left, right):
    return lax.dot_general(left, right, (((1,), (0,)), ((), ())), preferred_element_type=F32)


def nt(left, right):
    return lax.dot_general(left, right, (((1,), (1,)), ((), ())), preferred_element_type=F32)


def tn(left, right):
    return lax.dot_general(left, right, (((0,), (0,)), ((), ())), preferred_element_type=F32)


def lanes_low(rows):
    return lax.broadcasted_iota(jnp.int32, (rows, 128), 1) < 64


def half_turn(values):
    return pltpu.roll(values, 64, 1)


def read_wide(flat, start, rows, pair):
    count = rows // 2
    first = flat[pl.ds(start, count, stride=3), :]
    second = flat[pl.ds(start + 1, count, stride=3), :]
    third = half_turn(flat[pl.ds(start + 2, count, stride=3), :])
    pair[0, pl.ds(0, count, stride=2), :] = first
    pair[1, pl.ds(0, count, stride=2), :] = second
    pair[0, pl.ds(1, count, stride=2), :] = jnp.where(lanes_low(count), half_turn(second), third)
    pair[1, pl.ds(1, count, stride=2), :] = third
    return jnp.concatenate([pair[0, :rows, :], pair[1, :rows, :64]], axis=1)


def write_wide(flat, start, values, pair):
    rows = values.shape[0]
    count = rows // 2
    pair[0, :rows, :] = values[:, :128]
    pair[1, :rows, :64] = values[:, 128:]
    low = lanes_low(count)
    even_low = pair[0, pl.ds(0, count, stride=2), :]
    even_high = pair[1, pl.ds(0, count, stride=2), :]
    odd_low = half_turn(pair[0, pl.ds(1, count, stride=2), :])
    odd_high = half_turn(pair[1, pl.ds(1, count, stride=2), :])
    flat[pl.ds(start, count, stride=3), :] = even_low
    flat[pl.ds(start + 1, count, stride=3), :] = jnp.where(low, even_high, odd_low)
    flat[pl.ds(start + 2, count, stride=3), :] = jnp.where(low, odd_low, odd_high)


def vector_names(leading):
    names = ["b_query", "b_value", "b_output"]
    if not leading:
        names = names + ["gain_attn", "bias_attn"]
    return names + ["gain_ffn", "bias_ffn"]


def spread():
    row = lax.broadcasted_iota(jnp.int32, (HEADS * PAD, D), 0)
    col = lax.broadcasted_iota(jnp.int32, (HEADS * PAD, D), 1)
    inside = (row & (PAD - 1)) < HEAD_DIM
    source = (row >> 5) * HEAD_DIM + (row & (PAD - 1))
    return jnp.where(inside & (source == col), 1.0, 0.0).astype(BF)


def identity(size):
    row = lax.broadcasted_iota(jnp.int32, (size, size), 0)
    col = lax.broadcasted_iota(jnp.int32, (size, size), 1)
    return jnp.where(row == col, 1.0, 0.0).astype(BF)


def unit_entry(column):
    row = lax.broadcasted_iota(jnp.int32, (HEADS * PAD, AUG), 0)
    col = lax.broadcasted_iota(jnp.int32, (HEADS * PAD, AUG), 1)
    return jnp.where(((row & (PAD - 1)) == HEAD_DIM) & (col == column), 1.0, 0.0)


def column(row_vec):
    return jnp.broadcast_to(row_vec, (128, D)).T


def augment(matrix, bias):
    width = matrix.shape[1]
    return jnp.concatenate([matrix, bias, jnp.zeros((AUG - D - 1, width), F32)], axis=0).astype(BF)


def unpack_vectors(flat, leading, pair):
    names = vector_names(leading)
    vecs = read_wide(flat, MATS, len(names) + 1, pair)
    return {name: vecs[i : i + 1, :] for i, name in enumerate(names)}


def unpack_attention(flat, w, leading, pair):
    vec = unpack_vectors(flat, leading, pair)
    put = spread()
    zero_row = jnp.zeros((1, D), F32)
    for i, (bias, spare) in enumerate((("b_query", D), (None, D + 1), ("b_value", D))):
        mat = read_wide(flat, 288 * i, D, pair)
        aug = augment(mat, vec[bias] if bias else zero_row)
        w.qkv[i] = aug[:D]
        w.qkv_t[i] = (nt(put, aug) + unit_entry(spare)).astype(BF)
    if not leading:
        w.cols[3] = column(vec["gain_attn"])
        w.cols[4] = column(vec["bias_attn"])


def unpack_rest(flat, w, leading, pair, tail):
    names = vector_names(leading)
    vec = unpack_vectors(flat, leading, pair)
    put = spread()
    aug = augment(read_wide(flat, 864, D, pair), vec["b_output"])
    w.out_t[...] = nt(identity(D), aug).astype(BF)
    w.out_pad[...] = nn(put, aug[:D]).astype(BF)
    start = MATS + len(names) * 3 // 2
    count = 1160
    turned = half_turn(flat[pl.ds(start, count + 8), :])
    tail[:count, :] = jnp.where(lanes_low(count), turned[:count], turned[1 : count + 1])
    aug = augment(
        jnp.concatenate([tail[pl.ds(j, D, stride=4), :] for j in range(4)], axis=1),
        jnp.concatenate([tail[768 + j : 769 + j, :] for j in range(4)], axis=1),
    )
    w.inner[...] = aug[:D]
    for half in range(2):
        cols = slice(half * FF, (half + 1) * FF)
        w.inner_t[cols, :] = nt(identity(FF), aug[:, cols]).astype(BF)
    outer = read_wide(tail, 772, FF, pair).astype(BF)
    w.outer[...] = outer
    w.outer_t[...] = nt(identity(D), outer).astype(BF)
    b_outer = jnp.concatenate([tail[1156:1157, :], tail[1157:1158, :64]], axis=1)
    w.cols[0] = column(b_outer)
    w.cols[1] = column(vec["gain_ffn"])
    w.cols[2] = column(vec["bias_ffn"])


class Group:
    def __init__(self, **refs):
        self.__dict__.update(refs)


def wide(col):
    return jnp.concatenate([col] * (CHUNK // 128), axis=1)


def norm(values):
    center = values - jnp.sum(values, axis=0, keepdims=True) * (1.0 / D)
    inverse = lax.rsqrt(jnp.sum(center * center, axis=0, keepdims=True) * (1.0 / D) + EPS)
    return center * inverse, inverse


def norm_back(grad, normed, inverse, gain):
    scaled = grad * gain
    mean = jnp.sum(scaled, axis=0, keepdims=True) * (1.0 / D)
    cross = jnp.sum(scaled * normed, axis=0, keepdims=True) * (1.0 / D)
    return inverse * (scaled - mean - normed * cross)


def chunks(tokens, body, unroll=True):
    count = tokens // CHUNK

    def step(i, carry):
        body(pl.ds(pl.multiple_of(i * CHUNK, CHUNK), CHUNK))
        return carry

    if unroll is True:
        for i in range(count):
            body(pl.ds(i * CHUNK, CHUNK))
    else:
        lax.fori_loop(0, count, step, 0, unroll=unroll)


def attend_forward(s, a, seq, row_count, between):
    units = row_count * HEADS

    def place(u):
        row = u // HEADS if isinstance(u, int) else lax.div(u, HEADS)
        head = u - row * HEADS
        if isinstance(u, int):
            return head, pl.ds(head * PAD, PAD), pl.ds(row * seq, seq)
        return (
            head,
            pl.ds(pl.multiple_of(head * PAD, PAD), PAD),
            pl.ds(pl.multiple_of(row * seq, seq), seq),
        )

    def score(u, slot):
        _, rows, cols = place(u)
        key = a.key[rows, cols]
        keys = jnp.concatenate([key, key], axis=0)
        query = jnp.concatenate([a.query_hi[rows, cols], a.query_lo[rows, cols]], axis=0)
        scores = tn(keys, query)
        s.scores[slot] = scores
        s.top[slot] = jnp.max(scores, axis=0, keepdims=True)

    def expo(u, slot):
        a.expo[u] = jnp.exp2(s.scores[slot] - s.top[slot]).astype(BF)

    def mix(u):
        head, rows, cols = place(u)
        total = nn(a.value[rows, cols], a.expo[u])
        inverse = 1.0 / total[HEAD_DIM : HEAD_DIM + 1]
        mixed = total * inverse
        a.mixed[rows, cols] = mixed
        a.total[pl.ds(head, 1), cols] = inverse
        start = head * HEAD_DIM
        if not isinstance(u, int):
            start = pl.multiple_of(start, 8)
        s.compact[0, pl.ds(start, HEAD_DIM), cols] = mixed[:HEAD_DIM]

    def step(i, carry):
        mix(i - 2)
        expo(i - 1, (i - 1) & 1)
        score(i, i & 1)
        return carry

    score(0, 0)
    expo(0, 0)
    score(1, 1)
    half = units // 2
    lax.fori_loop(2, half, step, 0, unroll=2)
    between()
    lax.fori_loop(half, units, step, 0, unroll=2)
    mix(units - 2)
    expo(units - 1, (units - 1) % 2)
    mix(units - 1)


def attend_backward(s, a, seq, row_count, between):
    units = row_count * HEADS

    def step(u, carry):
        row = lax.div(u, HEADS)
        head = u - row * HEADS
        rows = pl.ds(pl.multiple_of(head * PAD, PAD), PAD)
        cols = pl.ds(pl.multiple_of(row * seq, seq), seq)
        value = a.value[rows, cols]
        grad_hi = s.grad_hi[rows, cols]
        values = jnp.concatenate([value, value], axis=0)
        grads = jnp.concatenate([grad_hi, s.grad_lo[rows, cols]], axis=0)
        expo = a.expo[u]
        grad_soft = tn(values, grads)
        grad_scores = (grad_soft * expo.astype(F32)).astype(BF)
        compact = pl.ds(pl.multiple_of(head * HEAD_DIM, 8), HEAD_DIM)
        s.compact[2, compact, cols] = nt(grad_hi, expo)[:HEAD_DIM]
        s.compact[1, compact, cols] = nt(a.query[rows, cols], grad_scores)[:HEAD_DIM] * SCALE
        s.compact[0, compact, cols] = nn(a.key[rows, cols], grad_scores)[:HEAD_DIM] * SCALE
        return carry

    half = units // 2
    lax.fori_loop(0, half, step, 0, unroll=4)
    between()
    lax.fori_loop(half, units, step, 0, unroll=4)


def forward_project(s, a, w, source, leading, tokens):
    def body(cols):
        x = source[:, cols]
        if not leading:
            normed, inverse = norm(x)
            a.normed_attn[:, cols] = normed
            a.inverse_attn[:, cols] = inverse
            x = normed * wide(w.cols[3]) + wide(w.cols[4])
        a.attn_low[:D, cols] = x.astype(BF)
        low = a.attn_low[:, cols]
        query = nn(w.qkv_t[0], low).astype(BF)
        a.query[:, cols] = query
        scaled = query.astype(F32) * (SCALE * LOG2E)
        high = scaled.astype(BF)
        a.query_hi[:, cols] = high
        a.query_lo[:, cols] = (scaled - high.astype(F32)).astype(BF)
        a.key[:, cols] = nn(w.qkv_t[1], low).astype(BF)
        a.value[:, cols] = nn(w.qkv_t[2], low).astype(BF)

    chunks(tokens, body)


def forward_feed(s, a, w, source, target, tokens):
    def body(cols):
        a.mixed_low[:D, cols] = s.compact[0, :, cols].astype(BF)
        middle = source[:, cols] + nn(w.out_t[...], a.mixed_low[:, cols])
        normed, inverse = norm(middle)
        a.normed_ffn[:, cols] = normed
        a.inverse_ffn[:, cols] = inverse
        a.ffn_low[:D, cols] = (normed * wide(w.cols[1]) + wide(w.cols[2])).astype(BF)
        low = a.ffn_low[:, cols]
        linear = nn(w.inner_t[:FF, :], low)
        gate = nn(w.inner_t[FF:, :], low)
        sigmoid = 1.0 / (1.0 + jnp.exp2(gate * (-LOG2E)))
        silu = gate * sigmoid
        a.silu[:, cols] = silu
        a.slope[:, cols] = linear * sigmoid * (1.0 + gate * (1.0 - sigmoid))
        hidden = (linear * silu).astype(BF)
        a.hidden[:FF, cols] = hidden
        target[:, cols] = middle + nn(w.outer_t[...], hidden) + wide(w.cols[0])

    chunks(tokens, body)


def backward_feed(s, a, w, grad, tokens):
    s.sums[...] = jnp.zeros_like(s.sums)

    def body(cols):
        g = grad[:, cols]
        low = g.astype(BF)
        s.grad_branch[:, cols] = low
        grad_hidden = nn(w.outer[...], low)
        grad_linear = (grad_hidden * a.silu[:, cols]).astype(BF)
        grad_gate = (grad_hidden * a.slope[:, cols]).astype(BF)
        s.grad_inner[:FF, cols] = grad_linear
        s.grad_inner[FF:, cols] = grad_gate
        u = nn(w.inner[:, :FF], grad_linear) + nn(w.inner[:, FF:], grad_gate)
        normed = a.normed_ffn[:, cols]
        s.sums[0] += u * normed
        s.sums[1] += u
        middle = g + norm_back(u, normed, a.inverse_ffn[:, cols], wide(w.cols[1]))
        s.grad_middle[:, cols] = middle
        low = middle.astype(BF)
        s.grad_attn[:, cols] = low
        grad_mixed = nn(w.out_pad[...], low).astype(BF).astype(F32)
        for head in range(HEADS):
            rows = slice(head * PAD, (head + 1) * PAD)
            part = grad_mixed[rows]
            dot = jnp.sum(part * a.mixed[rows, cols], axis=0, keepdims=True)
            spare = lax.broadcasted_iota(jnp.int32, (PAD, CHUNK), 0) == HEAD_DIM
            part = jnp.where(spare, -dot, part) * a.total[head : head + 1, cols]
            high = part.astype(BF)
            s.grad_hi[rows, cols] = high
            s.grad_lo[rows, cols] = (part - high.astype(F32)).astype(BF)

    chunks(tokens, body)


def write_vectors(flat, leading, vecs, pair):
    names = vector_names(leading)
    last = MATS + len(names) * 3 // 2
    keep = flat[last : last + 8, :]
    zero = jnp.zeros((1, D), F32)
    stack = jnp.concatenate([vecs.get(name, zero) for name in names] + [zero], axis=0)
    write_wide(flat, MATS, stack, pair)
    flat[last : last + 8, :] = keep


def grads_feed(s, a, leading, flat, pair, tail):
    names = vector_names(leading)
    vecs = {}
    grads = nt(a.hidden[...], s.grad_branch[...])
    write_wide(tail, 8 + 772, grads[:FF], pair)
    tail[8 + 1156 : 8 + 1157, :] = grads[FF : FF + 1, :128]
    tail[8 + 1157 : 8 + 1158, :64] = grads[FF : FF + 1, 128:]
    tail[8 + 1157 : 8 + 1158, 64:] = jnp.zeros((1, 64), F32)
    tail[8 + 1158 :, :] = jnp.zeros_like(tail[8 + 1158 :, :])
    grads = nt(a.ffn_low[...], s.grad_inner[...])
    for j in range(4):
        cols = slice(128 * j, 128 * j + 128)
        tail[pl.ds(8 + j, D, stride=4), :] = grads[:D, cols]
        tail[8 + 768 + j : 8 + 769 + j, :] = grads[D : D + 1, cols]
    vecs["gain_ffn"] = sum_lanes(s.sums[0])
    vecs["bias_ffn"] = sum_lanes(s.sums[1])
    tail[7:8, 64:] = vecs["bias_ffn"][:, 128:]
    start = MATS + len(names) * 3 // 2
    count = 1160
    turned = half_turn(tail[pl.ds(0, count + 8), :])
    flat[pl.ds(start, count), :] = jnp.where(
        lanes_low(count), turned[7 : 7 + count], turned[8 : 8 + count]
    )
    grads = nt(a.mixed_low[...], s.grad_attn[...])
    write_wide(flat, 864, grads[:D], pair)
    vecs["b_output"] = grads[D : D + 1]
    write_vectors(flat, leading, vecs, pair)
    return vecs


def grads_attention(s, a, leading, flat, pair, vecs):
    for i, bias in enumerate(("b_query", None, "b_value")):
        s.grad_qkv[i] = s.compact[i].astype(BF)
        grads = nt(a.attn_low[...], s.grad_qkv[i])
        write_wide(flat, 288 * i, grads[:D], pair)
        if bias:
            vecs[bias] = grads[D : D + 1]


def backward_project(s, a, w, target, leading, tokens):
    s.sums[...] = jnp.zeros_like(s.sums)

    def body(cols):
        total = nn(w.qkv[0], s.grad_qkv[0, :, cols])
        total = total + nn(w.qkv[1], s.grad_qkv[1, :, cols])
        total = total + nn(w.qkv[2], s.grad_qkv[2, :, cols])
        if not leading:
            normed = a.normed_attn[:, cols]
            s.sums[0] += total * normed
            s.sums[1] += total
            total = norm_back(total, normed, a.inverse_attn[:, cols], wide(w.cols[3]))
        target[:, cols] = s.grad_middle[:, cols] + total

    chunks(tokens, body)


def sum_lanes(values):
    total = values[:, :128]
    for start in range(128, values.shape[1], 128):
        total = total + values[:, start : start + 128]
    return jnp.sum(total.T, axis=0, keepdims=True)


def weight_shapes():
    return dict(
        qkv=((3, D, D), BF),
        qkv_t=((3, HEADS * PAD, AUG), BF),
        out_t=((D, AUG), BF),
        out_pad=((HEADS * PAD, D), BF),
        inner=((D, 2 * FF), BF),
        inner_t=((2 * FF, AUG), BF),
        outer=((FF, D), BF),
        outer_t=((D, FF), BF),
        cols=((5, D, 128), F32),
    )


def kept_shapes(tokens, seq, row_count):
    return dict(
        attn_low=((AUG, tokens), BF),
        query=((HEADS * PAD, tokens), BF),
        query_hi=((HEADS * PAD, tokens), BF),
        query_lo=((HEADS * PAD, tokens), BF),
        key=((HEADS * PAD, tokens), BF),
        value=((HEADS * PAD, tokens), BF),
        expo=((row_count * HEADS, seq, seq), BF),
        mixed=((HEADS * PAD, tokens), F32),
        total=((HEADS, tokens), F32),
        mixed_low=((AUG, tokens), BF),
        normed_ffn=((D, tokens), F32),
        inverse_ffn=((1, tokens), F32),
        ffn_low=((AUG, tokens), BF),
        silu=((FF, tokens), F32),
        slope=((FF, tokens), F32),
        hidden=((HID, tokens), BF),
    )


def norm_shapes(tokens):
    return dict(normed_attn=((D, tokens), F32), inverse_attn=((1, tokens), F32))


def shared_shapes(tokens, seq):
    return dict(
        scores=((2, seq, seq), F32),
        top=((2, 1, seq), F32),
        compact=((3, D, tokens), F32),
        grad_hi=((HEADS * PAD, tokens), BF),
        grad_lo=((HEADS * PAD, tokens), BF),
        grad_branch=((D, tokens), BF),
        grad_inner=((2 * FF, tokens), BF),
        grad_middle=((D, tokens), F32),
        grad_attn=((D, tokens), BF),
        grad_qkv=((3, D, tokens), BF),
        sums=((2, D, CHUNK), F32),
        grad_next=((D, tokens), F32),
        input_one=((D, tokens), F32),
        input_two=((D, tokens), F32),
        pair=((2, FF, 128), F32),
        tail=((1176, 128), F32),
    )


def fill_spare(group, widths, seq, row_count):
    tokens = seq * row_count
    row = lax.broadcasted_iota(jnp.int32, (AUG - D, tokens), 0)
    ones = jnp.where(row == 0, 1.0, 0.0)
    slot = lax.broadcasted_iota(jnp.int32, (AUG - D, seq), 1)
    masks = [jnp.where(slot < widths[r], 0.0, MASK) for r in range(row_count)]
    mask = jnp.where(row == 1, jnp.concatenate(masks, axis=1), 0.0)
    group.attn_low[D:, :] = (ones + mask).astype(BF)
    group.mixed_low[D:, :] = ones.astype(BF)
    group.ffn_low[D:, :] = ones.astype(BF)
    group.hidden[FF:, :] = ones.astype(BF)
MESH_ID = pl.DeviceIdType.MESH


class Plan:
    def __init__(self, mesh_shape):
        self.dp, self.fs = mesh_shape["dp"], mesh_shape["fsdp"]
        self.line = 2 ** ((self.dp.bit_length()) // 2)
        self.low = self.dp // self.line
        self.peers = self.low * self.fs // 2
        self.count = self.dp * self.fs

    def here(self):
        dp, fs = lax.axis_index("dp"), lax.axis_index("fsdp")
        half = self.fs // 2
        return dp // self.low, (dp % self.low) * half + fs // 2, fs % 2

    def device(self, hi, q, c):
        half = self.fs // 2
        return (hi * self.low + q // half, (q % half) * 2 + c)

    def shard(self, hi, q, c):
        return (hi * self.peers + q) * 2 + c

    def partners(self):
        hi, q, c = self.here()
        return (
            [self.device((hi + d) % self.line, q, c) for d in range(1, self.line)]
            + [self.device(hi, (q + d) % self.peers, c) for d in range(1, self.peers)]
            + [self.device(hi, q, 1 - c)]
        )

    def greet(self):
        barrier = pltpu.get_barrier_semaphore()
        for other in self.partners():
            pl.semaphore_signal(barrier, 1, device_id=other, device_id_type=MESH_ID)

    def meet(self):
        pl.semaphore_wait(pltpu.get_barrier_semaphore(), self.line + self.peers - 1)


def piece_rows(length):
    return -(-(length + 127) // 2048) * 16


def remote(source, target, sems, sent, received, device):
    return pltpu.make_async_remote_copy(
        source, target, sems.at[0, sent], sems.at[1, received], device_id=device, device_id_type=MESH_ID
    )


def send(source, target, sems, index, device):
    copy = remote(source, target, sems, index, index, device)
    copy.start()
    return copy


def place_shard(x, offset):
    turned = pltpu.roll(x, offset, 1)
    before = jnp.concatenate([jnp.zeros((1, 128), x.dtype), turned[:-1]], axis=0)
    lane = lax.broadcasted_iota(jnp.int32, x.shape, 1)
    return jnp.where(lane >= offset, turned, before)


def lift_shard(x, offset):
    turned = pltpu.roll(x, lax.rem(128 - offset, 128), 1)
    after = jnp.concatenate([turned[1:], turned[:1]], axis=0)
    lane = lax.broadcasted_iota(jnp.int32, x.shape, 1)
    return jnp.where(lane < 128 - offset, turned, after)


class Gather:
    def __init__(self, plan, sems, held, length, parts):
        self.plan, self.sems, self.held, self.length = plan, sems, held, length
        self.parts = parts
        self.across = [[] for _ in parts]
        self.pair = [[] for _ in parts]

    def base(self, part):
        return self.plan.line + 2 * self.plan.peers * part

    def begin(self, shard):
        p = self.plan
        hi, q, c = p.here()
        offset = lax.rem(p.shard(hi, q, c) * self.length, 128)
        self.held[c, q, hi] = place_shard(shard, offset).astype(BF)
        mine = self.held.at[c, q, hi]
        self.along = []
        for d in range(1, p.line):
            copy = remote(mine, mine, self.sems, d, hi, p.device((hi + d) % p.line, q, c))
            copy.start()
            self.along.append(copy)

    def spread(self, part):
        p = self.plan
        hi, q, c = p.here()
        first, last = self.parts[part]
        for t in range(first, last):

            @pl.when(hi != t)
            def _():
                piece = self.held.at[c, q, t]
                remote(piece, piece, self.sems, 0, t, p.device(t, q, c)).wait_recv()

        mine = self.held.at[c, q, first:last]
        base = self.base(part)
        self.across[part] = [
            send(mine, mine, self.sems, base + d, p.device(hi, (q + d) % p.peers, c))
            for d in range(1, p.peers)
        ]
        self.pair[part] = [send(mine, mine, self.sems, base, p.device(hi, q, 1 - c))]

    def mirror(self, part):
        p = self.plan
        hi, q, c = p.here()
        first, last = self.parts[part]
        base = self.base(part) + p.peers
        for d, copy in enumerate(self.across[part], 1):
            copy.wait_recv()
            piece = self.held.at[c, (q - d + p.peers) % p.peers, first:last]
            self.pair[part].append(send(piece, piece, self.sems, base + d, p.device(hi, q, 1 - c)))

    def finish(self, part):
        for copy in self.pair[part]:
            copy.wait_recv()

    def drain(self):
        for copies in [self.along] + self.across + self.pair:
            for copy in copies:
                copy.wait_send()

    def flatten(self, part, flat):
        p = self.plan
        rows = self.held.shape[3]
        first, last = self.parts[part]
        if part == 0:
            flat[0:8, :] = jnp.zeros((8, 128), F32)
        for hi in range(first, last):
            for q in range(p.peers):
                for c in range(2):
                    start = p.shard(hi, q, c) * self.length // 128
                    piece = self.held[c, q, hi].astype(F32)
                    flat[start : start + 1, :] += piece[:1]
                    flat[start + 1 : start + rows, :] = piece[1:]


def gather_sems(plan, parts):
    return pltpu.SemaphoreType.DMA((2, plan.line + 2 * plan.peers * parts))


class Reduce:
    def __init__(self, plan, sems, refs, length, part):
        self.plan, self.sems, self.r, self.length, self.part = plan, sems, refs, length, part

    def begin(self, flat):
        p, r = self.plan, self.r
        rows = r.mine.shape[3]
        first, last = self.part
        for hi in range(first, last):
            for q in range(p.peers):
                for c in range(2):
                    start = p.shard(hi, q, c) * self.length // 128
                    r.mine[c, q, hi - first] = flat[start : start + rows, :].astype(BF)
        hi, q, c = p.here()
        self.pair = send(r.mine.at[1 - c], r.pair, self.sems, 0, p.device(hi, q, 1 - c))

    def across(self):
        p, r = self.plan, self.r
        hi, q, c = p.here()
        self.pair.wait_recv()
        r.both[...] = (r.mine[c].astype(F32) + r.pair[...].astype(F32)).astype(BF)
        self.peers = [
            send(
                r.both.at[(q + d) % p.peers], r.peers.at[d], self.sems, d, p.device(hi, (q + d) % p.peers, c)
            )
            for d in range(1, p.peers)
        ]

    def lines(self):
        p, r = self.plan, self.r
        hi, q, c = p.here()
        first, last = self.part
        for t in range(first, last):
            slot = lax.rem(hi - t + p.line, p.line)
            yield t, remote(
                r.plane.at[t - first],
                r.line.at[slot],
                self.sems,
                p.peers + t,
                p.peers + p.line + slot,
                p.device(t, q, c),
            )

    def along(self):
        p, r = self.plan, self.r
        hi, q, c = p.here()
        total = r.both[q].astype(F32)
        for d, copy in enumerate(self.peers, 1):
            copy.wait_recv()
            total = total + r.peers[d].astype(F32)
        r.plane[...] = total.astype(BF)
        for t, copy in self.lines():

            @pl.when(hi != t)
            def _():
                copy.start()

    def finish(self, out):
        p, r = self.plan, self.r
        hi, q, c = p.here()
        first, last = self.part

        def collect():
            total = r.plane[hi - first].astype(F32)
            for d in range(1, p.line):
                index = p.peers + p.line + d
                source = p.device((hi + d) % p.line, q, c)
                remote(r.line.at[d], r.line.at[d], self.sems, 0, index, source).wait_recv()
                total = total + r.line[d].astype(F32)
            offset = lax.rem(p.shard(hi, q, c) * self.length, 128)
            out[...] = lift_shard(total, offset)

        if (first, last) == (0, p.line):
            collect()
        else:
            pl.when((hi >= first) & (hi < last))(collect)
        self.pair.wait_send()
        for copy in self.peers:
            copy.wait_send()
        for t, copy in self.lines():

            @pl.when(hi != t)
            def _():
                copy.wait_send()


def reduce_shapes(plan, rows, part):
    wide_part = part[1] - part[0]
    return dict(
        mine=((2, plan.peers, wide_part, rows, 128), BF),
        pair=((plan.peers, wide_part, rows, 128), BF),
        both=((plan.peers, wide_part, rows, 128), BF),
        peers=((plan.peers, wide_part, rows, 128), BF),
        plane=((wide_part, rows, 128), BF),
        line=((plan.line, rows, 128), BF),
    )


def reduce_sems(plan):
    return pltpu.SemaphoreType.DMA((2, plan.peers + 2 * plan.line))
def vmem():
    return pl.BlockSpec(memory_space=pltpu.VMEM)


def hbm():
    return pl.BlockSpec(memory_space=pl.ANY)


def scratch(*dicts):
    shapes, names = [], []
    for entry in dicts:
        names.append(list(entry))
        shapes += [pltpu.VMEM(*entry[name]) for name in entry]
    return shapes, names


def grouped(names, refs):
    it = iter(refs)
    return [Group(**{name: next(it) for name in entry}) for entry in names]


def row_copies(source, target, sems, base, seq, row_count, out):
    copies = []
    for r in range(row_count):
        inside = target.at[:, pl.ds(r * seq, seq)]
        outside = source.at[r]
        pair = (inside, outside) if out else (outside, inside)
        copies.append(pltpu.make_async_copy(*pair, sems.at[base + r]))
    return copies


def whole_kernel(plan, lengths, names, halves, seq, row_count, *refs):
    widths, one, two, features, out_grad, activations, grad_features, out_one, out_two = refs[:9]
    sem_one, sem_two, red_early, red_late, red_two, io = refs[9:15]
    w_one, w_two, a_one, a_two, s, h, r_early, r_late, r_two = grouped(names, refs[15:])
    tokens = seq * row_count
    everything = (0, plan.line)
    plan.greet()
    loads = row_copies(features, s.input_one, io, 0, seq, row_count, False)
    loads_grad = row_copies(out_grad, s.grad_next, io, row_count, seq, row_count, False)
    for copy in loads:
        copy.start()
    live = [widths[r] for r in range(row_count)]
    for a in (a_one, a_two):
        fill_spare(a, live, seq, row_count)
    gather_one = Gather(plan, sem_one, h.one, lengths[0], halves)
    gather_two = Gather(plan, sem_two, h.two, lengths[1], [everything])
    plan.meet()
    gather_one.begin(one[...])
    gather_one.spread(0)
    gather_one.spread(1)
    gather_one.mirror(0)
    gather_one.finish(0)
    gather_one.flatten(0, h.flat)
    unpack_attention(h.flat, w_one, True, s.pair)
    gather_one.mirror(1)
    gather_two.begin(two[...])
    for copy in loads:
        copy.wait()
    forward_project(s, a_one, w_one, s.input_one, True, tokens)
    attend_forward(s, a_one, seq, row_count, lambda: gather_two.spread(0))
    gather_one.finish(1)
    gather_one.flatten(1, h.flat)
    unpack_rest(h.flat, w_one, True, s.pair, s.tail)
    gather_two.mirror(0)
    forward_feed(s, a_one, w_one, s.input_one, s.input_two, tokens)
    gather_two.finish(0)
    gather_one.drain()
    gather_two.drain()
    gather_two.flatten(0, h.flat)
    unpack_attention(h.flat, w_two, False, s.pair)
    unpack_rest(h.flat, w_two, False, s.pair, s.tail)
    forward_project(s, a_two, w_two, s.input_two, False, tokens)
    for copy in loads_grad:
        copy.start()
    attend_forward(s, a_two, seq, row_count, lambda: None)
    forward_feed(s, a_two, w_two, s.input_two, s.input_one, tokens)
    stores = row_copies(activations, s.input_one, io, 2 * row_count, seq, row_count, True)
    for copy in stores:
        copy.start()
    for copy in loads_grad:
        copy.wait()

    reduce_two = Reduce(plan, red_two, r_two, lengths[1], everything)
    reduce_early = Reduce(plan, red_early, r_early, lengths[0], halves[1])
    reduce_late = Reduce(plan, red_late, r_late, lengths[0], halves[0])
    backward_feed(s, a_two, w_two, s.grad_next, tokens)
    vecs = grads_feed(s, a_two, False, h.flat, s.pair, s.tail)
    attend_backward(s, a_two, seq, row_count, lambda: None)
    grads_attention(s, a_two, False, h.flat, s.pair, vecs)
    backward_project(s, a_two, w_two, s.grad_next, False, tokens)
    vecs["gain_attn"] = sum_lanes(s.sums[0])
    vecs["bias_attn"] = sum_lanes(s.sums[1])
    write_vectors(h.flat, False, vecs, s.pair)
    reduce_two.begin(h.flat)
    backward_feed(s, a_one, w_one, s.grad_next, tokens)
    reduce_two.across()
    vecs = grads_feed(s, a_one, True, h.flat, s.pair, s.tail)
    reduce_early.begin(h.flat)

    def between():
        reduce_two.along()
        reduce_early.across()

    attend_backward(s, a_one, seq, row_count, between)
    reduce_early.along()
    grads_attention(s, a_one, True, h.flat, s.pair, vecs)
    write_vectors(h.flat, True, vecs, s.pair)
    reduce_late.begin(h.flat)
    backward_project(s, a_one, w_one, s.input_two, True, tokens)
    reduce_late.across()
    last = row_copies(grad_features, s.input_two, io, 3 * row_count, seq, row_count, True)
    for copy in last:
        copy.start()
    reduce_two.finish(out_two)
    reduce_early.finish(out_one)
    reduce_late.along()
    for copy in stores + last:
        copy.wait()
    reduce_late.finish(out_one)


def on_device(plan, features, widths, params_one, params_two, out_grad):
    row_count, seq, _ = features.shape
    tokens = row_count * seq
    lengths = [params_one.shape[0], params_two.shape[0]]
    rows = [piece_rows(length) for length in lengths]
    flat_rows = [plan.count * length // 128 for length in lengths]
    room = max(2360, max(flat_rows) + max(rows) + 16) // 8 * 8
    halves = [(0, plan.line // 2), (plan.line // 2, plan.line)]
    everything = (0, plan.line)
    padded = [
        jnp.pad(shard, (0, r * 128 - shard.shape[0])).reshape(r, 128)
        for shard, r in zip((params_one, params_two), rows)
    ]
    held = {
        name: ((2, plan.peers, plan.line, r, 128), BF) for name, r in zip(("one", "two"), rows)
    }
    kept = kept_shapes(tokens, seq, row_count)
    shapes, names = scratch(
        weight_shapes(),
        weight_shapes(),
        kept,
        {**kept, **norm_shapes(tokens)},
        shared_shapes(tokens, seq),
        {**held, "flat": ((room, 128), F32)},
        reduce_shapes(plan, rows[0], halves[1]),
        reduce_shapes(plan, rows[0], halves[0]),
        reduce_shapes(plan, rows[1], everything),
    )
    sems = [gather_sems(plan, 2), gather_sems(plan, 1)] + [reduce_sems(plan)] * 3
    sems.append(pltpu.SemaphoreType.DMA((4 * row_count,)))
    turned = jax.ShapeDtypeStruct((row_count, D, seq), F32)
    activations, grad_features, grad_one, grad_two = pl.pallas_call(
        functools.partial(whole_kernel, plan, lengths, names, halves, seq, row_count),
        out_shape=[turned, turned] + [jax.ShapeDtypeStruct((r, 128), F32) for r in rows],
        in_specs=[pl.BlockSpec(memory_space=pltpu.SMEM), vmem(), vmem(), hbm(), hbm()],
        out_specs=[hbm(), hbm(), vmem(), vmem()],
        scratch_shapes=sems + shapes,
        compiler_params=pltpu.CompilerParams(
            vmem_limit_bytes=62 * 2**20, collective_id=0, has_side_effects=True
        ),
        name="blocks",
    )(widths, *padded, jnp.swapaxes(features, 1, 2), jnp.swapaxes(out_grad, 1, 2))
    shards = [g.reshape(-1)[:length] for g, length in zip((grad_one, grad_two), lengths)]
    return (jnp.swapaxes(activations, 1, 2), jnp.swapaxes(grad_features, 1, 2), *shards)


def solution(mesh):
    plan = Plan(dict(mesh.shape))
    rows = P(("dp", "fsdp"), None, None)
    flat = P(("dp", "fsdp"))
    return jax.shard_map(
        functools.partial(on_device, plan),
        mesh=mesh,
        in_specs=(rows, flat, flat, flat, rows),
        out_specs=(rows, rows, flat, flat),
        check_vma=False,
    )
```

```python
import functools
import math

import jax
import jax.numpy as jnp
from jax import lax
from jax.experimental import pallas as pl
from jax.experimental.pallas import tpu as pltpu
from jax.sharding import PartitionSpec as P

D = 192
HEADS = 8
FF = 256
HEAD_DIM = 24
PAD = 32
AUG = 208
HID = 272
GROUP = 4
LAG = 2
CHUNK = 1024
EPS = 1e-5
MASK = -4e30
SCALE = HEAD_DIM**-0.5
LOG2E = math.log2(math.e)
MATS = 1152
BF = jnp.bfloat16
F32 = jnp.float32


def nn(left, right):
    return lax.dot_general(left, right, (((1,), (0,)), ((), ())), preferred_element_type=F32)


def nt(left, right):
    return lax.dot_general(left, right, (((1,), (1,)), ((), ())), preferred_element_type=F32)


def tn(left, right):
    return lax.dot_general(left, right, (((0,), (0,)), ((), ())), preferred_element_type=F32)


def lanes_low(rows):
    return lax.broadcasted_iota(jnp.int32, (rows, 128), 1) < 64


def half_turn(values):
    return pltpu.roll(values, 64, 1)


def read_wide(flat, start, rows, pair):
    count = rows // 2
    first = flat[pl.ds(start, count, stride=3), :]
    second = flat[pl.ds(start + 1, count, stride=3), :]
    third = half_turn(flat[pl.ds(start + 2, count, stride=3), :])
    pair[0, pl.ds(0, count, stride=2), :] = first
    pair[1, pl.ds(0, count, stride=2), :] = second
    pair[0, pl.ds(1, count, stride=2), :] = jnp.where(lanes_low(count), half_turn(second), third)
    pair[1, pl.ds(1, count, stride=2), :] = third
    return jnp.concatenate([pair[0, :rows, :], pair[1, :rows, :64]], axis=1)


def write_wide(flat, start, values, pair):
    rows = values.shape[0]
    count = rows // 2
    pair[0, :rows, :] = values[:, :128]
    pair[1, :rows, :64] = values[:, 128:]
    low = lanes_low(count)
    even_low = pair[0, pl.ds(0, count, stride=2), :]
    even_high = pair[1, pl.ds(0, count, stride=2), :]
    odd_low = half_turn(pair[0, pl.ds(1, count, stride=2), :])
    odd_high = half_turn(pair[1, pl.ds(1, count, stride=2), :])
    flat[pl.ds(start, count, stride=3), :] = even_low
    flat[pl.ds(start + 1, count, stride=3), :] = jnp.where(low, even_high, odd_low)
    flat[pl.ds(start + 2, count, stride=3), :] = jnp.where(low, odd_low, odd_high)


def vector_names(leading):
    names = ["b_query", "b_value", "b_output"]
    if not leading:
        names = names + ["gain_attn", "bias_attn"]
    return names + ["gain_ffn", "bias_ffn"]


def spread():
    row = lax.broadcasted_iota(jnp.int32, (HEADS * PAD, D), 0)
    col = lax.broadcasted_iota(jnp.int32, (HEADS * PAD, D), 1)
    inside = (row & (PAD - 1)) < HEAD_DIM
    source = (row >> 5) * HEAD_DIM + (row & (PAD - 1))
    return jnp.where(inside & (source == col), 1.0, 0.0).astype(BF)


def identity(size):
    row = lax.broadcasted_iota(jnp.int32, (size, size), 0)
    col = lax.broadcasted_iota(jnp.int32, (size, size), 1)
    return jnp.where(row == col, 1.0, 0.0).astype(BF)


def unit_entry(column):
    row = lax.broadcasted_iota(jnp.int32, (HEADS * PAD, AUG), 0)
    col = lax.broadcasted_iota(jnp.int32, (HEADS * PAD, AUG), 1)
    return jnp.where(((row & (PAD - 1)) == HEAD_DIM) & (col == column), 1.0, 0.0)


def column(row_vec):
    return jnp.broadcast_to(row_vec, (128, D)).T


def augment(matrix, bias):
    width = matrix.shape[1]
    return jnp.concatenate([matrix, bias, jnp.zeros((AUG - D - 1, width), F32)], axis=0).astype(BF)


def unpack_vectors(flat, leading, pair):
    names = vector_names(leading)
    vecs = read_wide(flat, MATS, len(names) + 1, pair)
    return {name: vecs[i : i + 1, :] for i, name in enumerate(names)}


def unpack_attention(flat, w, leading, pair):
    vec = unpack_vectors(flat, leading, pair)
    put = spread()
    zero_row = jnp.zeros((1, D), F32)
    for i, (bias, spare) in enumerate((("b_query", D), (None, D + 1), ("b_value", D))):
        mat = read_wide(flat, 288 * i, D, pair)
        aug = augment(mat, vec[bias] if bias else zero_row)
        w.qkv[i] = aug[:D]
        w.qkv_t[i] = (nt(put, aug) + unit_entry(spare)).astype(BF)
    if not leading:
        w.cols[3] = column(vec["gain_attn"])
        w.cols[4] = column(vec["bias_attn"])


def unpack_rest(flat, w, leading, pair, tail):
    names = vector_names(leading)
    vec = unpack_vectors(flat, leading, pair)
    put = spread()
    aug = augment(read_wide(flat, 864, D, pair), vec["b_output"])
    w.out_t[...] = nt(identity(D), aug).astype(BF)
    w.out_pad[...] = nn(put, aug[:D]).astype(BF)
    start = MATS + len(names) * 3 // 2
    count = 1160
    turned = half_turn(flat[pl.ds(start, count + 8), :])
    tail[:count, :] = jnp.where(lanes_low(count), turned[:count], turned[1 : count + 1])
    aug = augment(
        jnp.concatenate([tail[pl.ds(j, D, stride=4), :] for j in range(4)], axis=1),
        jnp.concatenate([tail[768 + j : 769 + j, :] for j in range(4)], axis=1),
    )
    w.inner[...] = aug[:D]
    for half in range(2):
        cols = slice(half * FF, (half + 1) * FF)
        w.inner_t[cols, :] = nt(identity(FF), aug[:, cols]).astype(BF)
    outer = read_wide(tail, 772, FF, pair).astype(BF)
    w.outer[...] = outer
    w.outer_t[...] = nt(identity(D), outer).astype(BF)
    b_outer = jnp.concatenate([tail[1156:1157, :], tail[1157:1158, :64]], axis=1)
    w.cols[0] = column(b_outer)
    w.cols[1] = column(vec["gain_ffn"])
    w.cols[2] = column(vec["bias_ffn"])


class Group:
    def __init__(self, **refs):
        self.__dict__.update(refs)


def wide(col):
    return jnp.concatenate([col] * (CHUNK // 128), axis=1)


def norm(values):
    center = values - jnp.sum(values, axis=0, keepdims=True) * (1.0 / D)
    inverse = lax.rsqrt(jnp.sum(center * center, axis=0, keepdims=True) * (1.0 / D) + EPS)
    return center * inverse, inverse


def norm_back(grad, normed, inverse, gain):
    scaled = grad * gain
    mean = jnp.sum(scaled, axis=0, keepdims=True) * (1.0 / D)
    cross = jnp.sum(scaled * normed, axis=0, keepdims=True) * (1.0 / D)
    return inverse * (scaled - mean - normed * cross)


def chunks(tokens, body, unroll=True):
    count = tokens // CHUNK

    def step(i, carry):
        body(pl.ds(pl.multiple_of(i * CHUNK, CHUNK), CHUNK))
        return carry

    if unroll is True:
        for i in range(count):
            body(pl.ds(i * CHUNK, CHUNK))
    else:
        lax.fori_loop(0, count, step, 0, unroll=unroll)


def place(u, seq):
    if isinstance(u, int):
        row, head = divmod(u, HEADS)
        return head, pl.ds(head * PAD, PAD), pl.ds(head * HEAD_DIM, HEAD_DIM), pl.ds(row * seq, seq)
    row = lax.div(u, HEADS)
    head = u - row * HEADS
    return (
        head,
        pl.ds(pl.multiple_of(head * PAD, PAD), PAD),
        pl.ds(pl.multiple_of(head * HEAD_DIM, 8), HEAD_DIM),
        pl.ds(pl.multiple_of(row * seq, seq), seq),
    )


def grouped_loop(units, body, between):
    groups = units // GROUP

    def step(g, carry):
        for j in range(GROUP):
            body(j, lambda back: lax.rem(g * GROUP + (j - back + units), units))
        return carry

    lax.fori_loop(0, groups // 2, step, 0)
    between()
    lax.fori_loop(groups // 2, groups, step, 0)


def attend_forward(s, a, seq, row_count, between):
    units = row_count * HEADS

    def score(u, slot):
        _, rows, _, cols = place(u, seq)
        key = a.key[rows, cols]
        keys = jnp.concatenate([key, key], axis=0)
        query = jnp.concatenate([s.high[rows, cols], s.low[rows, cols]], axis=0)
        scores = tn(keys, query)
        s.scores[slot] = scores
        s.top[slot] = jnp.max(scores, axis=0, keepdims=True)

    def expo(u, slot):
        a.expo[u] = jnp.exp2(s.scores[slot] - s.top[slot]).astype(BF)

    def mix(u):
        head, rows, compact, cols = place(u, seq)
        total = nn(a.value[rows, cols], a.expo[u])
        inverse = 1.0 / total[HEAD_DIM : HEAD_DIM + 1]
        mixed = total * inverse
        a.mixed[rows, cols] = mixed
        a.total[pl.ds(head, 1), cols] = inverse
        s.compact[0, compact, cols] = mixed[:HEAD_DIM]

    def body(j, unit):
        mix(unit(LAG + 1))
        expo(unit(LAG), (j - LAG) % GROUP)
        score(unit(0), j)

    grouped_loop(units, body, between)
    for u in range(units - LAG - 1, units):
        mix(u)
        if u + 1 < units:
            expo(u + 1, (u + 1) % GROUP)


def attend_backward(s, a, seq, row_count, between):
    units = row_count * HEADS

    def score(u, slot):
        _, rows, compact, cols = place(u, seq)
        value = a.value[rows, cols]
        grad_hi = s.high[rows, cols]
        values = jnp.concatenate([value, value], axis=0)
        grads = jnp.concatenate([grad_hi, s.low[rows, cols]], axis=0)
        expo = a.expo[u]
        grad_soft = tn(values, grads)
        s.grad_scores[slot] = (grad_soft * expo.astype(F32)).astype(BF)
        s.compact[2, compact, cols] = nt(grad_hi, expo)[:HEAD_DIM]

    def back(u, slot):
        _, rows, compact, cols = place(u, seq)
        grad_scores = s.grad_scores[slot]
        s.compact[1, compact, cols] = nt(a.query[rows, cols], grad_scores)[:HEAD_DIM] * SCALE
        s.compact[0, compact, cols] = nn(a.key[rows, cols], grad_scores)[:HEAD_DIM] * SCALE

    def body(j, unit):
        back(unit(1), (j - 1) % GROUP)
        score(unit(0), j)

    grouped_loop(units, body, between)
    back(units - 1, (units - 1) % GROUP)


def forward_project(s, a, w, source, leading, tokens):
    def body(cols):
        x = source[:, cols]
        if not leading:
            normed, inverse = norm(x)
            a.normed_attn[:, cols] = normed
            a.inverse_attn[:, cols] = inverse
            x = normed * wide(w.cols[3]) + wide(w.cols[4])
        a.attn_low[:D, cols] = x.astype(BF)
        low = a.attn_low[:, cols]
        query = nn(w.qkv_t[0], low).astype(BF)
        a.query[:, cols] = query
        scaled = query.astype(F32) * (SCALE * LOG2E)
        high = scaled.astype(BF)
        s.high[:, cols] = high
        s.low[:, cols] = (scaled - high.astype(F32)).astype(BF)
        a.key[:, cols] = nn(w.qkv_t[1], low).astype(BF)
        a.value[:, cols] = nn(w.qkv_t[2], low).astype(BF)

    chunks(tokens, body)


def forward_feed(s, a, w, source, target, tokens):
    def body(cols):
        a.mixed_low[:D, cols] = s.compact[0, :, cols].astype(BF)
        middle = source[:, cols] + nn(w.out_t[...], a.mixed_low[:, cols])
        normed, inverse = norm(middle)
        a.normed_ffn[:, cols] = normed
        a.inverse_ffn[:, cols] = inverse
        a.ffn_low[:D, cols] = (normed * wide(w.cols[1]) + wide(w.cols[2])).astype(BF)
        low = a.ffn_low[:, cols]
        linear = nn(w.inner_t[:FF, :], low)
        gate = nn(w.inner_t[FF:, :], low)
        sigmoid = 1.0 / (1.0 + jnp.exp2(gate * (-LOG2E)))
        silu = gate * sigmoid
        a.silu[:, cols] = silu
        a.slope[:, cols] = linear * sigmoid * (1.0 + gate * (1.0 - sigmoid))
        hidden = (linear * silu).astype(BF)
        a.hidden[:FF, cols] = hidden
        target[:, cols] = middle + nn(w.outer_t[...], hidden) + wide(w.cols[0])

    chunks(tokens, body)


def backward_feed(s, a, w, grad, tokens):
    s.sums[...] = jnp.zeros_like(s.sums)

    def body(cols):
        g = grad[:, cols]
        low = g.astype(BF)
        s.grad_branch[:, cols] = low
        grad_hidden = nn(w.outer[...], low)
        grad_linear = (grad_hidden * a.silu[:, cols]).astype(BF)
        grad_gate = (grad_hidden * a.slope[:, cols]).astype(BF)
        s.grad_inner[:FF, cols] = grad_linear
        s.grad_inner[FF:, cols] = grad_gate
        u = nn(w.inner[:, :FF], grad_linear) + nn(w.inner[:, FF:], grad_gate)
        normed = a.normed_ffn[:, cols]
        s.sums[0] += fold(u * normed)
        s.sums[1] += fold(u)
        middle = g + norm_back(u, normed, a.inverse_ffn[:, cols], wide(w.cols[1]))
        s.grad_middle[:, cols] = middle
        low = middle.astype(BF)
        s.grad_attn[:, cols] = low
        grad_mixed = nn(w.out_pad[...], low).astype(BF).astype(F32)
        for head in range(HEADS):
            rows = slice(head * PAD, (head + 1) * PAD)
            part = grad_mixed[rows]
            dot = jnp.sum(part * a.mixed[rows, cols], axis=0, keepdims=True)
            spare = lax.broadcasted_iota(jnp.int32, (PAD, CHUNK), 0) == HEAD_DIM
            part = jnp.where(spare, -dot, part) * a.total[head : head + 1, cols]
            high = part.astype(BF)
            s.high[rows, cols] = high
            s.low[rows, cols] = (part - high.astype(F32)).astype(BF)

    chunks(tokens, body)


def write_vectors(flat, leading, vecs, pair):
    names = vector_names(leading)
    last = MATS + len(names) * 3 // 2
    keep = flat[last : last + 8, :]
    zero = jnp.zeros((1, D), F32)
    stack = jnp.concatenate([vecs.get(name, zero) for name in names] + [zero], axis=0)
    write_wide(flat, MATS, stack, pair)
    flat[last : last + 8, :] = keep


def grads_feed(s, a, leading, flat, pair, tail):
    names = vector_names(leading)
    vecs = {}
    grads = nt(a.hidden[...], s.grad_branch[...])
    write_wide(tail, 8 + 772, grads[:FF], pair)
    tail[8 + 1156 : 8 + 1157, :] = grads[FF : FF + 1, :128]
    tail[8 + 1157 : 8 + 1158, :64] = grads[FF : FF + 1, 128:]
    tail[8 + 1157 : 8 + 1158, 64:] = jnp.zeros((1, 64), F32)
    tail[8 + 1158 :, :] = jnp.zeros_like(tail[8 + 1158 :, :])
    grads = nt(a.ffn_low[...], s.grad_inner[...])
    for j in range(4):
        cols = slice(128 * j, 128 * j + 128)
        tail[pl.ds(8 + j, D, stride=4), :] = grads[:D, cols]
        tail[8 + 768 + j : 8 + 769 + j, :] = grads[D : D + 1, cols]
    vecs["gain_ffn"] = sum_lanes(s.sums[0])
    vecs["bias_ffn"] = sum_lanes(s.sums[1])
    tail[7:8, 64:] = vecs["bias_ffn"][:, 128:]
    start = MATS + len(names) * 3 // 2
    count = 1160
    turned = half_turn(tail[pl.ds(0, count + 8), :])
    flat[pl.ds(start, count), :] = jnp.where(
        lanes_low(count), turned[7 : 7 + count], turned[8 : 8 + count]
    )
    grads = nt(a.mixed_low[...], s.grad_attn[...])
    write_wide(flat, 864, grads[:D], pair)
    vecs["b_output"] = grads[D : D + 1]
    write_vectors(flat, leading, vecs, pair)
    return vecs


def grads_attention(s, a, leading, flat, pair, vecs):
    for i, bias in enumerate(("b_query", None, "b_value")):
        s.grad_qkv[i] = s.compact[i].astype(BF)
        grads = nt(a.attn_low[...], s.grad_qkv[i])
        write_wide(flat, 288 * i, grads[:D], pair)
        if bias:
            vecs[bias] = grads[D : D + 1]


def backward_project(s, a, w, target, leading, tokens):
    s.sums[...] = jnp.zeros_like(s.sums)

    def body(cols):
        total = nn(w.qkv[0], s.grad_qkv[0, :, cols])
        total = total + nn(w.qkv[1], s.grad_qkv[1, :, cols])
        total = total + nn(w.qkv[2], s.grad_qkv[2, :, cols])
        if not leading:
            normed = a.normed_attn[:, cols]
            s.sums[0] += fold(total * normed)
            s.sums[1] += fold(total)
            total = norm_back(total, normed, a.inverse_attn[:, cols], wide(w.cols[3]))
        target[:, cols] = s.grad_middle[:, cols] + total

    chunks(tokens, body)


def fold(values):
    total = values[:, :128]
    for start in range(128, values.shape[1], 128):
        total = total + values[:, start : start + 128]
    return total


def sum_lanes(values):
    return jnp.sum(values.T, axis=0, keepdims=True)


def weight_shapes():
    return dict(
        qkv=((3, D, D), BF),
        qkv_t=((3, HEADS * PAD, AUG), BF),
        out_t=((D, AUG), BF),
        out_pad=((HEADS * PAD, D), BF),
        inner=((D, 2 * FF), BF),
        inner_t=((2 * FF, AUG), BF),
        outer=((FF, D), BF),
        outer_t=((D, FF), BF),
        cols=((5, D, 128), F32),
    )


def kept_shapes(tokens, seq, row_count):
    return dict(
        attn_low=((AUG, tokens), BF),
        query=((HEADS * PAD, tokens), BF),
        key=((HEADS * PAD, tokens), BF),
        value=((HEADS * PAD, tokens), BF),
        expo=((row_count * HEADS, seq, seq), BF),
        mixed=((HEADS * PAD, tokens), F32),
        total=((HEADS, tokens), F32),
        mixed_low=((AUG, tokens), BF),
        normed_ffn=((D, tokens), F32),
        inverse_ffn=((1, tokens), F32),
        ffn_low=((AUG, tokens), BF),
        silu=((FF, tokens), F32),
        slope=((FF, tokens), F32),
        hidden=((HID, tokens), BF),
    )


def norm_shapes(tokens):
    return dict(normed_attn=((D, tokens), F32), inverse_attn=((1, tokens), F32))


def shared_shapes(tokens, seq):
    return dict(
        scores=((GROUP, seq, seq), F32),
        top=((GROUP, 1, seq), F32),
        grad_scores=((GROUP, seq, seq), BF),
        compact=((3, D, tokens), F32),
        high=((HEADS * PAD, tokens), BF),
        low=((HEADS * PAD, tokens), BF),
        grad_branch=((D, tokens), BF),
        grad_inner=((2 * FF, tokens), BF),
        grad_middle=((D, tokens), F32),
        grad_attn=((D, tokens), BF),
        grad_qkv=((3, D, tokens), BF),
        sums=((2, D, 128), F32),
        grad_next=((D, tokens), F32),
        input_one=((D, tokens), F32),
        input_two=((D, tokens), F32),
        pair=((2, FF, 128), F32),
        tail=((1176, 128), F32),
    )


def fill_spare(group, widths, seq, row_count):
    tokens = seq * row_count
    row = lax.broadcasted_iota(jnp.int32, (AUG - D, tokens), 0)
    ones = jnp.where(row == 0, 1.0, 0.0)
    slot = lax.broadcasted_iota(jnp.int32, (AUG - D, seq), 1)
    masks = [jnp.where(slot < widths[r], 0.0, MASK) for r in range(row_count)]
    mask = jnp.where(row == 1, jnp.concatenate(masks, axis=1), 0.0)
    group.attn_low[D:, :] = (ones + mask).astype(BF)
    group.mixed_low[D:, :] = ones.astype(BF)
    group.ffn_low[D:, :] = ones.astype(BF)
    group.hidden[FF:, :] = ones.astype(BF)
MESH_ID = pl.DeviceIdType.MESH


class Plan:
    def __init__(self, mesh_shape):
        self.dp, self.fs = mesh_shape["dp"], mesh_shape["fsdp"]
        self.line = 2 ** ((self.dp.bit_length()) // 2)
        self.low = self.dp // self.line
        self.peers = self.low * self.fs // 2
        self.count = self.dp * self.fs

    def here(self):
        dp, fs = lax.axis_index("dp"), lax.axis_index("fsdp")
        half = self.fs // 2
        return dp // self.low, (dp % self.low) * half + fs // 2, fs % 2

    def device(self, hi, q, c):
        half = self.fs // 2
        return (hi * self.low + q // half, (q % half) * 2 + c)

    def shard(self, hi, q, c):
        return (hi * self.peers + q) * 2 + c

    def partners(self):
        hi, q, c = self.here()
        return (
            [self.device((hi + d) % self.line, q, c) for d in range(1, self.line)]
            + [self.device(hi, (q + d) % self.peers, c) for d in range(1, self.peers)]
            + [self.device(hi, q, 1 - c)]
        )

    def greet(self):
        barrier = pltpu.get_barrier_semaphore()
        for other in self.partners():
            pl.semaphore_signal(barrier, 1, device_id=other, device_id_type=MESH_ID)

    def meet(self):
        pl.semaphore_wait(pltpu.get_barrier_semaphore(), self.line + self.peers - 1)


def piece_rows(length):
    return -(-(length + 127) // 2048) * 16


def remote(source, target, sems, sent, received, device):
    return pltpu.make_async_remote_copy(
        source, target, sems.at[0, sent], sems.at[1, received], device_id=device, device_id_type=MESH_ID
    )


def send(source, target, sems, index, device):
    copy = remote(source, target, sems, index, index, device)
    copy.start()
    return copy


def place_shard(x, offset):
    turned = pltpu.roll(x, offset, 1)
    before = jnp.concatenate([jnp.zeros((1, 128), x.dtype), turned[:-1]], axis=0)
    lane = lax.broadcasted_iota(jnp.int32, x.shape, 1)
    return jnp.where(lane >= offset, turned, before)


def lift_shard(x, offset):
    turned = pltpu.roll(x, lax.rem(128 - offset, 128), 1)
    after = jnp.concatenate([turned[1:], turned[:1]], axis=0)
    lane = lax.broadcasted_iota(jnp.int32, x.shape, 1)
    return jnp.where(lane < 128 - offset, turned, after)


class Gather:
    def __init__(self, plan, sems, held, length, parts):
        self.plan, self.sems, self.held, self.length = plan, sems, held, length
        self.parts = parts
        self.across = [[] for _ in parts]
        self.pair = [[] for _ in parts]

    def steps(self, part):
        first, last = self.parts[part]
        if part > 0 or len(self.parts) == 1:
            return [(None, slice(first, last))]
        near = jnp.clip(self.plan.here()[0], first, last - 1)
        count = last - first
        indices = [first + lax.rem(near - first + count - k, count) for k in range(count)]
        return [(t, pl.ds(t, 1)) for t in indices]

    def base(self, part):
        p = self.plan
        return p.line + 2 * p.peers * (p.line if part else 0)

    def prepare(self, shard):
        p = self.plan
        hi, q, c = p.here()
        offset = lax.rem(p.shard(hi, q, c) * self.length, 128)
        self.held[c, q, hi] = place_shard(shard, offset).astype(BF)
        mine = self.held.at[c, q, hi]
        self.along = [
            remote(mine, mine, self.sems, d, hi, p.device((hi + d) % p.line, q, c)) for d in range(1, p.line)
        ]

    def begin(self, part):
        hi = self.plan.here()[0]
        first, last = self.parts[part]

        def start():
            for copy in self.along:
                copy.start()

        if (first, last) == (0, self.plan.line):
            start()
        else:
            pl.when((hi >= first) & (hi < last))(start)

    def await_line(self, t):
        p = self.plan
        hi, q, c = p.here()

        @pl.when(hi != t)
        def _():
            piece = self.held.at[c, q, t]
            remote(piece, piece, self.sems, 0, t, p.device(t, q, c)).wait_recv()

    def spread(self, part):
        p = self.plan
        hi, q, c = p.here()
        for k, (t, where) in enumerate(self.steps(part)):
            for index in range(*self.parts[part]) if t is None else [t]:
                self.await_line(index)
            mine = self.held.at[c, q, where]
            base = self.base(part) + 2 * p.peers * k
            self.across[part].append(
                [
                    send(mine, mine, self.sems, base + d, p.device(hi, (q + d) % p.peers, c))
                    for d in range(1, p.peers)
                ]
            )
            self.pair[part].append(send(mine, mine, self.sems, base, p.device(hi, q, 1 - c)))

    def mirror(self, part):
        p = self.plan
        hi, q, c = p.here()
        for k, (_, where) in enumerate(self.steps(part)):
            base = self.base(part) + 2 * p.peers * k + p.peers
            for d, copy in enumerate(self.across[part][k], 1):
                copy.wait_recv()
                piece = self.held.at[c, (q - d + p.peers) % p.peers, where]
                self.pair[part].append(send(piece, piece, self.sems, base + d, p.device(hi, q, 1 - c)))

    def finish(self, part):
        for copy in self.pair[part]:
            copy.wait_recv()

    def drain(self):
        for copy in self.along:
            copy.wait_send()
        for copies in self.pair + [copies for part in self.across for copies in part]:
            for copy in copies:
                copy.wait_send()

    def flatten(self, part, flat):
        p = self.plan
        rows = self.held.shape[3]
        first, last = self.parts[part]
        if part == 0:
            flat[0:8, :] = jnp.zeros((8, 128), F32)
        for hi in range(first, last):
            for q in range(p.peers):
                for c in range(2):
                    start = p.shard(hi, q, c) * self.length // 128
                    piece = self.held[c, q, hi].astype(F32)
                    flat[start : start + 1, :] += piece[:1]
                    flat[start + 1 : start + rows, :] = piece[1:]


def gather_sems(plan):
    return pltpu.SemaphoreType.DMA((2, plan.line + 2 * plan.peers * (plan.line + 1)))


class Reduce:
    def __init__(self, plan, sems, refs, length, part):
        self.plan, self.sems, self.r, self.length, self.part = plan, sems, refs, length, part

    def begin(self, flat):
        p, r = self.plan, self.r
        rows = r.mine.shape[3]
        first, last = self.part
        for hi in range(first, last):
            for q in range(p.peers):
                for c in range(2):
                    start = p.shard(hi, q, c) * self.length // 128
                    r.mine[c, q, hi - first] = flat[start : start + rows, :].astype(BF)
        hi, q, c = p.here()
        self.pair = {}
        for d in list(range(1, p.peers)) + [0]:
            peer = (q + d) % p.peers
            self.pair[d] = send(
                r.mine.at[1 - c, peer], r.pair.at[peer], self.sems, d, p.device(hi, q, 1 - c)
            )

    def join(self, d):
        p, r = self.plan, self.r
        hi, q, c = p.here()
        peer = (q + d) % p.peers
        self.pair[d].wait_recv()
        return r.mine[c, peer].astype(F32) + r.pair[peer].astype(F32)

    def across(self):
        p, r = self.plan, self.r
        hi, q, c = p.here()
        self.peers = []
        for d in range(1, p.peers):
            peer = (q + d) % p.peers
            r.both[d] = self.join(d).astype(BF)
            self.peers.append(
                send(r.both.at[d], r.peers.at[d], self.sems, p.peers + d, p.device(hi, peer, c))
            )
        r.own[...] = self.join(0)

    def lines(self):
        p, r = self.plan, self.r
        hi, q, c = p.here()
        first, last = self.part
        for t in range(first, last):
            slot = lax.rem(hi - t + p.line, p.line)
            yield t, remote(
                r.plane.at[t - first],
                r.line.at[slot],
                self.sems,
                2 * p.peers + t,
                2 * p.peers + slot,
                p.device(t, q, c),
            )

    def along(self):
        p, r = self.plan, self.r
        hi, q, c = p.here()
        total = r.own[...]
        for d, copy in enumerate(self.peers, 1):
            copy.wait_recv()
            total = total + r.peers[d].astype(F32)
        r.plane[...] = total.astype(BF)
        for t, copy in self.lines():

            @pl.when(hi != t)
            def _():
                copy.start()

    def finish(self, out):
        p, r = self.plan, self.r
        hi, q, c = p.here()
        first, last = self.part

        def collect():
            total = r.plane[hi - first].astype(F32)
            for d in range(1, p.line):
                index = 2 * p.peers + d
                source = p.device((hi + d) % p.line, q, c)
                remote(r.line.at[d], r.line.at[d], self.sems, 0, index, source).wait_recv()
                total = total + r.line[d].astype(F32)
            offset = lax.rem(p.shard(hi, q, c) * self.length, 128)
            out[...] = lift_shard(total, offset)

        if (first, last) == (0, p.line):
            collect()
        else:
            pl.when((hi >= first) & (hi < last))(collect)
        for copy in self.pair.values():
            copy.wait_send()
        for copy in self.peers:
            copy.wait_send()
        for t, copy in self.lines():

            @pl.when(hi != t)
            def _():
                copy.wait_send()


def reduce_shapes(plan, rows, part):
    wide_part = part[1] - part[0]
    return dict(
        mine=((2, plan.peers, wide_part, rows, 128), BF),
        pair=((plan.peers, wide_part, rows, 128), BF),
        both=((plan.peers, wide_part, rows, 128), BF),
        peers=((plan.peers, wide_part, rows, 128), BF),
        own=((wide_part, rows, 128), F32),
        plane=((wide_part, rows, 128), BF),
        line=((plan.line, rows, 128), BF),
    )


def reduce_sems(plan):
    return pltpu.SemaphoreType.DMA((2, 2 * plan.peers + plan.line))
def vmem():
    return pl.BlockSpec(memory_space=pltpu.VMEM)


def hbm():
    return pl.BlockSpec(memory_space=pl.ANY)


def scratch(*dicts):
    shapes, names = [], []
    for entry in dicts:
        names.append(list(entry))
        shapes += [pltpu.VMEM(*entry[name]) for name in entry]
    return shapes, names


def grouped(names, refs):
    it = iter(refs)
    return [Group(**{name: next(it) for name in entry}) for entry in names]


def shard_rows(ref, rows):
    fill = jnp.zeros((rows * 128 - ref.shape[0],), F32)
    return jnp.concatenate([ref[...], fill]).reshape(rows, 128)


def row_copies(source, target, sems, base, seq, row_count, out):
    copies = []
    for r in range(row_count):
        inside = target.at[:, pl.ds(r * seq, seq)]
        outside = source.at[r]
        pair = (inside, outside) if out else (outside, inside)
        copies.append(pltpu.make_async_copy(*pair, sems.at[base + r]))
    return copies


def whole_kernel(plan, lengths, names, halves, seq, row_count, *refs):
    widths, one, two, features, out_grad, activations, grad_features, out_one, out_two = refs[:9]
    sem_one, sem_two, red_early, red_late, red_two, io = refs[9:15]
    w_one, w_two, a_one, a_two, s, h, r_early, r_late, r_two = grouped(names, refs[15:])
    tokens = seq * row_count
    everything = (0, plan.line)
    plan.greet()
    loads = row_copies(features, s.input_one, io, 0, seq, row_count, False)
    loads_grad = row_copies(out_grad, s.grad_next, io, row_count, seq, row_count, False)
    for copy in loads:
        copy.start()
    live = [widths[r] for r in range(row_count)]
    for a in (a_one, a_two):
        fill_spare(a, live, seq, row_count)
    gather_one = Gather(plan, sem_one, h.one, lengths[0], halves)
    gather_two = Gather(plan, sem_two, h.two, lengths[1], [everything])
    gather_one.prepare(shard_rows(one, h.one.shape[3]))
    gather_two.prepare(shard_rows(two, h.two.shape[3]))
    plan.meet()
    gather_one.begin(0)
    gather_one.spread(0)
    gather_one.begin(1)
    gather_two.begin(0)
    gather_one.mirror(0)
    for copy in loads:
        copy.wait()
    gather_one.finish(0)
    gather_one.flatten(0, h.flat)
    unpack_attention(h.flat, w_one, True, s.pair)
    gather_one.spread(1)
    forward_project(s, a_one, w_one, s.input_one, True, tokens)

    def forward():
        gather_one.mirror(1)
        gather_two.spread(0)

    attend_forward(s, a_one, seq, row_count, forward)
    gather_one.finish(1)
    gather_one.flatten(1, h.flat)
    unpack_rest(h.flat, w_one, True, s.pair, s.tail)
    gather_two.mirror(0)
    forward_feed(s, a_one, w_one, s.input_one, s.input_two, tokens)
    gather_two.finish(0)
    gather_one.drain()
    gather_two.drain()
    gather_two.flatten(0, h.flat)
    unpack_attention(h.flat, w_two, False, s.pair)
    unpack_rest(h.flat, w_two, False, s.pair, s.tail)
    forward_project(s, a_two, w_two, s.input_two, False, tokens)
    for copy in loads_grad:
        copy.start()
    attend_forward(s, a_two, seq, row_count, lambda: None)
    forward_feed(s, a_two, w_two, s.input_two, s.input_one, tokens)
    stores = row_copies(activations, s.input_one, io, 2 * row_count, seq, row_count, True)
    for copy in stores:
        copy.start()
    for copy in loads_grad:
        copy.wait()

    reduce_two = Reduce(plan, red_two, r_two, lengths[1], everything)
    reduce_early = Reduce(plan, red_early, r_early, lengths[0], halves[1])
    reduce_late = Reduce(plan, red_late, r_late, lengths[0], halves[0])
    backward_feed(s, a_two, w_two, s.grad_next, tokens)
    vecs = grads_feed(s, a_two, False, h.flat, s.pair, s.tail)
    attend_backward(s, a_two, seq, row_count, lambda: None)
    grads_attention(s, a_two, False, h.flat, s.pair, vecs)
    backward_project(s, a_two, w_two, s.grad_next, False, tokens)
    vecs["gain_attn"] = sum_lanes(s.sums[0])
    vecs["bias_attn"] = sum_lanes(s.sums[1])
    write_vectors(h.flat, False, vecs, s.pair)
    reduce_two.begin(h.flat)
    backward_feed(s, a_one, w_one, s.grad_next, tokens)
    reduce_two.across()
    vecs = grads_feed(s, a_one, True, h.flat, s.pair, s.tail)
    reduce_early.begin(h.flat)

    def between():
        reduce_two.along()
        reduce_early.across()

    attend_backward(s, a_one, seq, row_count, between)
    reduce_early.along()
    grads_attention(s, a_one, True, h.flat, s.pair, vecs)
    write_vectors(h.flat, True, vecs, s.pair)
    reduce_late.begin(h.flat)
    backward_project(s, a_one, w_one, s.input_two, True, tokens)
    reduce_late.across()
    last = row_copies(grad_features, s.input_two, io, 3 * row_count, seq, row_count, True)
    for copy in last:
        copy.start()
    reduce_two.finish(out_two)
    reduce_early.finish(out_one)
    reduce_late.along()
    for copy in stores + last:
        copy.wait()
    reduce_late.finish(out_one)


def deliver_kernel(*refs):
    count = len(refs) // 2
    sources, targets, sems = refs[:count], refs[count : 2 * count], refs[2 * count]
    copies = [pltpu.make_async_copy(a, b, sems.at[i]) for i, (a, b) in enumerate(zip(sources, targets))]
    for copy in copies:
        copy.start()
    for copy in copies:
        copy.wait()


def deliver(arrays):
    return pl.pallas_call(
        deliver_kernel,
        out_shape=[jax.ShapeDtypeStruct(x.shape, x.dtype) for x in arrays],
        in_specs=[hbm()] * len(arrays),
        out_specs=[hbm()] * len(arrays),
        scratch_shapes=[pltpu.SemaphoreType.DMA((len(arrays),))],
        name="deliver",
    )(*arrays)


def on_device(plan, features, widths, params_one, params_two, out_grad):
    row_count, seq, _ = features.shape
    tokens = row_count * seq
    lengths = [params_one.shape[0], params_two.shape[0]]
    rows = [piece_rows(length) for length in lengths]
    flat_rows = [plan.count * length // 128 for length in lengths]
    room = max(2360, max(flat_rows) + max(rows) + 16) // 8 * 8
    halves = [(0, plan.line // 2), (plan.line // 2, plan.line)]
    everything = (0, plan.line)
    held = {
        name: ((2, plan.peers, plan.line, r, 128), BF) for name, r in zip(("one", "two"), rows)
    }
    kept = kept_shapes(tokens, seq, row_count)
    shapes, names = scratch(
        weight_shapes(),
        weight_shapes(),
        kept,
        {**kept, **norm_shapes(tokens)},
        shared_shapes(tokens, seq),
        {**held, "flat": ((room, 128), F32)},
        reduce_shapes(plan, rows[0], halves[1]),
        reduce_shapes(plan, rows[0], halves[0]),
        reduce_shapes(plan, rows[1], everything),
    )
    sems = [gather_sems(plan)] * 2 + [reduce_sems(plan)] * 3
    sems.append(pltpu.SemaphoreType.DMA((4 * row_count,)))
    turned = jax.ShapeDtypeStruct((row_count, D, seq), F32)
    results = pl.pallas_call(
        functools.partial(whole_kernel, plan, lengths, names, halves, seq, row_count),
        out_shape=[turned, turned] + [jax.ShapeDtypeStruct((r, 128), F32) for r in rows],
        in_specs=[pl.BlockSpec(memory_space=pltpu.SMEM), vmem(), vmem(), hbm(), hbm()],
        out_specs=[hbm(), hbm(), vmem(), vmem()],
        scratch_shapes=sems + shapes,
        compiler_params=pltpu.CompilerParams(
            vmem_limit_bytes=62 * 2**20, collective_id=0, has_side_effects=True
        ),
        name="blocks",
    )(widths, params_one, params_two, jnp.swapaxes(features, 1, 2), jnp.swapaxes(out_grad, 1, 2))
    activations, grad_features, grad_one, grad_two = deliver(results)
    shards = [g.reshape(-1)[:length] for g, length in zip((grad_one, grad_two), lengths)]
    return (jnp.swapaxes(activations, 1, 2), jnp.swapaxes(grad_features, 1, 2), *shards)


def solution(mesh):
    plan = Plan(dict(mesh.shape))
    rows = P(("dp", "fsdp"), None, None)
    flat = P(("dp", "fsdp"))
    return jax.shard_map(
        functools.partial(on_device, plan),
        mesh=mesh,
        in_specs=(rows, flat, flat, flat, rows),
        out_specs=(rows, rows, flat, flat),
        check_vma=False,
    )
```

```python
import functools
import math

import jax
import jax.numpy as jnp
from jax import lax
from jax.experimental import pallas as pl
from jax.experimental.pallas import tpu as pltpu
from jax.sharding import PartitionSpec as P

D = 192
HEADS = 8
FF = 256
HEAD_DIM = 24
PAD = 32
AUG = 208
HID = 272
GROUP = 4
LAG = 2
CHUNK = 1024
EPS = 1e-5
MASK = -4e30
SCALE = HEAD_DIM**-0.5
LOG2E = math.log2(math.e)
MATS = 1152
BF = jnp.bfloat16
F32 = jnp.float32


def nn(left, right):
    return lax.dot_general(left, right, (((1,), (0,)), ((), ())), preferred_element_type=F32)


def nt(left, right):
    return lax.dot_general(left, right, (((1,), (1,)), ((), ())), preferred_element_type=F32)


def tn(left, right):
    return lax.dot_general(left, right, (((0,), (0,)), ((), ())), preferred_element_type=F32)


def lanes_low(rows):
    return lax.broadcasted_iota(jnp.int32, (rows, 128), 1) < 64


def half_turn(values):
    return pltpu.roll(values, 64, 1)


def read_wide(flat, start, rows, pair):
    count = rows // 2
    first = flat[pl.ds(start, count, stride=3), :]
    second = flat[pl.ds(start + 1, count, stride=3), :]
    third = half_turn(flat[pl.ds(start + 2, count, stride=3), :])
    pair[0, pl.ds(0, count, stride=2), :] = first
    pair[1, pl.ds(0, count, stride=2), :] = second
    pair[0, pl.ds(1, count, stride=2), :] = jnp.where(lanes_low(count), half_turn(second), third)
    pair[1, pl.ds(1, count, stride=2), :] = third
    return jnp.concatenate([pair[0, :rows, :], pair[1, :rows, :64]], axis=1)


def write_wide(flat, start, values, pair):
    rows = values.shape[0]
    count = rows // 2
    pair[0, :rows, :] = values[:, :128]
    pair[1, :rows, :64] = values[:, 128:]
    low = lanes_low(count)
    even_low = pair[0, pl.ds(0, count, stride=2), :]
    even_high = pair[1, pl.ds(0, count, stride=2), :]
    odd_low = half_turn(pair[0, pl.ds(1, count, stride=2), :])
    odd_high = half_turn(pair[1, pl.ds(1, count, stride=2), :])
    flat[pl.ds(start, count, stride=3), :] = even_low
    flat[pl.ds(start + 1, count, stride=3), :] = jnp.where(low, even_high, odd_low)
    flat[pl.ds(start + 2, count, stride=3), :] = jnp.where(low, odd_low, odd_high)


def vector_names(leading):
    names = ["b_query", "b_value", "b_output"]
    if not leading:
        names = names + ["gain_attn", "bias_attn"]
    return names + ["gain_ffn", "bias_ffn"]


def spread():
    row = lax.broadcasted_iota(jnp.int32, (HEADS * PAD, D), 0)
    col = lax.broadcasted_iota(jnp.int32, (HEADS * PAD, D), 1)
    inside = (row & (PAD - 1)) < HEAD_DIM
    source = (row >> 5) * HEAD_DIM + (row & (PAD - 1))
    return jnp.where(inside & (source == col), 1.0, 0.0).astype(BF)


def identity(size):
    row = lax.broadcasted_iota(jnp.int32, (size, size), 0)
    col = lax.broadcasted_iota(jnp.int32, (size, size), 1)
    return jnp.where(row == col, 1.0, 0.0).astype(BF)


def unit_entry(column):
    row = lax.broadcasted_iota(jnp.int32, (HEADS * PAD, AUG), 0)
    col = lax.broadcasted_iota(jnp.int32, (HEADS * PAD, AUG), 1)
    return jnp.where(((row & (PAD - 1)) == HEAD_DIM) & (col == column), 1.0, 0.0)


def column(row_vec):
    return jnp.broadcast_to(row_vec, (128, D)).T


def augment(matrix, bias):
    width = matrix.shape[1]
    return jnp.concatenate([matrix, bias, jnp.zeros((AUG - D - 1, width), F32)], axis=0).astype(BF)


def unpack_vectors(flat, leading, pair):
    names = vector_names(leading)
    vecs = read_wide(flat, MATS, len(names) + 1, pair)
    return {name: vecs[i : i + 1, :] for i, name in enumerate(names)}


def unpack_attention(flat, w, leading, pair):
    vec = unpack_vectors(flat, leading, pair)
    put = spread()
    zero_row = jnp.zeros((1, D), F32)
    for i, (bias, spare) in enumerate((("b_query", D), (None, D + 1), ("b_value", D))):
        mat = read_wide(flat, 288 * i, D, pair)
        aug = augment(mat, vec[bias] if bias else zero_row)
        w.qkv[i] = aug[:D]
        w.qkv_t[i] = (nt(put, aug) + unit_entry(spare)).astype(BF)
    if not leading:
        w.cols[3] = column(vec["gain_attn"])
        w.cols[4] = column(vec["bias_attn"])


def unpack_rest(flat, w, leading, pair, tail):
    names = vector_names(leading)
    vec = unpack_vectors(flat, leading, pair)
    put = spread()
    aug = augment(read_wide(flat, 864, D, pair), vec["b_output"])
    w.out_t[...] = nt(identity(D), aug).astype(BF)
    w.out_pad[...] = nn(put, aug[:D]).astype(BF)
    start = MATS + len(names) * 3 // 2
    count = 1160
    turned = half_turn(flat[pl.ds(start, count + 8), :])
    tail[:count, :] = jnp.where(lanes_low(count), turned[:count], turned[1 : count + 1])
    aug = augment(
        jnp.concatenate([tail[pl.ds(j, D, stride=4), :] for j in range(4)], axis=1),
        jnp.concatenate([tail[768 + j : 769 + j, :] for j in range(4)], axis=1),
    )
    w.inner[...] = aug[:D]
    for half in range(2):
        cols = slice(half * FF, (half + 1) * FF)
        w.inner_t[cols, :] = nt(identity(FF), aug[:, cols]).astype(BF)
    outer = read_wide(tail, 772, FF, pair).astype(BF)
    w.outer[...] = outer
    w.outer_t[...] = nt(identity(D), outer).astype(BF)
    b_outer = jnp.concatenate([tail[1156:1157, :], tail[1157:1158, :64]], axis=1)
    w.cols[0] = column(b_outer)
    w.cols[1] = column(vec["gain_ffn"])
    w.cols[2] = column(vec["bias_ffn"])


class Group:
    def __init__(self, **refs):
        self.__dict__.update(refs)


def wide(col):
    return jnp.concatenate([col] * (CHUNK // 128), axis=1)


def norm(values):
    center = values - jnp.sum(values, axis=0, keepdims=True) * (1.0 / D)
    inverse = lax.rsqrt(jnp.sum(center * center, axis=0, keepdims=True) * (1.0 / D) + EPS)
    return center * inverse, inverse


def norm_back(grad, normed, inverse, gain):
    scaled = grad * gain
    mean = jnp.sum(scaled, axis=0, keepdims=True) * (1.0 / D)
    cross = jnp.sum(scaled * normed, axis=0, keepdims=True) * (1.0 / D)
    return inverse * (scaled - mean - normed * cross)


def chunks(tokens, body):
    for start in range(0, tokens, CHUNK):
        body(pl.ds(start, CHUNK))


def place(u, seq):
    if isinstance(u, int):
        row, head = divmod(u, HEADS)
        return head, pl.ds(head * PAD, PAD), pl.ds(head * HEAD_DIM, HEAD_DIM), pl.ds(row * seq, seq)
    row = lax.div(u, HEADS)
    head = u - row * HEADS
    return (
        head,
        pl.ds(pl.multiple_of(head * PAD, PAD), PAD),
        pl.ds(pl.multiple_of(head * HEAD_DIM, 8), HEAD_DIM),
        pl.ds(pl.multiple_of(row * seq, seq), seq),
    )


def grouped_loop(units, body, hooks):
    groups = units // GROUP

    def step(g, carry):
        for j in range(GROUP):
            body(j, lambda back: lax.rem(g * GROUP + (j - back + units), units))
        return carry

    hooks = {min(g, groups - 1): hook for g, hook in hooks.items()}
    cuts = sorted({0, groups, *hooks})
    for first, last in zip(cuts, cuts[1:]):
        if first in hooks:
            hooks[first]()
        lax.fori_loop(first, last, step, 0)


def attend_forward(s, a, seq, row_count, hooks):
    units = row_count * HEADS

    def score(u, slot):
        _, rows, _, cols = place(u, seq)
        key = a.key[rows, cols]
        keys = jnp.concatenate([key, key], axis=0)
        query = jnp.concatenate([s.high[rows, cols], s.low[rows, cols]], axis=0)
        scores = tn(keys, query)
        s.scores[slot] = scores
        s.top[slot] = jnp.max(scores, axis=0, keepdims=True)

    def expo(u, slot):
        a.expo[u] = jnp.exp2(s.scores[slot] - s.top[slot]).astype(BF)

    def mix(u):
        head, rows, compact, cols = place(u, seq)
        total = nn(a.value[rows, cols], a.expo[u])
        inverse = 1.0 / total[HEAD_DIM : HEAD_DIM + 1]
        mixed = total * inverse
        a.mixed[rows, cols] = mixed
        a.total[pl.ds(head, 1), cols] = inverse
        s.compact[0, compact, cols] = mixed[:HEAD_DIM]

    def body(j, unit):
        mix(unit(LAG + 1))
        expo(unit(LAG), (j - LAG) % GROUP)
        score(unit(0), j)

    grouped_loop(units, body, hooks)
    for u in range(units - LAG - 1, units):
        mix(u)
        if u + 1 < units:
            expo(u + 1, (u + 1) % GROUP)


def attend_backward(s, a, seq, row_count, hooks):
    units = row_count * HEADS

    def score(u, slot):
        _, rows, compact, cols = place(u, seq)
        value = a.value[rows, cols]
        grad_hi = s.high[rows, cols]
        values = jnp.concatenate([value, value], axis=0)
        grads = jnp.concatenate([grad_hi, s.low[rows, cols]], axis=0)
        expo = a.expo[u]
        grad_soft = tn(values, grads)
        s.grad_scores[slot] = (grad_soft * expo.astype(F32)).astype(BF)
        s.compact[2, compact, cols] = nt(grad_hi, expo)[:HEAD_DIM]

    def back(u, slot):
        _, rows, compact, cols = place(u, seq)
        grad_scores = s.grad_scores[slot]
        s.compact[1, compact, cols] = nt(a.query[rows, cols], grad_scores)[:HEAD_DIM] * SCALE
        s.compact[0, compact, cols] = nn(a.key[rows, cols], grad_scores)[:HEAD_DIM] * SCALE

    def body(j, unit):
        back(unit(1), (j - 1) % GROUP)
        score(unit(0), j)

    grouped_loop(units, body, hooks)
    back(units - 1, (units - 1) % GROUP)


def forward_project(s, a, w, source, leading, tokens):
    def body(cols):
        x = source[:, cols]
        if not leading:
            normed, inverse = norm(x)
            a.normed_attn[:, cols] = normed
            a.inverse_attn[:, cols] = inverse
            x = normed * wide(w.cols[3]) + wide(w.cols[4])
        a.attn_low[:D, cols] = x.astype(BF)
        low = a.attn_low[:, cols]
        query = nn(w.qkv_t[0], low).astype(BF)
        a.query[:, cols] = query
        scaled = query.astype(F32) * (SCALE * LOG2E)
        high = scaled.astype(BF)
        s.high[:, cols] = high
        s.low[:, cols] = (scaled - high.astype(F32)).astype(BF)
        a.key[:, cols] = nn(w.qkv_t[1], low).astype(BF)
        a.value[:, cols] = nn(w.qkv_t[2], low).astype(BF)

    chunks(tokens, body)


def forward_feed(s, a, w, source, target, tokens):
    def body(cols):
        a.mixed_low[:D, cols] = s.compact[0, :, cols].astype(BF)
        middle = source[:, cols] + nn(w.out_t[...], a.mixed_low[:, cols])
        normed, inverse = norm(middle)
        a.normed_ffn[:, cols] = normed
        a.inverse_ffn[:, cols] = inverse
        a.ffn_low[:D, cols] = (normed * wide(w.cols[1]) + wide(w.cols[2])).astype(BF)
        low = a.ffn_low[:, cols]
        linear = nn(w.inner_t[:FF, :], low)
        gate = nn(w.inner_t[FF:, :], low)
        sigmoid = 1.0 / (1.0 + jnp.exp2(gate * (-LOG2E)))
        silu = gate * sigmoid
        a.silu[:, cols] = silu
        a.slope[:, cols] = linear * sigmoid * (1.0 + gate * (1.0 - sigmoid))
        hidden = (linear * silu).astype(BF)
        a.hidden[:FF, cols] = hidden
        target[:, cols] = middle + nn(w.outer_t[...], hidden) + wide(w.cols[0])

    chunks(tokens, body)


def backward_feed(s, a, w, grad, tokens):
    s.sums[...] = jnp.zeros_like(s.sums)

    def body(cols):
        g = grad[:, cols]
        low = g.astype(BF)
        s.grad_branch[:, cols] = low
        grad_hidden = nn(w.outer[...], low)
        grad_linear = (grad_hidden * a.silu[:, cols]).astype(BF)
        grad_gate = (grad_hidden * a.slope[:, cols]).astype(BF)
        s.grad_inner[:FF, cols] = grad_linear
        s.grad_inner[FF:, cols] = grad_gate
        u = nn(w.inner[:, :FF], grad_linear) + nn(w.inner[:, FF:], grad_gate)
        normed = a.normed_ffn[:, cols]
        s.sums[0] += fold(u * normed)
        s.sums[1] += fold(u)
        middle = g + norm_back(u, normed, a.inverse_ffn[:, cols], wide(w.cols[1]))
        s.grad_middle[:, cols] = middle
        low = middle.astype(BF)
        s.grad_attn[:, cols] = low
        grad_mixed = nn(w.out_pad[...], low).astype(BF).astype(F32)
        for head in range(HEADS):
            rows = slice(head * PAD, (head + 1) * PAD)
            part = grad_mixed[rows]
            dot = jnp.sum(part * a.mixed[rows, cols], axis=0, keepdims=True)
            spare = lax.broadcasted_iota(jnp.int32, (PAD, CHUNK), 0) == HEAD_DIM
            part = jnp.where(spare, -dot, part) * a.total[head : head + 1, cols]
            high = part.astype(BF)
            s.high[rows, cols] = high
            s.low[rows, cols] = (part - high.astype(F32)).astype(BF)

    chunks(tokens, body)


def write_vectors(flat, leading, vecs, pair):
    names = vector_names(leading)
    last = MATS + len(names) * 3 // 2
    keep = flat[last : last + 8, :]
    zero = jnp.zeros((1, D), F32)
    stack = jnp.concatenate([vecs.get(name, zero) for name in names] + [zero], axis=0)
    write_wide(flat, MATS, stack, pair)
    flat[last : last + 8, :] = keep


def grads_feed(s, a, leading, flat, pair, tail):
    names = vector_names(leading)
    vecs = {}
    grads = nt(a.hidden[...], s.grad_branch[...])
    write_wide(tail, 8 + 772, grads[:FF], pair)
    tail[8 + 1156 : 8 + 1157, :] = grads[FF : FF + 1, :128]
    tail[8 + 1157 : 8 + 1158, :64] = grads[FF : FF + 1, 128:]
    tail[8 + 1157 : 8 + 1158, 64:] = jnp.zeros((1, 64), F32)
    tail[8 + 1158 :, :] = jnp.zeros_like(tail[8 + 1158 :, :])
    grads = nt(a.ffn_low[...], s.grad_inner[...])
    for j in range(4):
        cols = slice(128 * j, 128 * j + 128)
        tail[pl.ds(8 + j, D, stride=4), :] = grads[:D, cols]
        tail[8 + 768 + j : 8 + 769 + j, :] = grads[D : D + 1, cols]
    vecs["gain_ffn"] = sum_lanes(s.sums[0])
    vecs["bias_ffn"] = sum_lanes(s.sums[1])
    tail[7:8, 64:] = vecs["bias_ffn"][:, 128:]
    start = MATS + len(names) * 3 // 2
    count = 1160
    turned = half_turn(tail[pl.ds(0, count + 8), :])
    flat[pl.ds(start, count), :] = jnp.where(
        lanes_low(count), turned[7 : 7 + count], turned[8 : 8 + count]
    )
    grads = nt(a.mixed_low[...], s.grad_attn[...])
    write_wide(flat, 864, grads[:D], pair)
    vecs["b_output"] = grads[D : D + 1]
    write_vectors(flat, leading, vecs, pair)
    return vecs


def grads_attention(s, a, leading, flat, pair, vecs):
    for i, bias in enumerate(("b_query", None, "b_value")):
        s.grad_qkv[i] = s.compact[i].astype(BF)
        grads = nt(a.attn_low[...], s.grad_qkv[i])
        write_wide(flat, 288 * i, grads[:D], pair)
        if bias:
            vecs[bias] = grads[D : D + 1]


def backward_project(s, a, w, target, leading, tokens):
    s.sums[...] = jnp.zeros_like(s.sums)

    def body(cols):
        total = nn(w.qkv[0], s.grad_qkv[0, :, cols])
        total = total + nn(w.qkv[1], s.grad_qkv[1, :, cols])
        total = total + nn(w.qkv[2], s.grad_qkv[2, :, cols])
        if not leading:
            normed = a.normed_attn[:, cols]
            s.sums[0] += fold(total * normed)
            s.sums[1] += fold(total)
            total = norm_back(total, normed, a.inverse_attn[:, cols], wide(w.cols[3]))
        target[:, cols] = s.grad_middle[:, cols] + total

    chunks(tokens, body)


def fold(values):
    total = values[:, :128]
    for start in range(128, values.shape[1], 128):
        total = total + values[:, start : start + 128]
    return total


def sum_lanes(values):
    return jnp.sum(values.T, axis=0, keepdims=True)


def weight_shapes():
    return dict(
        qkv=((3, D, D), BF),
        qkv_t=((3, HEADS * PAD, AUG), BF),
        out_t=((D, AUG), BF),
        out_pad=((HEADS * PAD, D), BF),
        inner=((D, 2 * FF), BF),
        inner_t=((2 * FF, AUG), BF),
        outer=((FF, D), BF),
        outer_t=((D, FF), BF),
        cols=((5, D, 128), F32),
    )


def kept_shapes(tokens, seq, row_count):
    return dict(
        attn_low=((AUG, tokens), BF),
        query=((HEADS * PAD, tokens), BF),
        key=((HEADS * PAD, tokens), BF),
        value=((HEADS * PAD, tokens), BF),
        expo=((row_count * HEADS, seq, seq), BF),
        mixed=((HEADS * PAD, tokens), F32),
        total=((HEADS, tokens), F32),
        mixed_low=((AUG, tokens), BF),
        normed_ffn=((D, tokens), F32),
        inverse_ffn=((1, tokens), F32),
        ffn_low=((AUG, tokens), BF),
        silu=((FF, tokens), F32),
        slope=((FF, tokens), F32),
        hidden=((HID, tokens), BF),
    )


def norm_shapes(tokens):
    return dict(normed_attn=((D, tokens), F32), inverse_attn=((1, tokens), F32))


def shared_shapes(tokens, seq):
    return dict(
        scores=((GROUP, seq, seq), F32),
        top=((GROUP, 1, seq), F32),
        grad_scores=((GROUP, seq, seq), BF),
        compact=((3, D, tokens), F32),
        high=((HEADS * PAD, tokens), BF),
        low=((HEADS * PAD, tokens), BF),
        grad_branch=((D, tokens), BF),
        grad_inner=((2 * FF, tokens), BF),
        grad_middle=((D, tokens), F32),
        grad_attn=((D, tokens), BF),
        grad_qkv=((3, D, tokens), BF),
        sums=((2, D, 128), F32),
        grad_next=((D, tokens), F32),
        input_one=((D, tokens), F32),
        input_two=((D, tokens), F32),
        pair=((2, FF, 128), F32),
        tail=((1176, 128), F32),
    )


def fill_spare(group, widths, seq, row_count):
    tokens = seq * row_count
    row = lax.broadcasted_iota(jnp.int32, (AUG - D, tokens), 0)
    ones = jnp.where(row == 0, 1.0, 0.0)
    slot = lax.broadcasted_iota(jnp.int32, (AUG - D, seq), 1)
    masks = [jnp.where(slot < widths[r], 0.0, MASK) for r in range(row_count)]
    mask = jnp.where(row == 1, jnp.concatenate(masks, axis=1), 0.0)
    group.attn_low[D:, :] = (ones + mask).astype(BF)
    group.mixed_low[D:, :] = ones.astype(BF)
    group.ffn_low[D:, :] = ones.astype(BF)
    group.hidden[FF:, :] = ones.astype(BF)
MESH_ID = pl.DeviceIdType.MESH


class Plan:
    def __init__(self, mesh_shape):
        self.dp, self.fs = mesh_shape["dp"], mesh_shape["fsdp"]
        self.line = 2 ** ((self.dp.bit_length()) // 2)
        self.low = self.dp // self.line
        self.peers = self.low * self.fs // 2
        self.count = self.dp * self.fs

    def here(self):
        dp, fs = lax.axis_index("dp"), lax.axis_index("fsdp")
        half = self.fs // 2
        return dp // self.low, (dp % self.low) * half + fs // 2, fs % 2

    def device(self, hi, q, c):
        half = self.fs // 2
        return (hi * self.low + q // half, (q % half) * 2 + c)

    def shard(self, hi, q, c):
        return (hi * self.peers + q) * 2 + c

    def partners(self):
        hi, q, c = self.here()
        return (
            [self.device((hi + d) % self.line, q, c) for d in range(1, self.line)]
            + [self.device(hi, (q + d) % self.peers, c) for d in range(1, self.peers)]
            + [self.device(hi, q, 1 - c)]
        )

    def greet(self):
        barrier = pltpu.get_barrier_semaphore()
        for other in self.partners():
            pl.semaphore_signal(barrier, 1, device_id=other, device_id_type=MESH_ID)

    def meet(self):
        pl.semaphore_wait(pltpu.get_barrier_semaphore(), self.line + self.peers - 1)


def piece_rows(length):
    return -(-(length + 127) // 2048) * 16


def remote(source, target, sems, sent, received, device):
    return pltpu.make_async_remote_copy(
        source, target, sems.at[0, sent], sems.at[1, received], device_id=device, device_id_type=MESH_ID
    )


def send(source, target, sems, index, device):
    copy = remote(source, target, sems, index, index, device)
    copy.start()
    return copy


def place_shard(x, offset):
    turned = pltpu.roll(x, offset, 1)
    before = jnp.concatenate([jnp.zeros((1, 128), x.dtype), turned[:-1]], axis=0)
    lane = lax.broadcasted_iota(jnp.int32, x.shape, 1)
    return jnp.where(lane >= offset, turned, before)


def lift_shard(x, offset):
    turned = pltpu.roll(x, lax.rem(128 - offset, 128), 1)
    after = jnp.concatenate([turned[1:], turned[:1]], axis=0)
    lane = lax.broadcasted_iota(jnp.int32, x.shape, 1)
    return jnp.where(lane < 128 - offset, turned, after)


class Gather:
    def __init__(self, plan, sems, held, length, parts):
        self.plan, self.sems, self.held, self.length = plan, sems, held, length
        self.parts = parts
        self.across = [[] for _ in parts]
        self.pair = [[] for _ in parts]

    def steps(self, part):
        first, last = self.parts[part]
        if part > 0 or len(self.parts) == 1:
            return [(None, slice(first, last))]
        near = jnp.clip(self.plan.here()[0], first, last - 1)
        count = last - first
        indices = [first + lax.rem(near - first + count - k, count) for k in range(count)]
        return [(t, pl.ds(t, 1)) for t in indices]

    def base(self, part):
        p = self.plan
        return p.line + 2 * p.peers * (p.line if part else 0)

    def prepare(self, shard):
        p = self.plan
        hi, q, c = p.here()
        offset = lax.rem(p.shard(hi, q, c) * self.length, 128)
        self.held[c, q, hi] = place_shard(shard, offset).astype(BF)
        mine = self.held.at[c, q, hi]
        self.along = [
            remote(mine, mine, self.sems, d, hi, p.device((hi + d) % p.line, q, c)) for d in range(1, p.line)
        ]

    def begin(self, part):
        hi = self.plan.here()[0]
        first, last = self.parts[part]

        def start():
            for copy in self.along:
                copy.start()

        if (first, last) == (0, self.plan.line):
            start()
        else:
            pl.when((hi >= first) & (hi < last))(start)

    def await_line(self, t):
        p = self.plan
        hi, q, c = p.here()

        @pl.when(hi != t)
        def _():
            piece = self.held.at[c, q, t]
            remote(piece, piece, self.sems, 0, t, p.device(t, q, c)).wait_recv()

    def spread(self, part):
        p = self.plan
        hi, q, c = p.here()
        for k, (t, where) in enumerate(self.steps(part)):
            for index in range(*self.parts[part]) if t is None else [t]:
                self.await_line(index)
            mine = self.held.at[c, q, where]
            base = self.base(part) + 2 * p.peers * k
            self.across[part].append(
                [
                    send(mine, mine, self.sems, base + d, p.device(hi, (q + d) % p.peers, c))
                    for d in range(1, p.peers)
                ]
            )
            self.pair[part].append(send(mine, mine, self.sems, base, p.device(hi, q, 1 - c)))

    def mirror(self, part):
        p = self.plan
        hi, q, c = p.here()
        for k, (_, where) in enumerate(self.steps(part)):
            base = self.base(part) + 2 * p.peers * k + p.peers
            for d, copy in enumerate(self.across[part][k], 1):
                copy.wait_recv()
                piece = self.held.at[c, (q - d + p.peers) % p.peers, where]
                self.pair[part].append(send(piece, piece, self.sems, base + d, p.device(hi, q, 1 - c)))

    def finish(self, part):
        for copy in self.pair[part]:
            copy.wait_recv()

    def drain(self):
        for copy in self.along:
            copy.wait_send()
        for copies in self.pair + [copies for part in self.across for copies in part]:
            for copy in copies:
                copy.wait_send()

    def flatten(self, part, flat):
        p = self.plan
        rows = self.held.shape[3]
        first, last = self.parts[part]
        if part == 0:
            flat[0:8, :] = jnp.zeros((8, 128), F32)
        for hi in range(first, last):
            for q in range(p.peers):
                for c in range(2):
                    start = p.shard(hi, q, c) * self.length // 128
                    piece = self.held[c, q, hi].astype(F32)
                    flat[start : start + 1, :] += piece[:1]
                    flat[start + 1 : start + rows, :] = piece[1:]


def gather_sems(plan):
    return pltpu.SemaphoreType.DMA((2, plan.line + 2 * plan.peers * (plan.line + 1)))


class Reduce:
    def __init__(self, plan, sems, refs, length, part):
        self.plan, self.sems, self.r, self.length, self.part = plan, sems, refs, length, part

    def begin(self, flat):
        p, r = self.plan, self.r
        rows = r.mine.shape[3]
        first, last = self.part
        for hi in range(first, last):
            for q in range(p.peers):
                for c in range(2):
                    start = p.shard(hi, q, c) * self.length // 128
                    r.mine[c, q, hi - first] = flat[start : start + rows, :].astype(BF)
        hi, q, c = p.here()
        self.pair = {}
        for d in list(range(1, p.peers)) + [0]:
            peer = (q + d) % p.peers
            self.pair[d] = send(
                r.mine.at[1 - c, peer], r.pair.at[peer], self.sems, d, p.device(hi, q, 1 - c)
            )

    def join(self, d):
        p, r = self.plan, self.r
        hi, q, c = p.here()
        peer = (q + d) % p.peers
        self.pair[d].wait_recv()
        return r.mine[c, peer].astype(F32) + r.pair[peer].astype(F32)

    def across(self):
        p, r = self.plan, self.r
        hi, q, c = p.here()
        self.peers = []
        for d in range(1, p.peers):
            peer = (q + d) % p.peers
            r.both[d] = self.join(d).astype(BF)
            self.peers.append(
                send(r.both.at[d], r.peers.at[d], self.sems, p.peers + d, p.device(hi, peer, c))
            )
        r.own[...] = self.join(0)

    def lines(self):
        p, r = self.plan, self.r
        hi, q, c = p.here()
        first, last = self.part
        for t in range(first, last):
            slot = lax.rem(hi - t + p.line, p.line)
            yield t, remote(
                r.plane.at[t - first],
                r.line.at[slot],
                self.sems,
                2 * p.peers + t,
                2 * p.peers + slot,
                p.device(t, q, c),
            )

    def along(self):
        p, r = self.plan, self.r
        hi, q, c = p.here()
        total = r.own[...]
        for d, copy in enumerate(self.peers, 1):
            copy.wait_recv()
            total = total + r.peers[d].astype(F32)
        r.plane[...] = total.astype(BF)
        for t, copy in self.lines():

            @pl.when(hi != t)
            def _():
                copy.start()

    def finish(self, out):
        p, r = self.plan, self.r
        hi, q, c = p.here()
        first, last = self.part

        def collect():
            total = r.plane[hi - first].astype(F32)
            for d in range(1, p.line):
                index = 2 * p.peers + d
                source = p.device((hi + d) % p.line, q, c)
                remote(r.line.at[d], r.line.at[d], self.sems, 0, index, source).wait_recv()
                total = total + r.line[d].astype(F32)
            offset = lax.rem(p.shard(hi, q, c) * self.length, 128)
            out[...] = lift_shard(total, offset)

        if (first, last) == (0, p.line):
            collect()
        else:
            pl.when((hi >= first) & (hi < last))(collect)
        for copy in self.pair.values():
            copy.wait_send()
        for copy in self.peers:
            copy.wait_send()
        for t, copy in self.lines():

            @pl.when(hi != t)
            def _():
                copy.wait_send()


def reduce_shapes(plan, rows, part):
    wide_part = part[1] - part[0]
    return dict(
        mine=((2, plan.peers, wide_part, rows, 128), BF),
        pair=((plan.peers, wide_part, rows, 128), BF),
        both=((plan.peers, wide_part, rows, 128), BF),
        peers=((plan.peers, wide_part, rows, 128), BF),
        own=((wide_part, rows, 128), F32),
        plane=((wide_part, rows, 128), BF),
        line=((plan.line, rows, 128), BF),
    )


def reduce_sems(plan):
    return pltpu.SemaphoreType.DMA((2, 2 * plan.peers + plan.line))
def vmem():
    return pl.BlockSpec(memory_space=pltpu.VMEM)


def hbm():
    return pl.BlockSpec(memory_space=pl.ANY)


def scratch(*dicts):
    shapes, names = [], []
    for entry in dicts:
        names.append(list(entry))
        shapes += [pltpu.VMEM(*entry[name]) for name in entry]
    return shapes, names


def grouped(names, refs):
    it = iter(refs)
    return [Group(**{name: next(it) for name in entry}) for entry in names]


def shard_rows(ref, rows):
    fill = jnp.zeros((rows * 128 - ref.shape[0],), F32)
    return jnp.concatenate([ref[...], fill]).reshape(rows, 128)


def row_copies(source, target, sems, base, seq, row_count, out):
    copies = []
    for r in range(row_count):
        inside = target.at[:, pl.ds(r * seq, seq)]
        outside = source.at[r]
        pair = (inside, outside) if out else (outside, inside)
        copies.append(pltpu.make_async_copy(*pair, sems.at[base + r]))
    return copies


def whole_kernel(plan, lengths, names, halves, seq, row_count, *refs):
    widths, one, two, features, out_grad, activations, grad_features, out_one, out_two = refs[:9]
    sem_one, sem_two, red_early, red_late, red_two, io = refs[9:15]
    w_one, w_two, a_one, a_two, s, h, r_early, r_late, r_two = grouped(names, refs[15:])
    tokens = seq * row_count
    everything = (0, plan.line)
    plan.greet()
    loads = row_copies(features, s.input_one, io, 0, seq, row_count, False)
    loads_grad = row_copies(out_grad, s.grad_next, io, row_count, seq, row_count, False)
    for copy in loads:
        copy.start()
    live = [widths[r] for r in range(row_count)]
    for a in (a_one, a_two):
        fill_spare(a, live, seq, row_count)
    gather_one = Gather(plan, sem_one, h.one, lengths[0], halves)
    gather_two = Gather(plan, sem_two, h.two, lengths[1], halves)
    gather_one.prepare(shard_rows(one, h.one.shape[3]))
    gather_two.prepare(shard_rows(two, h.two.shape[3]))
    plan.meet()
    gather_one.begin(0)
    gather_one.spread(0)
    gather_one.begin(1)
    gather_one.mirror(0)
    gather_two.begin(0)
    for copy in loads:
        copy.wait()
    gather_one.finish(0)
    gather_one.flatten(0, h.flat)
    unpack_attention(h.flat, w_one, True, s.pair)
    forward_project(s, a_one, w_one, s.input_one, True, tokens)
    gather_one.spread(1)
    attend_forward(
        s,
        a_one,
        seq,
        row_count,
        {1: lambda: gather_two.spread(0), 3: lambda: gather_one.mirror(1)},
    )
    gather_two.mirror(0)
    gather_one.finish(1)
    gather_two.begin(1)
    gather_one.flatten(1, h.flat)
    unpack_rest(h.flat, w_one, True, s.pair, s.tail)
    forward_feed(s, a_one, w_one, s.input_one, s.input_two, tokens)
    gather_two.finish(0)
    gather_two.flatten(0, h.flat)
    unpack_attention(h.flat, w_two, False, s.pair)
    forward_project(s, a_two, w_two, s.input_two, False, tokens)
    for copy in loads_grad:
        copy.start()
    attend_forward(
        s,
        a_two,
        seq,
        row_count,
        {1: lambda: gather_two.spread(1), 3: lambda: gather_two.mirror(1)},
    )
    gather_two.finish(1)
    gather_two.flatten(1, h.flat)
    unpack_rest(h.flat, w_two, False, s.pair, s.tail)
    forward_feed(s, a_two, w_two, s.input_two, s.input_one, tokens)
    gather_one.drain()
    gather_two.drain()
    stores = row_copies(activations, s.input_one, io, 2 * row_count, seq, row_count, True)
    for copy in stores:
        copy.start()
    for copy in loads_grad:
        copy.wait()

    reduce_two = Reduce(plan, red_two, r_two, lengths[1], everything)
    reduce_early = Reduce(plan, red_early, r_early, lengths[0], halves[1])
    reduce_late = Reduce(plan, red_late, r_late, lengths[0], halves[0])
    backward_feed(s, a_two, w_two, s.grad_next, tokens)
    vecs = grads_feed(s, a_two, False, h.flat, s.pair, s.tail)
    attend_backward(s, a_two, seq, row_count, {})
    grads_attention(s, a_two, False, h.flat, s.pair, vecs)
    backward_project(s, a_two, w_two, s.grad_next, False, tokens)
    vecs["gain_attn"] = sum_lanes(s.sums[0])
    vecs["bias_attn"] = sum_lanes(s.sums[1])
    write_vectors(h.flat, False, vecs, s.pair)
    reduce_two.begin(h.flat)
    backward_feed(s, a_one, w_one, s.grad_next, tokens)
    vecs = grads_feed(s, a_one, True, h.flat, s.pair, s.tail)
    reduce_early.begin(h.flat)
    reduce_two.across()
    attend_backward(s, a_one, seq, row_count, {2: reduce_early.across})
    reduce_two.along()
    reduce_early.along()
    grads_attention(s, a_one, True, h.flat, s.pair, vecs)
    write_vectors(h.flat, True, vecs, s.pair)
    reduce_late.begin(h.flat)
    backward_project(s, a_one, w_one, s.input_two, True, tokens)
    reduce_late.across()
    last = row_copies(grad_features, s.input_two, io, 3 * row_count, seq, row_count, True)
    for copy in last:
        copy.start()
    reduce_two.finish(out_two)
    reduce_early.finish(out_one)
    reduce_late.along()
    for copy in stores + last:
        copy.wait()
    reduce_late.finish(out_one)


def deliver_kernel(count, *refs):
    sources, targets, held = refs[:count], refs[count : 2 * count], refs[2 * count : 3 * count]
    sems = refs[3 * count]
    inward = [pltpu.make_async_copy(a, b, sems.at[0, i]) for i, (a, b) in enumerate(zip(sources, held))]
    outward = [pltpu.make_async_copy(a, b, sems.at[1, i]) for i, (a, b) in enumerate(zip(held, targets))]
    for copy in inward:
        copy.start()
    for first, second in zip(inward, outward):
        first.wait()
        second.start()
    for copy in outward:
        copy.wait()


def deliver(arrays):
    count = len(arrays)
    return pl.pallas_call(
        functools.partial(deliver_kernel, count),
        out_shape=[jax.ShapeDtypeStruct(x.shape, x.dtype) for x in arrays],
        in_specs=[hbm()] * count,
        out_specs=[hbm()] * count,
        scratch_shapes=[pltpu.VMEM(x.shape, x.dtype) for x in arrays]
        + [pltpu.SemaphoreType.DMA((2, count))],
        name="deliver",
    )(*arrays)


def on_device(plan, features, widths, params_one, params_two, out_grad):
    row_count, seq, _ = features.shape
    tokens = row_count * seq
    lengths = [params_one.shape[0], params_two.shape[0]]
    rows = [piece_rows(length) for length in lengths]
    flat_rows = [plan.count * length // 128 for length in lengths]
    room = max(2360, max(flat_rows) + max(rows) + 16) // 8 * 8
    halves = [(0, plan.line // 2), (plan.line // 2, plan.line)]
    everything = (0, plan.line)
    held = {
        name: ((2, plan.peers, plan.line, r, 128), BF) for name, r in zip(("one", "two"), rows)
    }
    kept = kept_shapes(tokens, seq, row_count)
    shapes, names = scratch(
        weight_shapes(),
        weight_shapes(),
        kept,
        {**kept, **norm_shapes(tokens)},
        shared_shapes(tokens, seq),
        {**held, "flat": ((room, 128), F32)},
        reduce_shapes(plan, rows[0], halves[1]),
        reduce_shapes(plan, rows[0], halves[0]),
        reduce_shapes(plan, rows[1], everything),
    )
    sems = [gather_sems(plan)] * 2 + [reduce_sems(plan)] * 3
    sems.append(pltpu.SemaphoreType.DMA((4 * row_count,)))
    turned = jax.ShapeDtypeStruct((row_count, D, seq), F32)
    results = pl.pallas_call(
        functools.partial(whole_kernel, plan, lengths, names, halves, seq, row_count),
        out_shape=[turned, turned] + [jax.ShapeDtypeStruct((r, 128), F32) for r in rows],
        in_specs=[pl.BlockSpec(memory_space=pltpu.SMEM), vmem(), vmem(), hbm(), hbm()],
        out_specs=[hbm(), hbm(), vmem(), vmem()],
        scratch_shapes=sems + shapes,
        compiler_params=pltpu.CompilerParams(
            vmem_limit_bytes=62 * 2**20, collective_id=0, has_side_effects=True
        ),
        name="blocks",
    )(widths, params_one, params_two, jnp.swapaxes(features, 1, 2), jnp.swapaxes(out_grad, 1, 2))
    activations, grad_features, grad_one, grad_two = deliver(results)
    shards = [g.reshape(-1)[:length] for g, length in zip((grad_one, grad_two), lengths)]
    return (jnp.swapaxes(activations, 1, 2), jnp.swapaxes(grad_features, 1, 2), *shards)


def solution(mesh):
    plan = Plan(dict(mesh.shape))
    rows = P(("dp", "fsdp"), None, None)
    flat = P(("dp", "fsdp"))
    return jax.shard_map(
        functools.partial(on_device, plan),
        mesh=mesh,
        in_specs=(rows, flat, flat, flat, rows),
        out_specs=(rows, rows, flat, flat),
        check_vma=False,
    )
```

```python
import functools
import math

import jax
import jax.numpy as jnp
from jax import lax
from jax.experimental import pallas as pl
from jax.experimental.pallas import tpu as pltpu
from jax.sharding import PartitionSpec as P

D = 192
HEADS = 8
FF = 256
HEAD_DIM = 24
PAD = 32
AUG = 208
HID = 272
GROUP = 4
SLOTS = 3
LAG = 2
EPS = 1e-5
MASK = -4e30
SCALE = HEAD_DIM**-0.5
LOG2E = math.log2(math.e)
MATS = 1152
BF = jnp.bfloat16
F32 = jnp.float32


def nn(left, right):
    return lax.dot_general(left, right, (((1,), (0,)), ((), ())), preferred_element_type=F32)


def nt(left, right):
    return lax.dot_general(left, right, (((1,), (1,)), ((), ())), preferred_element_type=F32)


def tn(left, right):
    return lax.dot_general(left, right, (((0,), (0,)), ((), ())), preferred_element_type=F32)


def lanes_low(rows):
    return lax.broadcasted_iota(jnp.int32, (rows, 128), 1) < 64


def half_turn(values):
    return pltpu.roll(values, 64, 1)


def read_wide(flat, start, rows, pair):
    count = rows // 2
    first = flat[pl.ds(start, count, stride=3), :]
    second = flat[pl.ds(start + 1, count, stride=3), :]
    third = half_turn(flat[pl.ds(start + 2, count, stride=3), :])
    pair[0, pl.ds(0, count, stride=2), :] = first
    pair[1, pl.ds(0, count, stride=2), :] = second
    pair[0, pl.ds(1, count, stride=2), :] = jnp.where(lanes_low(count), half_turn(second), third)
    pair[1, pl.ds(1, count, stride=2), :] = third
    return jnp.concatenate([pair[0, :rows, :], pair[1, :rows, :64]], axis=1)


def write_wide(flat, start, values, pair):
    rows = values.shape[0]
    count = rows // 2
    pair[0, :rows, :] = values[:, :128]
    pair[1, :rows, :64] = values[:, 128:]
    low = lanes_low(count)
    even_low = pair[0, pl.ds(0, count, stride=2), :]
    even_high = pair[1, pl.ds(0, count, stride=2), :]
    odd_low = half_turn(pair[0, pl.ds(1, count, stride=2), :])
    odd_high = half_turn(pair[1, pl.ds(1, count, stride=2), :])
    flat[pl.ds(start, count, stride=3), :] = even_low
    flat[pl.ds(start + 1, count, stride=3), :] = jnp.where(low, even_high, odd_low)
    flat[pl.ds(start + 2, count, stride=3), :] = jnp.where(low, odd_low, odd_high)


def vector_names(leading):
    names = ["b_query", "b_value", "b_output"]
    if not leading:
        names = names + ["gain_attn", "bias_attn"]
    return names + ["gain_ffn", "bias_ffn"]


def spread():
    row = lax.broadcasted_iota(jnp.int32, (HEADS * PAD, D), 0)
    col = lax.broadcasted_iota(jnp.int32, (HEADS * PAD, D), 1)
    inside = (row & (PAD - 1)) < HEAD_DIM
    source = (row >> 5) * HEAD_DIM + (row & (PAD - 1))
    return jnp.where(inside & (source == col), 1.0, 0.0).astype(BF)


def identity(size):
    row = lax.broadcasted_iota(jnp.int32, (size, size), 0)
    col = lax.broadcasted_iota(jnp.int32, (size, size), 1)
    return jnp.where(row == col, 1.0, 0.0).astype(BF)


def unit_entry(column):
    row = lax.broadcasted_iota(jnp.int32, (HEADS * PAD, AUG), 0)
    col = lax.broadcasted_iota(jnp.int32, (HEADS * PAD, AUG), 1)
    return jnp.where(((row & (PAD - 1)) == HEAD_DIM) & (col == column), 1.0, 0.0)


def column(row_vec):
    return jnp.broadcast_to(row_vec, (128, D)).T


def augment(matrix, bias):
    width = matrix.shape[1]
    return jnp.concatenate([matrix, bias, jnp.zeros((AUG - D - 1, width), F32)], axis=0).astype(BF)


def unpack_vectors(flat, leading, pair):
    names = vector_names(leading)
    vecs = read_wide(flat, MATS, len(names) + 1, pair)
    return {name: vecs[i : i + 1, :] for i, name in enumerate(names)}


def unpack_attention(flat, w, leading, pair):
    vec = unpack_vectors(flat, leading, pair)
    put = spread()
    zero_row = jnp.zeros((1, D), F32)
    for i, (bias, spare) in enumerate((("b_query", D), (None, D + 1), ("b_value", D))):
        mat = read_wide(flat, 288 * i, D, pair)
        aug = augment(mat, vec[bias] if bias else zero_row)
        w.qkv[i] = aug[:D]
        w.qkv_t[i] = (nt(put, aug) + unit_entry(spare)).astype(BF)
    if not leading:
        w.cols[3] = column(vec["gain_attn"])
        w.cols[4] = column(vec["bias_attn"])


def unpack_rest(flat, w, leading, pair, tail):
    names = vector_names(leading)
    vec = unpack_vectors(flat, leading, pair)
    put = spread()
    aug = augment(read_wide(flat, 864, D, pair), vec["b_output"])
    w.out_t[...] = nt(identity(D), aug).astype(BF)
    w.out_pad[...] = nn(put, aug[:D]).astype(BF)
    start = MATS + len(names) * 3 // 2
    count = 1160
    turned = half_turn(flat[pl.ds(start, count + 8), :])
    tail[:count, :] = jnp.where(lanes_low(count), turned[:count], turned[1 : count + 1])
    aug = augment(
        jnp.concatenate([tail[pl.ds(j, D, stride=4), :] for j in range(4)], axis=1),
        jnp.concatenate([tail[768 + j : 769 + j, :] for j in range(4)], axis=1),
    )
    w.inner[...] = aug[:D]
    for half in range(2):
        cols = slice(half * FF, (half + 1) * FF)
        w.inner_t[cols, :] = nt(identity(FF), aug[:, cols]).astype(BF)
    outer = read_wide(tail, 772, FF, pair).astype(BF)
    w.outer[...] = outer
    w.outer_t[...] = nt(identity(D), outer).astype(BF)
    b_outer = jnp.concatenate([tail[1156:1157, :], tail[1157:1158, :64]], axis=1)
    w.cols[0] = column(b_outer)
    w.cols[1] = column(vec["gain_ffn"])
    w.cols[2] = column(vec["bias_ffn"])


class Group:
    def __init__(self, **refs):
        self.__dict__.update(refs)


def wide(col, cols):
    return jnp.concatenate([col] * (cols.size // 128), axis=1)


def norm(values):
    center = values - jnp.sum(values, axis=0, keepdims=True) * (1.0 / D)
    inverse = lax.rsqrt(jnp.sum(center * center, axis=0, keepdims=True) * (1.0 / D) + EPS)
    return center * inverse, inverse


def norm_back(grad, normed, inverse, gain):
    scaled = grad * gain
    mean = jnp.sum(scaled, axis=0, keepdims=True) * (1.0 / D)
    cross = jnp.sum(scaled * normed, axis=0, keepdims=True) * (1.0 / D)
    return inverse * (scaled - mean - normed * cross)


def place(u, seq):
    row, head = divmod(u, HEADS)
    return head, pl.ds(head * PAD, PAD), pl.ds(head * HEAD_DIM, HEAD_DIM), pl.ds(row * seq, seq)


def grouped_units(units, body, hooks, beside):
    always = lax.axis_index("dp") >= 0
    for g in range(units // GROUP):
        hooks.get(g, lambda: None)()

        @pl.when(always)
        def _():
            beside.get(g, lambda: None)()
            for j in range(GROUP):
                body(g * GROUP + j)


def attend_forward(s, a, seq, row_count, hooks, beside):
    units = row_count * HEADS

    def score(u, slot):
        _, rows, _, cols = place(u, seq)
        key = a.key[rows, cols]
        keys = jnp.concatenate([key, key], axis=0)
        query = jnp.concatenate([s.high[rows, cols], s.low[rows, cols]], axis=0)
        scores = tn(keys, query)
        s.scores[slot] = scores
        s.top[slot] = jnp.max(scores, axis=0, keepdims=True)

    def expo(u, slot):
        a.expo[u] = jnp.exp2(s.scores[slot] - s.top[slot]).astype(BF)

    def mix(u):
        head, rows, compact, cols = place(u, seq)
        total = nn(a.value[rows, cols], a.expo[u])
        inverse = 1.0 / total[HEAD_DIM : HEAD_DIM + 1]
        mixed = total * inverse
        a.mixed[rows, cols] = mixed
        a.total[head : head + 1, cols] = inverse
        s.compact[0, compact, cols] = mixed[:HEAD_DIM]

    def body(u):
        if u > LAG:
            mix(u - LAG - 1)
        if u >= LAG:
            expo(u - LAG, (u - LAG) % SLOTS)
        score(u, u % SLOTS)

    grouped_units(units, body, hooks, beside)
    for u in range(units - LAG - 1, units):
        mix(u)
        if u + 1 < units:
            expo(u + 1, (u + 1) % SLOTS)


def attend_backward(s, a, seq, row_count, hooks, beside):
    units = row_count * HEADS

    def score(u, slot):
        _, rows, compact, cols = place(u, seq)
        value = a.value[rows, cols]
        grad_hi = s.high[rows, cols]
        values = jnp.concatenate([value, value], axis=0)
        grads = jnp.concatenate([grad_hi, s.low[rows, cols]], axis=0)
        expo = a.expo[u]
        grad_soft = tn(values, grads)
        s.grad_scores[slot] = (grad_soft * expo.astype(F32)).astype(BF)
        s.compact[2, compact, cols] = nt(grad_hi, expo)[:HEAD_DIM]

    def back(u, slot):
        _, rows, compact, cols = place(u, seq)
        grad_scores = s.grad_scores[slot]
        s.compact[1, compact, cols] = nt(a.query[rows, cols], grad_scores)[:HEAD_DIM] * SCALE
        s.compact[0, compact, cols] = nn(a.key[rows, cols], grad_scores)[:HEAD_DIM] * SCALE

    def body(u):
        if u > 0:
            back(u - 1, (u - 1) % 2)
        score(u, u % 2)

    grouped_units(units, body, hooks, beside)
    back(units - 1, (units - 1) % 2)


def forward_project(s, a, w, source, leading, cols):
    x = source[:, cols]
    if not leading:
        normed, inverse = norm(x)
        a.normed_attn[:, cols] = normed
        a.inverse_attn[:, cols] = inverse
        x = normed * wide(w.cols[3], cols) + wide(w.cols[4], cols)
    a.attn_low[:D, cols] = x.astype(BF)
    low = a.attn_low[:, cols]
    query = nn(w.qkv_t[0], low).astype(BF)
    a.query[:, cols] = query
    scaled = query.astype(F32) * (SCALE * LOG2E)
    high = scaled.astype(BF)
    s.high[:, cols] = high
    s.low[:, cols] = (scaled - high.astype(F32)).astype(BF)
    a.key[:, cols] = nn(w.qkv_t[1], low).astype(BF)
    a.value[:, cols] = nn(w.qkv_t[2], low).astype(BF)


def forward_feed(s, a, w, source, target, cols):
    a.mixed_low[:D, cols] = s.compact[0, :, cols].astype(BF)
    middle = source[:, cols] + nn(w.out_t[...], a.mixed_low[:, cols])
    normed, inverse = norm(middle)
    a.normed_ffn[:, cols] = normed
    a.inverse_ffn[:, cols] = inverse
    a.ffn_low[:D, cols] = (normed * wide(w.cols[1], cols) + wide(w.cols[2], cols)).astype(BF)
    low = a.ffn_low[:, cols]
    linear = nn(w.inner_t[:FF, :], low)
    gate = nn(w.inner_t[FF:, :], low)
    sigmoid = 1.0 / (1.0 + jnp.exp2(gate * (-LOG2E)))
    silu = gate * sigmoid
    a.silu[:, cols] = silu
    a.slope[:, cols] = linear * sigmoid * (1.0 + gate * (1.0 - sigmoid))
    hidden = (linear * silu).astype(BF)
    a.hidden[:FF, cols] = hidden
    target[:, cols] = middle + nn(w.outer_t[...], hidden) + wide(w.cols[0], cols)


def backward_feed(s, a, w, grad, cols):
    g = grad[:, cols]
    low = g.astype(BF)
    s.grad_branch[:, cols] = low
    grad_hidden = nn(w.outer[...], low)
    grad_linear = (grad_hidden * a.silu[:, cols]).astype(BF)
    grad_gate = (grad_hidden * a.slope[:, cols]).astype(BF)
    s.grad_inner[:FF, cols] = grad_linear
    s.grad_inner[FF:, cols] = grad_gate
    u = nn(w.inner[:, :FF], grad_linear) + nn(w.inner[:, FF:], grad_gate)
    normed = a.normed_ffn[:, cols]
    s.sums[0] += fold(u * normed)
    s.sums[1] += fold(u)
    middle = g + norm_back(u, normed, a.inverse_ffn[:, cols], wide(w.cols[1], cols))
    s.grad_middle[:, cols] = middle
    low = middle.astype(BF)
    s.grad_attn[:, cols] = low
    grad_mixed = nn(w.out_pad[...], low).astype(BF).astype(F32)
    for head in range(HEADS):
        rows = slice(head * PAD, (head + 1) * PAD)
        part = grad_mixed[rows]
        dot = jnp.sum(part * a.mixed[rows, cols], axis=0, keepdims=True)
        spare = lax.broadcasted_iota(jnp.int32, part.shape, 0) == HEAD_DIM
        part = jnp.where(spare, -dot, part) * a.total[head : head + 1, cols]
        high = part.astype(BF)
        s.high[rows, cols] = high
        s.low[rows, cols] = (part - high.astype(F32)).astype(BF)


def keep_vector(s, leading, name, value):
    row = vector_names(leading).index(name)
    s.vectors[row : row + 1, :] = value


def write_vectors(s, flat, leading, pair):
    count = len(vector_names(leading))
    last = MATS + count * 3 // 2
    keep = flat[last : last + 8, :]
    write_wide(flat, MATS, s.vectors[: count + 1, :], pair)
    flat[last : last + 8, :] = keep


def grads_feed(s, a, leading, flat, pair, tail):
    names = vector_names(leading)
    grads = nt(a.hidden[...], s.grad_branch[...])
    write_wide(tail, 8 + 772, grads[:FF], pair)
    tail[8 + 1156 : 8 + 1157, :] = grads[FF : FF + 1, :128]
    tail[8 + 1157 : 8 + 1158, :64] = grads[FF : FF + 1, 128:]
    tail[8 + 1157 : 8 + 1158, 64:] = jnp.zeros((1, 64), F32)
    tail[8 + 1158 :, :] = jnp.zeros_like(tail[8 + 1158 :, :])
    grads = nt(a.ffn_low[...], s.grad_inner[...])
    for j in range(4):
        cols = slice(128 * j, 128 * j + 128)
        tail[pl.ds(8 + j, D, stride=4), :] = grads[:D, cols]
        tail[8 + 768 + j : 8 + 769 + j, :] = grads[D : D + 1, cols]
    bias_ffn = sum_lanes(s.sums[1])
    keep_vector(s, leading, "gain_ffn", sum_lanes(s.sums[0]))
    keep_vector(s, leading, "bias_ffn", bias_ffn)
    tail[7:8, 64:] = bias_ffn[:, 128:]
    start = MATS + len(names) * 3 // 2
    count = 1160
    turned = half_turn(tail[pl.ds(0, count + 8), :])
    flat[pl.ds(start, count), :] = jnp.where(
        lanes_low(count), turned[7 : 7 + count], turned[8 : 8 + count]
    )
    grads = nt(a.mixed_low[...], s.grad_attn[...])
    write_wide(flat, 864, grads[:D], pair)
    keep_vector(s, leading, "b_output", grads[D : D + 1])
    write_vectors(s, flat, leading, pair)


def grads_attention(s, a, leading, flat, pair):
    for i, bias in enumerate(("b_query", None, "b_value")):
        grads = nt(a.attn_low[...], s.grad_qkv[i])
        write_wide(flat, 288 * i, grads[:D], pair)
        if bias:
            keep_vector(s, leading, bias, grads[D : D + 1])
    if not leading:
        keep_vector(s, leading, "gain_attn", sum_lanes(s.sums[2]))
        keep_vector(s, leading, "bias_attn", sum_lanes(s.sums[3]))
    write_vectors(s, flat, leading, pair)


def backward_begin(s):
    s.sums[...] = jnp.zeros_like(s.sums)
    s.vectors[...] = jnp.zeros_like(s.vectors)


def round_qkv(s, cols):
    for i in range(3):
        s.grad_qkv[i, :, cols] = s.compact[i, :, cols].astype(BF)


def backward_project(s, a, w, target, leading, cols):
    total = nn(w.qkv[0], s.grad_qkv[0, :, cols])
    total = total + nn(w.qkv[1], s.grad_qkv[1, :, cols])
    total = total + nn(w.qkv[2], s.grad_qkv[2, :, cols])
    if not leading:
        normed = a.normed_attn[:, cols]
        s.sums[2] += fold(total * normed)
        s.sums[3] += fold(total)
        total = norm_back(total, normed, a.inverse_attn[:, cols], wide(w.cols[3], cols))
    target[:, cols] = s.grad_middle[:, cols] + total


def fold(values):
    total = values[:, :128]
    for start in range(128, values.shape[1], 128):
        total = total + values[:, start : start + 128]
    return total


def sum_lanes(values):
    return jnp.sum(values.T, axis=0, keepdims=True)


def weight_shapes():
    return dict(
        qkv=((3, D, D), BF),
        qkv_t=((3, HEADS * PAD, AUG), BF),
        out_t=((D, AUG), BF),
        out_pad=((HEADS * PAD, D), BF),
        inner=((D, 2 * FF), BF),
        inner_t=((2 * FF, AUG), BF),
        outer=((FF, D), BF),
        outer_t=((D, FF), BF),
        cols=((5, D, 128), F32),
    )


def kept_shapes(tokens, seq, row_count):
    return dict(
        attn_low=((AUG, tokens), BF),
        query=((HEADS * PAD, tokens), BF),
        key=((HEADS * PAD, tokens), BF),
        value=((HEADS * PAD, tokens), BF),
        expo=((row_count * HEADS, seq, seq), BF),
        mixed=((HEADS * PAD, tokens), F32),
        total=((HEADS, tokens), F32),
        mixed_low=((AUG, tokens), BF),
        normed_ffn=((D, tokens), F32),
        inverse_ffn=((1, tokens), F32),
        ffn_low=((AUG, tokens), BF),
        silu=((FF, tokens), F32),
        slope=((FF, tokens), F32),
        hidden=((HID, tokens), BF),
    )


def norm_shapes(tokens):
    return dict(normed_attn=((D, tokens), F32), inverse_attn=((1, tokens), F32))


def shared_shapes(tokens, seq):
    return dict(
        scores=((SLOTS, seq, seq), F32),
        top=((SLOTS, 1, seq), F32),
        grad_scores=((2, seq, seq), BF),
        compact=((3, D, tokens), F32),
        high=((HEADS * PAD, tokens), BF),
        low=((HEADS * PAD, tokens), BF),
        grad_branch=((D, tokens), BF),
        grad_inner=((2 * FF, tokens), BF),
        grad_middle=((D, tokens), F32),
        grad_attn=((D, tokens), BF),
        grad_qkv=((3, D, tokens), BF),
        sums=((4, D, 128), F32),
        vectors=((8, D), F32),
        grad_next=((D, tokens), F32),
        input_one=((D, tokens), F32),
        input_two=((D, tokens), F32),
        pair=((2, FF, 128), F32),
        tail=((1176, 128), F32),
    )


def fill_spare(group, widths, seq, row_count):
    tokens = seq * row_count
    row = lax.broadcasted_iota(jnp.int32, (AUG - D, tokens), 0)
    ones = jnp.where(row == 0, 1.0, 0.0)
    slot = lax.broadcasted_iota(jnp.int32, (AUG - D, seq), 1)
    masks = [jnp.where(slot < widths[r], 0.0, MASK) for r in range(row_count)]
    mask = jnp.where(row == 1, jnp.concatenate(masks, axis=1), 0.0)
    group.attn_low[D:, :] = (ones + mask).astype(BF)
    group.mixed_low[D:, :] = ones.astype(BF)
    group.ffn_low[D:, :] = ones.astype(BF)
    group.hidden[FF:, :] = ones.astype(BF)
MESH_ID = pl.DeviceIdType.MESH


class Plan:
    def __init__(self, mesh_shape):
        self.dp, self.fs = mesh_shape["dp"], mesh_shape["fsdp"]
        self.line = 2 ** ((self.dp.bit_length()) // 2)
        self.low = self.dp // self.line
        self.peers = self.low * self.fs // 2
        self.count = self.dp * self.fs

    def here(self):
        dp, fs = lax.axis_index("dp"), lax.axis_index("fsdp")
        half = self.fs // 2
        return dp // self.low, (dp % self.low) * half + fs // 2, fs % 2

    def device(self, hi, q, c):
        half = self.fs // 2
        return (hi * self.low + q // half, (q % half) * 2 + c)

    def shard(self, hi, q, c):
        return (hi * self.peers + q) * 2 + c

    def partners(self):
        hi, q, c = self.here()
        return (
            [self.device((hi + d) % self.line, q, c) for d in range(1, self.line)]
            + [self.device(hi, (q + d) % self.peers, c) for d in range(1, self.peers)]
            + [self.device(hi, q, 1 - c)]
        )

    def greet(self):
        barrier = pltpu.get_barrier_semaphore()
        for other in self.partners():
            pl.semaphore_signal(barrier, 1, device_id=other, device_id_type=MESH_ID)

    def meet(self):
        pl.semaphore_wait(pltpu.get_barrier_semaphore(), self.line + self.peers - 1)


def piece_rows(length):
    return -(-(length + 127) // 2048) * 16


def remote(source, target, sems, sent, received, device):
    return pltpu.make_async_remote_copy(
        source, target, sems.at[0, sent], sems.at[1, received], device_id=device, device_id_type=MESH_ID
    )


def send(source, target, sems, index, device):
    copy = remote(source, target, sems, index, index, device)
    copy.start()
    return copy


def place_shard(x, offset):
    turned = pltpu.roll(x, offset, 1)
    before = jnp.concatenate([jnp.zeros((1, 128), x.dtype), turned[:-1]], axis=0)
    lane = lax.broadcasted_iota(jnp.int32, x.shape, 1)
    return jnp.where(lane >= offset, turned, before)


def lift_shard(x, offset):
    turned = pltpu.roll(x, lax.rem(128 - offset, 128), 1)
    after = jnp.concatenate([turned[1:], turned[:1]], axis=0)
    lane = lax.broadcasted_iota(jnp.int32, x.shape, 1)
    return jnp.where(lane < 128 - offset, turned, after)


class Gather:
    def __init__(self, plan, sems, held, length, parts):
        self.plan, self.sems, self.held, self.length = plan, sems, held, length
        self.parts = parts
        self.across = [[] for _ in parts]
        self.pair = [[] for _ in parts]

    def steps(self, part):
        first, last = self.parts[part]
        if part > 0 or len(self.parts) == 1:
            return [(None, slice(first, last))]
        near = jnp.clip(self.plan.here()[0], first, last - 1)
        count = last - first
        indices = [first + lax.rem(near - first + count - k, count) for k in range(count)]
        return [(t, pl.ds(t, 1)) for t in indices]

    def base(self, part):
        p = self.plan
        return p.line + 2 * p.peers * (p.line if part else 0)

    def prepare(self, shard):
        p = self.plan
        hi, q, c = p.here()
        offset = lax.rem(p.shard(hi, q, c) * self.length, 128)
        self.held[c, q, hi] = place_shard(shard, offset).astype(BF)
        mine = self.held.at[c, q, hi]
        self.along = [
            remote(mine, mine, self.sems, d, hi, p.device((hi + d) % p.line, q, c)) for d in range(1, p.line)
        ]

    def begin(self, part):
        hi = self.plan.here()[0]
        first, last = self.parts[part]

        def start():
            for copy in self.along:
                copy.start()

        if (first, last) == (0, self.plan.line):
            start()
        else:
            pl.when((hi >= first) & (hi < last))(start)

    def await_line(self, t):
        p = self.plan
        hi, q, c = p.here()

        @pl.when(hi != t)
        def _():
            piece = self.held.at[c, q, t]
            remote(piece, piece, self.sems, 0, t, p.device(t, q, c)).wait_recv()

    def spread(self, part):
        p = self.plan
        hi, q, c = p.here()
        for k, (t, where) in enumerate(self.steps(part)):
            for index in range(*self.parts[part]) if t is None else [t]:
                self.await_line(index)
            mine = self.held.at[c, q, where]
            base = self.base(part) + 2 * p.peers * k
            self.across[part].append(
                [
                    send(mine, mine, self.sems, base + d, p.device(hi, (q + d) % p.peers, c))
                    for d in range(1, p.peers)
                ]
            )
            self.pair[part].append(send(mine, mine, self.sems, base, p.device(hi, q, 1 - c)))

    def mirror(self, part):
        p = self.plan
        hi, q, c = p.here()
        for k, (_, where) in enumerate(self.steps(part)):
            base = self.base(part) + 2 * p.peers * k + p.peers
            for d, copy in enumerate(self.across[part][k], 1):
                copy.wait_recv()
                piece = self.held.at[c, (q - d + p.peers) % p.peers, where]
                self.pair[part].append(send(piece, piece, self.sems, base + d, p.device(hi, q, 1 - c)))

    def finish(self, part):
        for copy in self.pair[part]:
            copy.wait_recv()

    def drain(self):
        for copy in self.along:
            copy.wait_send()
        for copies in self.pair + [copies for part in self.across for copies in part]:
            for copy in copies:
                copy.wait_send()

    def flatten(self, part, flat):
        p = self.plan
        rows = self.held.shape[3]
        first, last = self.parts[part]
        if part == 0:
            flat[0:8, :] = jnp.zeros((8, 128), F32)
        for hi in range(first, last):
            for q in range(p.peers):
                for c in range(2):
                    start = p.shard(hi, q, c) * self.length // 128
                    piece = self.held[c, q, hi].astype(F32)
                    flat[start : start + 1, :] += piece[:1]
                    flat[start + 1 : start + rows, :] = piece[1:]


def gather_sems(plan):
    return pltpu.SemaphoreType.DMA((2, plan.line + 2 * plan.peers * (plan.line + 1)))


class Reduce:
    def __init__(self, plan, sems, refs, length, part):
        self.plan, self.sems, self.r, self.length, self.part = plan, sems, refs, length, part

    def begin(self, flat):
        p, r = self.plan, self.r
        rows = r.mine.shape[3]
        first, last = self.part
        for hi in range(first, last):
            for q in range(p.peers):
                for c in range(2):
                    start = p.shard(hi, q, c) * self.length // 128
                    r.mine[c, q, hi - first] = flat[start : start + rows, :].astype(BF)
        hi, q, c = p.here()
        self.pair = {}
        for d in list(range(1, p.peers)) + [0]:
            peer = (q + d) % p.peers
            self.pair[d] = send(
                r.mine.at[1 - c, peer], r.pair.at[peer], self.sems, d, p.device(hi, q, 1 - c)
            )

    def join(self, d):
        p, r = self.plan, self.r
        hi, q, c = p.here()
        peer = (q + d) % p.peers
        self.pair[d].wait_recv()
        return r.mine[c, peer].astype(F32) + r.pair[peer].astype(F32)

    def across(self):
        p, r = self.plan, self.r
        hi, q, c = p.here()
        self.peers = []
        for d in range(1, p.peers):
            peer = (q + d) % p.peers
            r.both[d] = self.join(d).astype(BF)
            self.peers.append(
                send(r.both.at[d], r.peers.at[d], self.sems, p.peers + d, p.device(hi, peer, c))
            )
        r.own[...] = self.join(0)

    def lines(self):
        p, r = self.plan, self.r
        hi, q, c = p.here()
        first, last = self.part
        for t in range(first, last):
            slot = lax.rem(hi - t + p.line, p.line)
            yield t, remote(
                r.plane.at[t - first],
                r.line.at[slot],
                self.sems,
                2 * p.peers + t,
                2 * p.peers + slot,
                p.device(t, q, c),
            )

    def along(self):
        p, r = self.plan, self.r
        hi, q, c = p.here()
        total = r.own[...]
        for d, copy in enumerate(self.peers, 1):
            copy.wait_recv()
            total = total + r.peers[d].astype(F32)
        r.plane[...] = total.astype(BF)
        for t, copy in self.lines():

            @pl.when(hi != t)
            def _():
                copy.start()

    def finish(self, out):
        p, r = self.plan, self.r
        hi, q, c = p.here()
        first, last = self.part

        def collect():
            total = r.plane[hi - first].astype(F32)
            for d in range(1, p.line):
                index = 2 * p.peers + d
                source = p.device((hi + d) % p.line, q, c)
                remote(r.line.at[d], r.line.at[d], self.sems, 0, index, source).wait_recv()
                total = total + r.line[d].astype(F32)
            offset = lax.rem(p.shard(hi, q, c) * self.length, 128)
            out[...] = lift_shard(total, offset)

        if (first, last) == (0, p.line):
            collect()
        else:
            pl.when((hi >= first) & (hi < last))(collect)
        for copy in self.pair.values():
            copy.wait_send()
        for copy in self.peers:
            copy.wait_send()
        for t, copy in self.lines():

            @pl.when(hi != t)
            def _():
                copy.wait_send()


def reduce_shapes(plan, rows, part):
    wide_part = part[1] - part[0]
    return dict(
        mine=((2, plan.peers, wide_part, rows, 128), BF),
        pair=((plan.peers, wide_part, rows, 128), BF),
        both=((plan.peers, wide_part, rows, 128), BF),
        peers=((plan.peers, wide_part, rows, 128), BF),
        own=((wide_part, rows, 128), F32),
        plane=((wide_part, rows, 128), BF),
        line=((plan.line, rows, 128), BF),
    )


def reduce_sems(plan):
    return pltpu.SemaphoreType.DMA((2, 2 * plan.peers + plan.line))
def vmem():
    return pl.BlockSpec(memory_space=pltpu.VMEM)


def hbm():
    return pl.BlockSpec(memory_space=pl.ANY)


def scratch(*dicts):
    shapes, names = [], []
    for entry in dicts:
        names.append(list(entry))
        shapes += [pltpu.VMEM(*entry[name]) for name in entry]
    return shapes, names


def grouped(names, refs):
    it = iter(refs)
    return [Group(**{name: next(it) for name in entry}) for entry in names]


def shard_rows(ref, rows):
    fill = jnp.zeros((rows * 128 - ref.shape[0],), F32)
    return jnp.concatenate([ref[...], fill]).reshape(rows, 128)


def call_all(works):
    for work in works:
        work()


def row_copies(source, target, sems, base, seq, row_count, out):
    copies = []
    for r in range(row_count):
        inside = target.at[:, pl.ds(r * seq, seq)]
        outside = source.at[r]
        pair = (inside, outside) if out else (outside, inside)
        copies.append(pltpu.make_async_copy(*pair, sems.at[base + r]))
    return copies


def whole_kernel(plan, lengths, names, halves, seq, row_count, *refs):
    widths, one, two, features, out_grad, activations, grad_features, out_one, out_two = refs[:9]
    sem_one, sem_two, red_early, red_late, red_two, io = refs[9:15]
    w_one, w_two, a_one, a_two, s, h, r_early, r_late, r_two = grouped(names, refs[15:])
    tokens = seq * row_count
    everything = (0, plan.line)
    plan.greet()
    loads = row_copies(features, s.input_one, io, 0, seq, row_count, False)
    loads_grad = row_copies(out_grad, s.grad_next, io, row_count, seq, row_count, False)
    for copy in loads:
        copy.start()
    live = [widths[r] for r in range(row_count)]
    for a in (a_one, a_two):
        fill_spare(a, live, seq, row_count)
    gather_one = Gather(plan, sem_one, h.one, lengths[0], halves)
    gather_two = Gather(plan, sem_two, h.two, lengths[1], halves)
    gather_one.prepare(shard_rows(one, h.one.shape[3]))
    gather_two.prepare(shard_rows(two, h.two.shape[3]))
    plan.meet()
    gather_one.begin(0)
    gather_one.spread(0)
    gather_one.begin(1)
    gather_one.mirror(0)
    gather_two.begin(0)
    gather_two.begin(1)
    for copy in loads:
        copy.wait()
    gather_one.finish(0)
    gather_one.flatten(0, h.flat)
    unpack_attention(h.flat, w_one, True, s.pair)
    rows = [pl.ds(r * seq, seq) for r in range(row_count)]
    half = HEADS // GROUP

    def project(a, w, source, leading, r):
        forward_project(s, a, w, source, leading, rows[r])

    def feed(a, w, source, target, r):
        forward_feed(s, a, w, source, target, rows[r])

    def beside(entries):
        table = {}
        for g, work in entries:
            table.setdefault(g, []).append(work)
        return {g: functools.partial(call_all, works) for g, works in table.items()}

    later = range(1, row_count)
    before = range(row_count - 1)
    job = functools.partial
    one = (a_one, w_one, s.input_one)
    two = (a_two, w_two, s.input_two)

    project(*one, True, 0)
    gather_one.spread(1)
    attend_forward(
        s,
        a_one,
        seq,
        row_count,
        {1: lambda: gather_two.spread(0), 3: lambda: gather_one.mirror(1)},
        beside([(half * r - 1, job(project, *one, True, r)) for r in later]),
    )
    gather_two.mirror(0)
    gather_one.finish(1)
    gather_two.spread(1)
    gather_one.flatten(1, h.flat)
    unpack_rest(h.flat, w_one, True, s.pair, s.tail)
    for r in range(row_count):
        feed(*one, s.input_two, r)
    gather_two.finish(0)
    gather_two.flatten(0, h.flat)
    unpack_attention(h.flat, w_two, False, s.pair)
    project(*two, False, 0)
    for copy in loads_grad:
        copy.start()

    def rest():
        gather_two.finish(1)
        gather_two.flatten(1, h.flat)
        unpack_rest(h.flat, w_two, False, s.pair, s.tail)

    attend_forward(
        s,
        a_two,
        seq,
        row_count,
        {1: lambda: gather_two.mirror(1), 2: rest},
        beside(
            [(half * r - 1, job(project, *two, False, r)) for r in later]
            + [(half * (r + 2) - 1, job(feed, *two, s.input_one, r)) for r in before]
        ),
    )
    feed(*two, s.input_one, row_count - 1)
    gather_one.drain()
    gather_two.drain()
    stores = row_copies(activations, s.input_one, io, 2 * row_count, seq, row_count, True)
    for copy in stores:
        copy.start()
    for copy in loads_grad:
        copy.wait()

    reduce_two = Reduce(plan, red_two, r_two, lengths[1], everything)
    reduce_early = Reduce(plan, red_early, r_early, lengths[0], halves[1])
    reduce_late = Reduce(plan, red_late, r_late, lengths[0], halves[0])

    def back_feed(a, w, r):
        backward_feed(s, a, w, s.grad_next, rows[r])

    def back_project(a, w, target, leading, r):
        backward_project(s, a, w, target, leading, rows[r])

    def finish_row(a, w, target, leading, r):
        round_qkv(s, rows[r])
        back_project(a, w, target, leading, r)

    def grads(a, leading):
        grads_feed(s, a, leading, h.flat, s.pair, s.tail)

    backward_begin(s)
    back_feed(a_two, w_two, 0)
    attend_backward(
        s,
        a_two,
        seq,
        row_count,
        {},
        beside(
            [(half * r - 1, job(back_feed, a_two, w_two, r)) for r in later]
            + [(half * row_count - 2, job(grads, a_two, False))]
            + [(half * (r + 2) - 1, job(finish_row, a_two, w_two, s.grad_next, False, r)) for r in before]
        ),
    )
    finish_row(a_two, w_two, s.grad_next, False, row_count - 1)
    grads_attention(s, a_two, False, h.flat, s.pair)
    reduce_two.begin(h.flat)
    backward_begin(s)
    for r in range(row_count):
        back_feed(a_one, w_one, r)
    attend_backward(
        s,
        a_one,
        seq,
        row_count,
        {
            1: reduce_two.across,
            2: lambda: reduce_early.begin(h.flat),
            3: lambda: call_all([reduce_two.along, reduce_early.across]),
        },
        beside(
            [(1, job(grads, a_one, True))]
            + [(half * (r + 2) - 1, job(finish_row, a_one, w_one, s.input_two, True, r)) for r in before]
        ),
    )
    round_qkv(s, rows[-1])
    grads_attention(s, a_one, True, h.flat, s.pair)
    reduce_late.begin(h.flat)
    back_project(a_one, w_one, s.input_two, True, row_count - 1)
    reduce_late.across()
    last = row_copies(grad_features, s.input_two, io, 3 * row_count, seq, row_count, True)
    for copy in last:
        copy.start()
    reduce_early.along()
    reduce_late.along()
    reduce_two.finish(out_two)
    for copy in stores + last:
        copy.wait()
    reduce_early.finish(out_one)
    reduce_late.finish(out_one)


def deliver_kernel(count, *refs):
    sources, targets, sems = refs[:count], refs[count : 2 * count], refs[2 * count]
    copies = [pltpu.make_async_copy(a, b, sems.at[i]) for i, (a, b) in enumerate(zip(sources, targets))]
    for copy in copies:
        copy.start()
    for copy in copies:
        copy.wait()


def deliver(arrays):
    count = len(arrays)
    return pl.pallas_call(
        functools.partial(deliver_kernel, count),
        out_shape=[jax.ShapeDtypeStruct(x.shape, x.dtype) for x in arrays],
        in_specs=[vmem()] * count,
        out_specs=[hbm()] * count,
        scratch_shapes=[pltpu.SemaphoreType.DMA((count,))],
        name="deliver",
    )(*[pltpu.with_memory_space_constraint(x, pltpu.VMEM) for x in arrays])


def on_device(plan, features, widths, params_one, params_two, out_grad):
    row_count, seq, _ = features.shape
    tokens = row_count * seq
    lengths = [params_one.shape[0], params_two.shape[0]]
    rows = [piece_rows(length) for length in lengths]
    flat_rows = [plan.count * length // 128 for length in lengths]
    room = max(2360, max(flat_rows) + max(rows) + 16) // 8 * 8
    halves = [(0, plan.line // 2), (plan.line // 2, plan.line)]
    everything = (0, plan.line)
    held = {
        name: ((2, plan.peers, plan.line, r, 128), BF) for name, r in zip(("one", "two"), rows)
    }
    kept = kept_shapes(tokens, seq, row_count)
    shapes, names = scratch(
        weight_shapes(),
        weight_shapes(),
        kept,
        {**kept, **norm_shapes(tokens)},
        shared_shapes(tokens, seq),
        {**held, "flat": ((room, 128), F32)},
        reduce_shapes(plan, rows[0], halves[1]),
        reduce_shapes(plan, rows[0], halves[0]),
        reduce_shapes(plan, rows[1], everything),
    )
    sems = [gather_sems(plan)] * 2 + [reduce_sems(plan)] * 3
    sems.append(pltpu.SemaphoreType.DMA((4 * row_count,)))
    turned = pltpu.VMEM((row_count, D, seq), F32)
    results = pl.pallas_call(
        functools.partial(whole_kernel, plan, lengths, names, halves, seq, row_count),
        out_shape=[turned, turned] + [pltpu.VMEM((r, 128), F32) for r in rows],
        in_specs=[pl.BlockSpec(memory_space=pltpu.SMEM), vmem(), vmem(), hbm(), hbm()],
        out_specs=[hbm(), hbm(), vmem(), vmem()],
        scratch_shapes=sems + shapes,
        compiler_params=pltpu.CompilerParams(
            vmem_limit_bytes=62 * 2**20, collective_id=0, has_side_effects=True
        ),
        name="blocks",
    )(widths, params_one, params_two, jnp.swapaxes(features, 1, 2), jnp.swapaxes(out_grad, 1, 2))
    activations, grad_features, grad_one, grad_two = deliver(results)
    shards = [g.reshape(-1)[:length] for g, length in zip((grad_one, grad_two), lengths)]
    return (jnp.swapaxes(activations, 1, 2), jnp.swapaxes(grad_features, 1, 2), *shards)


def solution(mesh):
    plan = Plan(dict(mesh.shape))
    rows = P(("dp", "fsdp"), None, None)
    flat = P(("dp", "fsdp"))
    return jax.shard_map(
        functools.partial(on_device, plan),
        mesh=mesh,
        in_specs=(rows, flat, flat, flat, rows),
        out_specs=(rows, rows, flat, flat),
        check_vma=False,
    )
```

```python
import functools
import math

import jax
import jax.numpy as jnp
from jax import lax
from jax.experimental import pallas as pl
from jax.experimental.pallas import tpu as pltpu
from jax.sharding import PartitionSpec as P

D = 192
HEADS = 8
FF = 256
HEAD_DIM = 24
PAD = 32
AUG = 208
HID = 272
GROUP = 4
SLOTS = 3
LAG = 2
EPS = 1e-5
MASK = -4e30
SCALE = HEAD_DIM**-0.5
LOG2E = math.log2(math.e)
MATS = 1152
BF = jnp.bfloat16
F32 = jnp.float32


def nn(left, right):
    return lax.dot_general(left, right, (((1,), (0,)), ((), ())), preferred_element_type=F32)


def nt(left, right):
    return lax.dot_general(left, right, (((1,), (1,)), ((), ())), preferred_element_type=F32)


def tn(left, right):
    return lax.dot_general(left, right, (((0,), (0,)), ((), ())), preferred_element_type=F32)


def lanes_low(rows):
    return lax.broadcasted_iota(jnp.int32, (rows, 128), 1) < 64


def half_turn(values):
    return pltpu.roll(values, 64, 1)


def read_wide(flat, start, rows, pair):
    count = rows // 2
    first = flat[pl.ds(start, count, stride=3), :]
    second = flat[pl.ds(start + 1, count, stride=3), :]
    third = half_turn(flat[pl.ds(start + 2, count, stride=3), :])
    pair[0, pl.ds(0, count, stride=2), :] = first
    pair[1, pl.ds(0, count, stride=2), :] = second
    pair[0, pl.ds(1, count, stride=2), :] = jnp.where(lanes_low(count), half_turn(second), third)
    pair[1, pl.ds(1, count, stride=2), :] = third
    return jnp.concatenate([pair[0, :rows, :], pair[1, :rows, :64]], axis=1)


def write_wide(flat, start, values, pair):
    rows = values.shape[0]
    count = rows // 2
    pair[0, :rows, :] = values[:, :128]
    pair[1, :rows, :64] = values[:, 128:]
    low = lanes_low(count)
    even_low = pair[0, pl.ds(0, count, stride=2), :]
    even_high = pair[1, pl.ds(0, count, stride=2), :]
    odd_low = half_turn(pair[0, pl.ds(1, count, stride=2), :])
    odd_high = half_turn(pair[1, pl.ds(1, count, stride=2), :])
    flat[pl.ds(start, count, stride=3), :] = even_low
    flat[pl.ds(start + 1, count, stride=3), :] = jnp.where(low, even_high, odd_low)
    flat[pl.ds(start + 2, count, stride=3), :] = jnp.where(low, odd_low, odd_high)


def vector_names(leading):
    names = ["b_query", "b_value", "b_output"]
    if not leading:
        names = names + ["gain_attn", "bias_attn"]
    return names + ["gain_ffn", "bias_ffn"]


def spread():
    row = lax.broadcasted_iota(jnp.int32, (HEADS * PAD, D), 0)
    col = lax.broadcasted_iota(jnp.int32, (HEADS * PAD, D), 1)
    inside = (row & (PAD - 1)) < HEAD_DIM
    source = (row >> 5) * HEAD_DIM + (row & (PAD - 1))
    return jnp.where(inside & (source == col), 1.0, 0.0).astype(BF)


def identity(size):
    row = lax.broadcasted_iota(jnp.int32, (size, size), 0)
    col = lax.broadcasted_iota(jnp.int32, (size, size), 1)
    return jnp.where(row == col, 1.0, 0.0).astype(BF)


def unit_entry(column):
    row = lax.broadcasted_iota(jnp.int32, (HEADS * PAD, AUG), 0)
    col = lax.broadcasted_iota(jnp.int32, (HEADS * PAD, AUG), 1)
    return jnp.where(((row & (PAD - 1)) == HEAD_DIM) & (col == column), 1.0, 0.0)


def column(row_vec):
    return jnp.broadcast_to(row_vec, (128, D)).T


def augment(matrix, bias):
    width = matrix.shape[1]
    return jnp.concatenate([matrix, bias, jnp.zeros((AUG - D - 1, width), F32)], axis=0).astype(BF)


def unpack_vectors(flat, leading, pair):
    names = vector_names(leading)
    vecs = read_wide(flat, MATS, len(names) + 1, pair)
    return {name: vecs[i : i + 1, :] for i, name in enumerate(names)}


def unpack_attention(flat, w, leading, pair):
    vec = unpack_vectors(flat, leading, pair)
    put = spread()
    zero_row = jnp.zeros((1, D), F32)
    for i, (bias, spare) in enumerate((("b_query", D), (None, D + 1), ("b_value", D))):
        mat = read_wide(flat, 288 * i, D, pair)
        aug = augment(mat, vec[bias] if bias else zero_row)
        w.qkv[i] = aug[:D]
        w.qkv_t[i] = (nt(put, aug) + unit_entry(spare)).astype(BF)
    if not leading:
        w.cols[3] = column(vec["gain_attn"])
        w.cols[4] = column(vec["bias_attn"])


def unpack_rest(flat, w, leading, pair, tail):
    names = vector_names(leading)
    vec = unpack_vectors(flat, leading, pair)
    put = spread()
    aug = augment(read_wide(flat, 864, D, pair), vec["b_output"])
    w.out_t[...] = nt(identity(D), aug).astype(BF)
    w.out_pad[...] = nn(put, aug[:D]).astype(BF)
    start = MATS + len(names) * 3 // 2
    count = 1160
    turned = half_turn(flat[pl.ds(start, count + 8), :])
    tail[:count, :] = jnp.where(lanes_low(count), turned[:count], turned[1 : count + 1])
    aug = augment(
        jnp.concatenate([tail[pl.ds(j, D, stride=4), :] for j in range(4)], axis=1),
        jnp.concatenate([tail[768 + j : 769 + j, :] for j in range(4)], axis=1),
    )
    w.inner[...] = aug[:D]
    for half in range(2):
        cols = slice(half * FF, (half + 1) * FF)
        w.inner_t[cols, :] = nt(identity(FF), aug[:, cols]).astype(BF)
    outer = read_wide(tail, 772, FF, pair).astype(BF)
    w.outer[...] = outer
    w.outer_t[...] = nt(identity(D), outer).astype(BF)
    b_outer = jnp.concatenate([tail[1156:1157, :], tail[1157:1158, :64]], axis=1)
    w.cols[0] = column(b_outer)
    w.cols[1] = column(vec["gain_ffn"])
    w.cols[2] = column(vec["bias_ffn"])


class Group:
    def __init__(self, **refs):
        self.__dict__.update(refs)


def wide(col, cols):
    return jnp.concatenate([col] * (cols.size // 128), axis=1)


def norm(values):
    center = values - jnp.sum(values, axis=0, keepdims=True) * (1.0 / D)
    inverse = lax.rsqrt(jnp.sum(center * center, axis=0, keepdims=True) * (1.0 / D) + EPS)
    return center * inverse, inverse


def norm_back(grad, normed, inverse, gain):
    scaled = grad * gain
    mean = jnp.sum(scaled, axis=0, keepdims=True) * (1.0 / D)
    cross = jnp.sum(scaled * normed, axis=0, keepdims=True) * (1.0 / D)
    return inverse * (scaled - mean - normed * cross)


def place(u, seq):
    row, head = divmod(u, HEADS)
    return head, pl.ds(head * PAD, PAD), pl.ds(head * HEAD_DIM, HEAD_DIM), pl.ds(row * seq, seq)


def grouped_units(units, body, hooks, beside):
    always = lax.axis_index("dp") >= 0
    for g in range(units // GROUP):
        hooks.get(g, lambda: None)()

        @pl.when(always)
        def _():
            beside.get(g, lambda: None)()
            for j in range(GROUP):
                body(g * GROUP + j)


def attend_forward(s, a, seq, row_count, hooks, beside):
    units = row_count * HEADS

    def score(u, slot):
        _, rows, _, cols = place(u, seq)
        key = a.key[rows, cols]
        keys = jnp.concatenate([key, key], axis=0)
        query = jnp.concatenate([s.high[rows, cols], s.low[rows, cols]], axis=0)
        scores = tn(keys, query)
        s.scores[slot] = scores
        s.top[slot] = jnp.max(scores, axis=0, keepdims=True)

    def expo(u, slot):
        a.expo[u] = jnp.exp2(s.scores[slot] - s.top[slot]).astype(BF)

    def mix(u):
        head, rows, compact, cols = place(u, seq)
        total = nn(a.value[rows, cols], a.expo[u])
        inverse = 1.0 / total[HEAD_DIM : HEAD_DIM + 1]
        mixed = total * inverse
        a.mixed[rows, cols] = mixed
        a.total[head : head + 1, cols] = inverse
        s.compact[0, compact, cols] = mixed[:HEAD_DIM]

    def body(u):
        if u > LAG:
            mix(u - LAG - 1)
        if u >= LAG:
            expo(u - LAG, (u - LAG) % SLOTS)
        score(u, u % SLOTS)

    grouped_units(units, body, hooks, beside)
    for u in range(units - LAG - 1, units):
        mix(u)
        if u + 1 < units:
            expo(u + 1, (u + 1) % SLOTS)


def attend_backward(s, a, seq, row_count, hooks, beside):
    units = row_count * HEADS

    def score(u, slot):
        _, rows, compact, cols = place(u, seq)
        value = a.value[rows, cols]
        grad_hi = s.high[rows, cols]
        values = jnp.concatenate([value, value], axis=0)
        grads = jnp.concatenate([grad_hi, s.low[rows, cols]], axis=0)
        expo = a.expo[u]
        grad_soft = tn(values, grads)
        s.grad_scores[slot] = (grad_soft * expo.astype(F32)).astype(BF)
        s.compact[2, compact, cols] = nt(grad_hi, expo)[:HEAD_DIM]

    def back(u, slot):
        _, rows, compact, cols = place(u, seq)
        grad_scores = s.grad_scores[slot]
        s.compact[1, compact, cols] = nt(a.query[rows, cols], grad_scores)[:HEAD_DIM] * SCALE
        s.compact[0, compact, cols] = nn(a.key[rows, cols], grad_scores)[:HEAD_DIM] * SCALE

    def body(u):
        if u > 0:
            back(u - 1, (u - 1) % 2)
        score(u, u % 2)

    grouped_units(units, body, hooks, beside)
    back(units - 1, (units - 1) % 2)


def forward_project(s, a, w, source, leading, cols):
    x = source[:, cols]
    if not leading:
        normed, inverse = norm(x)
        a.normed_attn[:, cols] = normed
        a.inverse_attn[:, cols] = inverse
        x = normed * wide(w.cols[3], cols) + wide(w.cols[4], cols)
    a.attn_low[:D, cols] = x.astype(BF)
    low = a.attn_low[:, cols]
    query = nn(w.qkv_t[0], low).astype(BF)
    a.query[:, cols] = query
    scaled = query.astype(F32) * (SCALE * LOG2E)
    high = scaled.astype(BF)
    s.high[:, cols] = high
    s.low[:, cols] = (scaled - high.astype(F32)).astype(BF)
    a.key[:, cols] = nn(w.qkv_t[1], low).astype(BF)
    a.value[:, cols] = nn(w.qkv_t[2], low).astype(BF)


def forward_feed(s, a, w, source, target, cols):
    a.mixed_low[:D, cols] = s.compact[0, :, cols].astype(BF)
    middle = source[:, cols] + nn(w.out_t[...], a.mixed_low[:, cols])
    normed, inverse = norm(middle)
    a.normed_ffn[:, cols] = normed
    a.inverse_ffn[:, cols] = inverse
    a.ffn_low[:D, cols] = (normed * wide(w.cols[1], cols) + wide(w.cols[2], cols)).astype(BF)
    low = a.ffn_low[:, cols]
    linear = nn(w.inner_t[:FF, :], low)
    gate = nn(w.inner_t[FF:, :], low)
    sigmoid = 1.0 / (1.0 + jnp.exp2(gate * (-LOG2E)))
    silu = gate * sigmoid
    a.silu[:, cols] = silu
    a.slope[:, cols] = linear * sigmoid * (1.0 + gate * (1.0 - sigmoid))
    hidden = (linear * silu).astype(BF)
    a.hidden[:FF, cols] = hidden
    target[:, cols] = middle + nn(w.outer_t[...], hidden) + wide(w.cols[0], cols)


def backward_feed(s, a, w, grad, cols):
    g = grad[:, cols]
    low = g.astype(BF)
    s.grad_branch[:, cols] = low
    grad_hidden = nn(w.outer[...], low)
    grad_linear = (grad_hidden * a.silu[:, cols]).astype(BF)
    grad_gate = (grad_hidden * a.slope[:, cols]).astype(BF)
    s.grad_inner[:FF, cols] = grad_linear
    s.grad_inner[FF:, cols] = grad_gate
    u = nn(w.inner[:, :FF], grad_linear) + nn(w.inner[:, FF:], grad_gate)
    normed = a.normed_ffn[:, cols]
    s.sums[0] += fold(u * normed)
    s.sums[1] += fold(u)
    middle = g + norm_back(u, normed, a.inverse_ffn[:, cols], wide(w.cols[1], cols))
    s.grad_middle[:, cols] = middle
    low = middle.astype(BF)
    s.grad_attn[:, cols] = low
    grad_mixed = nn(w.out_pad[...], low).astype(BF).astype(F32)
    for head in range(HEADS):
        rows = slice(head * PAD, (head + 1) * PAD)
        part = grad_mixed[rows]
        dot = jnp.sum(part * a.mixed[rows, cols], axis=0, keepdims=True)
        spare = lax.broadcasted_iota(jnp.int32, part.shape, 0) == HEAD_DIM
        part = jnp.where(spare, -dot, part) * a.total[head : head + 1, cols]
        high = part.astype(BF)
        s.high[rows, cols] = high
        s.low[rows, cols] = (part - high.astype(F32)).astype(BF)


def keep_vector(s, leading, name, value):
    row = vector_names(leading).index(name)
    s.vectors[row : row + 1, :] = value


def write_vectors(s, flat, leading, pair):
    count = len(vector_names(leading))
    last = MATS + count * 3 // 2
    keep = flat[last : last + 8, :]
    write_wide(flat, MATS, s.vectors[: count + 1, :], pair)
    flat[last : last + 8, :] = keep


def grads_feed(s, a, leading, flat, pair, tail):
    names = vector_names(leading)
    grads = nt(a.hidden[...], s.grad_branch[...])
    write_wide(tail, 8 + 772, grads[:FF], pair)
    tail[8 + 1156 : 8 + 1157, :] = grads[FF : FF + 1, :128]
    tail[8 + 1157 : 8 + 1158, :64] = grads[FF : FF + 1, 128:]
    tail[8 + 1157 : 8 + 1158, 64:] = jnp.zeros((1, 64), F32)
    tail[8 + 1158 :, :] = jnp.zeros_like(tail[8 + 1158 :, :])
    grads = nt(a.ffn_low[...], s.grad_inner[...])
    for j in range(4):
        cols = slice(128 * j, 128 * j + 128)
        tail[pl.ds(8 + j, D, stride=4), :] = grads[:D, cols]
        tail[8 + 768 + j : 8 + 769 + j, :] = grads[D : D + 1, cols]
    bias_ffn = sum_lanes(s.sums[1])
    keep_vector(s, leading, "gain_ffn", sum_lanes(s.sums[0]))
    keep_vector(s, leading, "bias_ffn", bias_ffn)
    tail[7:8, 64:] = bias_ffn[:, 128:]
    start = MATS + len(names) * 3 // 2
    count = 1160
    turned = half_turn(tail[pl.ds(0, count + 8), :])
    flat[pl.ds(start, count), :] = jnp.where(
        lanes_low(count), turned[7 : 7 + count], turned[8 : 8 + count]
    )
    grads = nt(a.mixed_low[...], s.grad_attn[...])
    write_wide(flat, 864, grads[:D], pair)
    keep_vector(s, leading, "b_output", grads[D : D + 1])
    write_vectors(s, flat, leading, pair)


def grads_attention(s, a, leading, flat, pair):
    for i, bias in enumerate(("b_query", None, "b_value")):
        grads = nt(a.attn_low[...], s.grad_qkv[i])
        write_wide(flat, 288 * i, grads[:D], pair)
        if bias:
            keep_vector(s, leading, bias, grads[D : D + 1])
    if not leading:
        keep_vector(s, leading, "gain_attn", sum_lanes(s.sums[2]))
        keep_vector(s, leading, "bias_attn", sum_lanes(s.sums[3]))
    write_vectors(s, flat, leading, pair)


def backward_begin(s):
    s.sums[...] = jnp.zeros_like(s.sums)
    s.vectors[...] = jnp.zeros_like(s.vectors)


def round_qkv(s, cols):
    for i in range(3):
        s.grad_qkv[i, :, cols] = s.compact[i, :, cols].astype(BF)


def backward_project(s, a, w, target, leading, cols):
    total = nn(w.qkv[0], s.grad_qkv[0, :, cols])
    total = total + nn(w.qkv[1], s.grad_qkv[1, :, cols])
    total = total + nn(w.qkv[2], s.grad_qkv[2, :, cols])
    if not leading:
        normed = a.normed_attn[:, cols]
        s.sums[2] += fold(total * normed)
        s.sums[3] += fold(total)
        total = norm_back(total, normed, a.inverse_attn[:, cols], wide(w.cols[3], cols))
    target[:, cols] = s.grad_middle[:, cols] + total


def fold(values):
    total = values[:, :128]
    for start in range(128, values.shape[1], 128):
        total = total + values[:, start : start + 128]
    return total


def sum_lanes(values):
    return jnp.sum(values.T, axis=0, keepdims=True)


def weight_shapes():
    return dict(
        qkv=((3, D, D), BF),
        qkv_t=((3, HEADS * PAD, AUG), BF),
        out_t=((D, AUG), BF),
        out_pad=((HEADS * PAD, D), BF),
        inner=((D, 2 * FF), BF),
        inner_t=((2 * FF, AUG), BF),
        outer=((FF, D), BF),
        outer_t=((D, FF), BF),
        cols=((5, D, 128), F32),
    )


def kept_shapes(tokens, seq, row_count):
    return dict(
        attn_low=((AUG, tokens), BF),
        query=((HEADS * PAD, tokens), BF),
        key=((HEADS * PAD, tokens), BF),
        value=((HEADS * PAD, tokens), BF),
        expo=((row_count * HEADS, seq, seq), BF),
        mixed=((HEADS * PAD, tokens), F32),
        total=((HEADS, tokens), F32),
        mixed_low=((AUG, tokens), BF),
        normed_ffn=((D, tokens), F32),
        inverse_ffn=((1, tokens), F32),
        ffn_low=((AUG, tokens), BF),
        silu=((FF, tokens), F32),
        slope=((FF, tokens), F32),
        hidden=((HID, tokens), BF),
    )


def norm_shapes(tokens):
    return dict(normed_attn=((D, tokens), F32), inverse_attn=((1, tokens), F32))


def shared_shapes(tokens, seq):
    return dict(
        scores=((SLOTS, seq, seq), F32),
        top=((SLOTS, 1, seq), F32),
        grad_scores=((2, seq, seq), BF),
        compact=((3, D, tokens), F32),
        high=((HEADS * PAD, tokens), BF),
        low=((HEADS * PAD, tokens), BF),
        grad_branch=((D, tokens), BF),
        grad_inner=((2 * FF, tokens), BF),
        grad_middle=((D, tokens), F32),
        grad_attn=((D, tokens), BF),
        grad_qkv=((3, D, tokens), BF),
        sums=((4, D, 128), F32),
        vectors=((8, D), F32),
        grad_next=((D, tokens), F32),
        input_one=((D, tokens), F32),
        input_two=((D, tokens), F32),
        pair=((2, FF, 128), F32),
        tail=((1176, 128), F32),
    )


def fill_spare(group, widths, seq, row_count):
    tokens = seq * row_count
    row = lax.broadcasted_iota(jnp.int32, (AUG - D, tokens), 0)
    ones = jnp.where(row == 0, 1.0, 0.0)
    slot = lax.broadcasted_iota(jnp.int32, (AUG - D, seq), 1)
    masks = [jnp.where(slot < widths[r], 0.0, MASK) for r in range(row_count)]
    mask = jnp.where(row == 1, jnp.concatenate(masks, axis=1), 0.0)
    group.attn_low[D:, :] = (ones + mask).astype(BF)
    group.mixed_low[D:, :] = ones.astype(BF)
    group.ffn_low[D:, :] = ones.astype(BF)
    group.hidden[FF:, :] = ones.astype(BF)
MESH_ID = pl.DeviceIdType.MESH


class Plan:
    def __init__(self, mesh_shape):
        self.dp, self.fs = mesh_shape["dp"], mesh_shape["fsdp"]
        self.line = 2 ** ((self.dp.bit_length()) // 2)
        self.low = self.dp // self.line
        self.peers = self.low * self.fs // 2
        self.count = self.dp * self.fs

    def here(self):
        dp, fs = lax.axis_index("dp"), lax.axis_index("fsdp")
        half = self.fs // 2
        return dp // self.low, (dp % self.low) * half + fs // 2, fs % 2

    def device(self, hi, q, c):
        half = self.fs // 2
        return (hi * self.low + q // half, (q % half) * 2 + c)

    def shard(self, hi, q, c):
        return (hi * self.peers + q) * 2 + c

    def partners(self):
        hi, q, c = self.here()
        return (
            [self.device((hi + d) % self.line, q, c) for d in range(1, self.line)]
            + [self.device(hi, (q + d) % self.peers, c) for d in range(1, self.peers)]
            + [self.device(hi, q, 1 - c)]
        )

    def greet(self):
        barrier = pltpu.get_barrier_semaphore()
        for other in self.partners():
            pl.semaphore_signal(barrier, 1, device_id=other, device_id_type=MESH_ID)

    def meet(self):
        pl.semaphore_wait(pltpu.get_barrier_semaphore(), self.line + self.peers - 1)


def piece_rows(length):
    return -(-(length + 127) // 2048) * 16


def remote(source, target, sems, sent, received, device):
    return pltpu.make_async_remote_copy(
        source, target, sems.at[0, sent], sems.at[1, received], device_id=device, device_id_type=MESH_ID
    )


def send(source, target, sems, index, device):
    copy = remote(source, target, sems, index, index, device)
    copy.start()
    return copy


def place_shard(x, offset):
    turned = pltpu.roll(x, offset, 1)
    before = jnp.concatenate([jnp.zeros((1, 128), x.dtype), turned[:-1]], axis=0)
    lane = lax.broadcasted_iota(jnp.int32, x.shape, 1)
    return jnp.where(lane >= offset, turned, before)


def lift_shard(x, offset):
    turned = pltpu.roll(x, lax.rem(128 - offset, 128), 1)
    after = jnp.concatenate([turned[1:], turned[:1]], axis=0)
    lane = lax.broadcasted_iota(jnp.int32, x.shape, 1)
    return jnp.where(lane < 128 - offset, turned, after)


class Gather:
    def __init__(self, plan, sems, held, length, parts):
        self.plan, self.sems, self.held, self.length = plan, sems, held, length
        self.parts = parts
        self.across = [[] for _ in parts]
        self.pair = [[] for _ in parts]

    def steps(self, part):
        first, last = self.parts[part]
        if part > 0 or len(self.parts) == 1:
            return [(None, slice(first, last))]
        near = jnp.clip(self.plan.here()[0], first, last - 1)
        count = last - first
        indices = [first + lax.rem(near - first + count - k, count) for k in range(count)]
        return [(t, pl.ds(t, 1)) for t in indices]

    def base(self, part):
        p = self.plan
        return p.line + 2 * p.peers * (p.line if part else 0)

    def prepare(self, shard):
        p = self.plan
        hi, q, c = p.here()
        offset = lax.rem(p.shard(hi, q, c) * self.length, 128)
        self.held[c, q, hi] = place_shard(shard, offset).astype(BF)
        mine = self.held.at[c, q, hi]
        self.along = [
            remote(mine, mine, self.sems, d, hi, p.device((hi + d) % p.line, q, c)) for d in range(1, p.line)
        ]

    def begin(self, part):
        hi = self.plan.here()[0]
        first, last = self.parts[part]

        def start():
            for copy in self.along:
                copy.start()

        if (first, last) == (0, self.plan.line):
            start()
        else:
            pl.when((hi >= first) & (hi < last))(start)

    def await_line(self, t):
        p = self.plan
        hi, q, c = p.here()

        @pl.when(hi != t)
        def _():
            piece = self.held.at[c, q, t]
            remote(piece, piece, self.sems, 0, t, p.device(t, q, c)).wait_recv()

    def spread(self, part):
        p = self.plan
        hi, q, c = p.here()
        for k, (t, where) in enumerate(self.steps(part)):
            for index in range(*self.parts[part]) if t is None else [t]:
                self.await_line(index)
            mine = self.held.at[c, q, where]
            base = self.base(part) + 2 * p.peers * k
            self.across[part].append(
                [
                    send(mine, mine, self.sems, base + d, p.device(hi, (q + d) % p.peers, c))
                    for d in range(1, p.peers)
                ]
            )
            self.pair[part].append(send(mine, mine, self.sems, base, p.device(hi, q, 1 - c)))

    def mirror(self, part):
        p = self.plan
        hi, q, c = p.here()
        for k, (_, where) in enumerate(self.steps(part)):
            base = self.base(part) + 2 * p.peers * k + p.peers
            for d, copy in enumerate(self.across[part][k], 1):
                copy.wait_recv()
                piece = self.held.at[c, (q - d + p.peers) % p.peers, where]
                self.pair[part].append(send(piece, piece, self.sems, base + d, p.device(hi, q, 1 - c)))

    def finish(self, part):
        for copy in self.pair[part]:
            copy.wait_recv()

    def drain(self):
        for copy in self.along:
            copy.wait_send()
        for copies in self.pair + [copies for part in self.across for copies in part]:
            for copy in copies:
                copy.wait_send()

    def flatten(self, part, flat):
        p = self.plan
        rows = self.held.shape[3]
        first, last = self.parts[part]
        if part == 0:
            flat[0:8, :] = jnp.zeros((8, 128), F32)
        for hi in range(first, last):
            for q in range(p.peers):
                for c in range(2):
                    start = p.shard(hi, q, c) * self.length // 128
                    piece = self.held[c, q, hi].astype(F32)
                    flat[start : start + 1, :] += piece[:1]
                    flat[start + 1 : start + rows, :] = piece[1:]


def gather_sems(plan):
    return pltpu.SemaphoreType.DMA((2, plan.line + 2 * plan.peers * (plan.line + 1)))


class Reduce:
    def __init__(self, plan, sems, refs, length, part):
        self.plan, self.sems, self.r, self.length, self.part = plan, sems, refs, length, part

    def begin(self, flat):
        p, r = self.plan, self.r
        rows = r.mine.shape[3]
        first, last = self.part
        for hi in range(first, last):
            for q in range(p.peers):
                for c in range(2):
                    start = p.shard(hi, q, c) * self.length // 128
                    r.mine[c, q, hi - first] = flat[start : start + rows, :].astype(BF)
        hi, q, c = p.here()
        self.pair = {}
        for d in list(range(1, p.peers)) + [0]:
            peer = (q + d) % p.peers
            self.pair[d] = send(
                r.mine.at[1 - c, peer], r.pair.at[peer], self.sems, d, p.device(hi, q, 1 - c)
            )

    def join(self, d):
        p, r = self.plan, self.r
        hi, q, c = p.here()
        peer = (q + d) % p.peers
        self.pair[d].wait_recv()
        return r.mine[c, peer].astype(F32) + r.pair[peer].astype(F32)

    def across(self):
        p, r = self.plan, self.r
        hi, q, c = p.here()
        self.peers = []
        for d in range(1, p.peers):
            peer = (q + d) % p.peers
            r.both[d] = self.join(d).astype(BF)
            self.peers.append(
                send(r.both.at[d], r.peers.at[d], self.sems, p.peers + d, p.device(hi, peer, c))
            )
        r.own[...] = self.join(0)

    def lines(self):
        p, r = self.plan, self.r
        hi, q, c = p.here()
        first, last = self.part
        for t in range(first, last):
            slot = lax.rem(hi - t + p.line, p.line)
            yield t, remote(
                r.plane.at[t - first],
                r.line.at[slot],
                self.sems,
                2 * p.peers + t,
                2 * p.peers + slot,
                p.device(t, q, c),
            )

    def along(self):
        p, r = self.plan, self.r
        hi, q, c = p.here()
        total = r.own[...]
        for d, copy in enumerate(self.peers, 1):
            copy.wait_recv()
            total = total + r.peers[d].astype(F32)
        r.plane[...] = total.astype(BF)
        for t, copy in self.lines():

            @pl.when(hi != t)
            def _():
                copy.start()

    def finish(self, out):
        p, r = self.plan, self.r
        hi, q, c = p.here()
        first, last = self.part

        def collect():
            total = r.plane[hi - first].astype(F32)
            for d in range(1, p.line):
                index = 2 * p.peers + d
                source = p.device((hi + d) % p.line, q, c)
                remote(r.line.at[d], r.line.at[d], self.sems, 0, index, source).wait_recv()
                total = total + r.line[d].astype(F32)
            offset = lax.rem(p.shard(hi, q, c) * self.length, 128)
            out[...] = lift_shard(total, offset)

        if (first, last) == (0, p.line):
            collect()
        else:
            pl.when((hi >= first) & (hi < last))(collect)
        for copy in self.pair.values():
            copy.wait_send()
        for copy in self.peers:
            copy.wait_send()
        for t, copy in self.lines():

            @pl.when(hi != t)
            def _():
                copy.wait_send()


def reduce_shapes(plan, rows, part):
    wide_part = part[1] - part[0]
    return dict(
        mine=((2, plan.peers, wide_part, rows, 128), BF),
        pair=((plan.peers, wide_part, rows, 128), BF),
        both=((plan.peers, wide_part, rows, 128), BF),
        peers=((plan.peers, wide_part, rows, 128), BF),
        own=((wide_part, rows, 128), F32),
        plane=((wide_part, rows, 128), BF),
        line=((plan.line, rows, 128), BF),
    )


def reduce_sems(plan):
    return pltpu.SemaphoreType.DMA((2, 2 * plan.peers + plan.line))
def vmem():
    return pl.BlockSpec(memory_space=pltpu.VMEM)


def hbm():
    return pl.BlockSpec(memory_space=pl.ANY)


def scratch(*dicts):
    shapes, names = [], []
    for entry in dicts:
        names.append(list(entry))
        shapes += [pltpu.VMEM(*entry[name]) for name in entry]
    return shapes, names


def grouped(names, refs):
    it = iter(refs)
    return [Group(**{name: next(it) for name in entry}) for entry in names]


def shard_rows(ref, rows):
    fill = jnp.zeros((rows * 128 - ref.shape[0],), F32)
    return jnp.concatenate([ref[...], fill]).reshape(rows, 128)


def quarters(part):
    first, last = part
    middle = (first + last) // 2
    return [(first, middle), (middle, last)]


def call_all(works):
    for work in works:
        work()


def row_copies(source, target, sems, base, seq, row_count, out):
    copies = []
    for r in range(row_count):
        inside = target.at[:, pl.ds(r * seq, seq)]
        outside = source.at[r]
        pair = (inside, outside) if out else (outside, inside)
        copies.append(pltpu.make_async_copy(*pair, sems.at[base + r]))
    return copies


def whole_kernel(plan, lengths, names, halves, seq, row_count, *refs):
    widths, one, two, features, out_grad, activations, grad_features, out_one, out_two = refs[:9]
    sem_one, sem_two, red_early, red_first, red_second, red_two, io = refs[9:16]
    w_one, w_two, a_one, a_two, s, h, r_early, r_first, r_second, r_two = grouped(names, refs[16:])
    tokens = seq * row_count
    everything = (0, plan.line)
    plan.greet()
    loads = row_copies(features, s.input_one, io, 0, seq, row_count, False)
    loads_grad = row_copies(out_grad, s.grad_next, io, row_count, seq, row_count, False)
    for copy in loads:
        copy.start()
    live = [widths[r] for r in range(row_count)]
    for a in (a_one, a_two):
        fill_spare(a, live, seq, row_count)
    gather_one = Gather(plan, sem_one, h.one, lengths[0], halves)
    gather_two = Gather(plan, sem_two, h.two, lengths[1], halves)
    gather_one.prepare(shard_rows(one, h.one.shape[3]))
    gather_two.prepare(shard_rows(two, h.two.shape[3]))
    plan.meet()
    gather_one.begin(0)
    gather_one.spread(0)
    gather_one.begin(1)
    gather_one.mirror(0)
    gather_two.begin(0)
    gather_two.begin(1)
    for copy in loads:
        copy.wait()
    gather_one.finish(0)
    gather_one.flatten(0, h.flat)
    unpack_attention(h.flat, w_one, True, s.pair)
    rows = [pl.ds(r * seq, seq) for r in range(row_count)]
    half = HEADS // GROUP

    def project(a, w, source, leading, r):
        forward_project(s, a, w, source, leading, rows[r])

    def feed(a, w, source, target, r):
        forward_feed(s, a, w, source, target, rows[r])

    def beside(entries):
        table = {}
        for g, work in entries:
            table.setdefault(g, []).append(work)
        return {g: functools.partial(call_all, works) for g, works in table.items()}

    later = range(1, row_count)
    before = range(row_count - 1)
    job = functools.partial
    one = (a_one, w_one, s.input_one)
    two = (a_two, w_two, s.input_two)

    project(*one, True, 0)
    gather_one.spread(1)
    attend_forward(
        s,
        a_one,
        seq,
        row_count,
        {1: lambda: gather_two.spread(0), 3: lambda: gather_one.mirror(1)},
        beside([(half * r - 1, job(project, *one, True, r)) for r in later]),
    )
    gather_two.mirror(0)
    gather_one.finish(1)
    gather_two.spread(1)
    gather_one.flatten(1, h.flat)
    unpack_rest(h.flat, w_one, True, s.pair, s.tail)
    for r in range(row_count):
        feed(*one, s.input_two, r)
    gather_two.finish(0)
    gather_two.flatten(0, h.flat)
    unpack_attention(h.flat, w_two, False, s.pair)
    project(*two, False, 0)
    for copy in loads_grad:
        copy.start()

    def rest():
        gather_two.finish(1)
        gather_two.flatten(1, h.flat)
        unpack_rest(h.flat, w_two, False, s.pair, s.tail)

    attend_forward(
        s,
        a_two,
        seq,
        row_count,
        {1: lambda: gather_two.mirror(1), 2: rest},
        beside(
            [(half * r - 1, job(project, *two, False, r)) for r in later]
            + [(half * (r + 2) - 1, job(feed, *two, s.input_one, r)) for r in before]
        ),
    )
    feed(*two, s.input_one, row_count - 1)
    gather_one.drain()
    gather_two.drain()
    stores = row_copies(activations, s.input_one, io, 2 * row_count, seq, row_count, True)
    for copy in stores:
        copy.start()
    for copy in loads_grad:
        copy.wait()

    reduce_two = Reduce(plan, red_two, r_two, lengths[1], everything)
    reduce_early = Reduce(plan, red_early, r_early, lengths[0], halves[1])
    reduce_late = [
        Reduce(plan, sems, r, lengths[0], part)
        for sems, r, part in zip((red_first, red_second), (r_first, r_second), quarters(halves[0]))
    ]

    def back_feed(a, w, r):
        backward_feed(s, a, w, s.grad_next, rows[r])

    def back_project(a, w, target, leading, r):
        backward_project(s, a, w, target, leading, rows[r])

    def finish_row(a, w, target, leading, r):
        round_qkv(s, rows[r])
        back_project(a, w, target, leading, r)

    def grads(a, leading):
        grads_feed(s, a, leading, h.flat, s.pair, s.tail)

    backward_begin(s)
    back_feed(a_two, w_two, 0)
    attend_backward(
        s,
        a_two,
        seq,
        row_count,
        {},
        beside(
            [(half * r - 1, job(back_feed, a_two, w_two, r)) for r in later]
            + [(half * row_count - 2, job(grads, a_two, False))]
            + [(half * (r + 2) - 1, job(finish_row, a_two, w_two, s.grad_next, False, r)) for r in before]
        ),
    )
    finish_row(a_two, w_two, s.grad_next, False, row_count - 1)
    grads_attention(s, a_two, False, h.flat, s.pair)
    reduce_two.begin(h.flat)
    backward_begin(s)
    for r in range(row_count):
        back_feed(a_one, w_one, r)
    attend_backward(
        s,
        a_one,
        seq,
        row_count,
        {
            1: reduce_two.across,
            2: lambda: reduce_early.begin(h.flat),
            3: lambda: call_all([reduce_two.along, reduce_early.across]),
        },
        beside(
            [(1, job(grads, a_one, True))]
            + [(half * (r + 2) - 1, job(finish_row, a_one, w_one, s.input_two, True, r)) for r in before]
        ),
    )
    round_qkv(s, rows[-1])
    grads_attention(s, a_one, True, h.flat, s.pair)
    for late in reduce_late:
        late.begin(h.flat)
    back_project(a_one, w_one, s.input_two, True, row_count - 1)
    for late in reduce_late:
        late.across()
    last = row_copies(grad_features, s.input_two, io, 3 * row_count, seq, row_count, True)
    for copy in last:
        copy.start()
    for late in reduce_late:
        late.along()
    reduce_early.along()
    reduce_two.finish(out_two)
    for copy in stores + last:
        copy.wait()
    reduce_early.finish(out_one)
    for late in reduce_late:
        late.finish(out_one)


def deliver_kernel(count, *refs):
    sources, targets, sems = refs[:count], refs[count : 2 * count], refs[2 * count]
    copies = [pltpu.make_async_copy(a, b, sems.at[i]) for i, (a, b) in enumerate(zip(sources, targets))]
    for copy in copies:
        copy.start()
    for copy in copies:
        copy.wait()


def deliver(arrays):
    count = len(arrays)
    return pl.pallas_call(
        functools.partial(deliver_kernel, count),
        out_shape=[jax.ShapeDtypeStruct(x.shape, x.dtype) for x in arrays],
        in_specs=[vmem()] * count,
        out_specs=[hbm()] * count,
        scratch_shapes=[pltpu.SemaphoreType.DMA((count,))],
        compiler_params=pltpu.CompilerParams(vmem_limit_bytes=2**20),
        name="deliver",
    )(*[pltpu.with_memory_space_constraint(x, pltpu.VMEM) for x in arrays])


def on_device(plan, features, widths, params_one, params_two, out_grad):
    row_count, seq, _ = features.shape
    tokens = row_count * seq
    lengths = [params_one.shape[0], params_two.shape[0]]
    rows = [piece_rows(length) for length in lengths]
    flat_rows = [plan.count * length // 128 for length in lengths]
    room = max(2360, max(flat_rows) + max(rows) + 16) // 8 * 8
    halves = [(0, plan.line // 2), (plan.line // 2, plan.line)]
    everything = (0, plan.line)
    held = {
        name: ((2, plan.peers, plan.line, r, 128), BF) for name, r in zip(("one", "two"), rows)
    }
    kept = kept_shapes(tokens, seq, row_count)
    shapes, names = scratch(
        weight_shapes(),
        weight_shapes(),
        kept,
        {**kept, **norm_shapes(tokens)},
        shared_shapes(tokens, seq),
        {**held, "flat": ((room, 128), F32)},
        reduce_shapes(plan, rows[0], halves[1]),
        *[reduce_shapes(plan, rows[0], part) for part in quarters(halves[0])],
        reduce_shapes(plan, rows[1], everything),
    )
    sems = [gather_sems(plan)] * 2 + [reduce_sems(plan)] * 4
    sems.append(pltpu.SemaphoreType.DMA((4 * row_count,)))
    turned = pltpu.VMEM((row_count, D, seq), F32)
    results = pl.pallas_call(
        functools.partial(whole_kernel, plan, lengths, names, halves, seq, row_count),
        out_shape=[turned, turned] + [pltpu.VMEM((r, 128), F32) for r in rows],
        in_specs=[pl.BlockSpec(memory_space=pltpu.SMEM), vmem(), vmem(), hbm(), hbm()],
        out_specs=[hbm(), hbm(), vmem(), vmem()],
        scratch_shapes=sems + shapes,
        compiler_params=pltpu.CompilerParams(
            vmem_limit_bytes=62 * 2**20, collective_id=0, has_side_effects=True
        ),
        name="blocks",
    )(widths, params_one, params_two, jnp.swapaxes(features, 1, 2), jnp.swapaxes(out_grad, 1, 2))
    activations, grad_features, grad_one, grad_two = deliver(results)
    shards = [g.reshape(-1)[:length] for g, length in zip((grad_one, grad_two), lengths)]
    return (jnp.swapaxes(activations, 1, 2), jnp.swapaxes(grad_features, 1, 2), *shards)


def solution(mesh):
    plan = Plan(dict(mesh.shape))
    rows = P(("dp", "fsdp"), None, None)
    flat = P(("dp", "fsdp"))
    return jax.shard_map(
        functools.partial(on_device, plan),
        mesh=mesh,
        in_specs=(rows, flat, flat, flat, rows),
        out_specs=(rows, rows, flat, flat),
        check_vma=False,
    )
```

```python
import functools
import math

import jax
import jax.numpy as jnp
from jax import lax
from jax.experimental import pallas as pl
from jax.experimental.pallas import tpu as pltpu
from jax.sharding import PartitionSpec as P

D = 192
HEADS = 8
FF = 256
HEAD_DIM = 24
PAD = 32
AUG = 208
HID = 272
GROUP = 4
SLOTS = 3
LAG = 2
EPS = 1e-5
MASK = -4e30
SCALE = HEAD_DIM**-0.5
LOG2E = math.log2(math.e)
MATS = 1152
BF = jnp.bfloat16
F32 = jnp.float32


def nn(left, right):
    return lax.dot_general(left, right, (((1,), (0,)), ((), ())), preferred_element_type=F32)


def nt(left, right):
    return lax.dot_general(left, right, (((1,), (1,)), ((), ())), preferred_element_type=F32)


def tn(left, right):
    return lax.dot_general(left, right, (((0,), (0,)), ((), ())), preferred_element_type=F32)


def lanes_low(rows):
    return lax.broadcasted_iota(jnp.int32, (rows, 128), 1) < 64


def half_turn(values):
    return pltpu.roll(values, 64, 1)


def read_wide(flat, start, rows, pair):
    count = rows // 2
    first = flat[pl.ds(start, count, stride=3), :]
    second = flat[pl.ds(start + 1, count, stride=3), :]
    third = half_turn(flat[pl.ds(start + 2, count, stride=3), :])
    pair[0, pl.ds(0, count, stride=2), :] = first
    pair[1, pl.ds(0, count, stride=2), :] = second
    pair[0, pl.ds(1, count, stride=2), :] = jnp.where(lanes_low(count), half_turn(second), third)
    pair[1, pl.ds(1, count, stride=2), :] = third
    return jnp.concatenate([pair[0, :rows, :], pair[1, :rows, :64]], axis=1)


def write_wide(flat, start, values, pair):
    rows = values.shape[0]
    count = rows // 2
    pair[0, :rows, :] = values[:, :128]
    pair[1, :rows, :64] = values[:, 128:]
    low = lanes_low(count)
    even_low = pair[0, pl.ds(0, count, stride=2), :]
    even_high = pair[1, pl.ds(0, count, stride=2), :]
    odd_low = half_turn(pair[0, pl.ds(1, count, stride=2), :])
    odd_high = half_turn(pair[1, pl.ds(1, count, stride=2), :])
    flat[pl.ds(start, count, stride=3), :] = even_low
    flat[pl.ds(start + 1, count, stride=3), :] = jnp.where(low, even_high, odd_low)
    flat[pl.ds(start + 2, count, stride=3), :] = jnp.where(low, odd_low, odd_high)


def vector_names(leading):
    names = ["b_query", "b_value", "b_output"]
    if not leading:
        names = names + ["gain_attn", "bias_attn"]
    return names + ["gain_ffn", "bias_ffn"]


def spread():
    row = lax.broadcasted_iota(jnp.int32, (HEADS * PAD, D), 0)
    col = lax.broadcasted_iota(jnp.int32, (HEADS * PAD, D), 1)
    inside = (row & (PAD - 1)) < HEAD_DIM
    source = (row >> 5) * HEAD_DIM + (row & (PAD - 1))
    return jnp.where(inside & (source == col), 1.0, 0.0).astype(BF)


def identity(size):
    row = lax.broadcasted_iota(jnp.int32, (size, size), 0)
    col = lax.broadcasted_iota(jnp.int32, (size, size), 1)
    return jnp.where(row == col, 1.0, 0.0).astype(BF)


def unit_entry(column):
    row = lax.broadcasted_iota(jnp.int32, (HEADS * PAD, AUG), 0)
    col = lax.broadcasted_iota(jnp.int32, (HEADS * PAD, AUG), 1)
    return jnp.where(((row & (PAD - 1)) == HEAD_DIM) & (col == column), 1.0, 0.0)


def column(row_vec):
    return jnp.broadcast_to(row_vec, (128, D)).T


def augment(matrix, bias):
    width = matrix.shape[1]
    return jnp.concatenate([matrix, bias, jnp.zeros((AUG - D - 1, width), F32)], axis=0).astype(BF)


def unpack_vectors(flat, leading, pair):
    names = vector_names(leading)
    vecs = read_wide(flat, MATS, len(names) + 1, pair)
    return {name: vecs[i : i + 1, :] for i, name in enumerate(names)}


def unpack_attention(flat, w, leading, pair):
    vec = unpack_vectors(flat, leading, pair)
    put = spread()
    zero_row = jnp.zeros((1, D), F32)
    for i, (bias, spare) in enumerate((("b_query", D), (None, D + 1), ("b_value", D))):
        mat = read_wide(flat, 288 * i, D, pair)
        aug = augment(mat, vec[bias] if bias else zero_row)
        w.qkv[i] = aug[:D]
        w.qkv_t[i] = (nt(put, aug) + unit_entry(spare)).astype(BF)
    if not leading:
        w.cols[3] = column(vec["gain_attn"])
        w.cols[4] = column(vec["bias_attn"])


def unpack_rest(flat, w, leading, pair, tail):
    names = vector_names(leading)
    vec = unpack_vectors(flat, leading, pair)
    put = spread()
    aug = augment(read_wide(flat, 864, D, pair), vec["b_output"])
    w.out_t[...] = nt(identity(D), aug).astype(BF)
    w.out_pad[...] = nn(put, aug[:D]).astype(BF)
    start = MATS + len(names) * 3 // 2
    count = 1160
    turned = half_turn(flat[pl.ds(start, count + 8), :])
    tail[:count, :] = jnp.where(lanes_low(count), turned[:count], turned[1 : count + 1])
    aug = augment(
        jnp.concatenate([tail[pl.ds(j, D, stride=4), :] for j in range(4)], axis=1),
        jnp.concatenate([tail[768 + j : 769 + j, :] for j in range(4)], axis=1),
    )
    w.inner[...] = aug[:D]
    for half in range(2):
        cols = slice(half * FF, (half + 1) * FF)
        w.inner_t[cols, :] = nt(identity(FF), aug[:, cols]).astype(BF)
    outer = read_wide(tail, 772, FF, pair).astype(BF)
    w.outer[...] = outer
    w.outer_t[...] = nt(identity(D), outer).astype(BF)
    b_outer = jnp.concatenate([tail[1156:1157, :], tail[1157:1158, :64]], axis=1)
    w.cols[0] = column(b_outer)
    w.cols[1] = column(vec["gain_ffn"])
    w.cols[2] = column(vec["bias_ffn"])


class Group:
    def __init__(self, **refs):
        self.__dict__.update(refs)


def wide(col, cols):
    return jnp.concatenate([col] * (cols.size // 128), axis=1)


def norm(values):
    center = values - jnp.sum(values, axis=0, keepdims=True) * (1.0 / D)
    inverse = lax.rsqrt(jnp.sum(center * center, axis=0, keepdims=True) * (1.0 / D) + EPS)
    return center * inverse, inverse


def norm_back(grad, normed, inverse, gain):
    scaled = grad * gain
    mean = jnp.sum(scaled, axis=0, keepdims=True) * (1.0 / D)
    cross = jnp.sum(scaled * normed, axis=0, keepdims=True) * (1.0 / D)
    return inverse * (scaled - mean - normed * cross)


def place(u, seq):
    row, head = divmod(u, HEADS)
    return head, pl.ds(head * PAD, PAD), pl.ds(head * HEAD_DIM, HEAD_DIM), pl.ds(row * seq, seq)


def grouped_units(units, body, hooks, beside):
    always = lax.axis_index("dp") >= 0
    for g in range(units // GROUP):
        hooks.get(g, lambda: None)()

        @pl.when(always)
        def _():
            beside.get(g, lambda: None)()
            for j in range(GROUP):
                body(g * GROUP + j)


def attend_forward(s, a, seq, row_count, hooks, beside):
    units = row_count * HEADS

    def score(u, slot):
        _, rows, _, cols = place(u, seq)
        key = a.key[rows, cols]
        keys = jnp.concatenate([key, key], axis=0)
        query = jnp.concatenate([s.high[rows, cols], s.low[rows, cols]], axis=0)
        scores = tn(keys, query)
        s.scores[slot] = scores
        s.top[slot] = jnp.max(scores, axis=0, keepdims=True)

    def expo(u, slot):
        a.expo[u] = jnp.exp2(s.scores[slot] - s.top[slot]).astype(BF)

    def mix(u):
        head, rows, compact, cols = place(u, seq)
        total = nn(a.value[rows, cols], a.expo[u])
        inverse = 1.0 / total[HEAD_DIM : HEAD_DIM + 1]
        mixed = total * inverse
        a.mixed[rows, cols] = mixed
        a.total[head : head + 1, cols] = inverse
        s.compact[0, compact, cols] = mixed[:HEAD_DIM]

    def body(u):
        if u > LAG:
            mix(u - LAG - 1)
        if u >= LAG:
            expo(u - LAG, (u - LAG) % SLOTS)
        score(u, u % SLOTS)

    grouped_units(units, body, hooks, beside)
    for u in range(units - LAG - 1, units):
        mix(u)
        if u + 1 < units:
            expo(u + 1, (u + 1) % SLOTS)


def attend_backward(s, a, seq, row_count, hooks, beside):
    units = row_count * HEADS

    def score(u, slot):
        _, rows, compact, cols = place(u, seq)
        value = a.value[rows, cols]
        grad_hi = s.high[rows, cols]
        values = jnp.concatenate([value, value], axis=0)
        grads = jnp.concatenate([grad_hi, s.low[rows, cols]], axis=0)
        expo = a.expo[u]
        grad_soft = tn(values, grads)
        s.grad_scores[slot] = (grad_soft * expo.astype(F32)).astype(BF)
        s.compact[2, compact, cols] = nt(grad_hi, expo)[:HEAD_DIM]

    def back(u, slot):
        _, rows, compact, cols = place(u, seq)
        grad_scores = s.grad_scores[slot]
        s.compact[1, compact, cols] = nt(a.query[rows, cols], grad_scores)[:HEAD_DIM] * SCALE
        s.compact[0, compact, cols] = nn(a.key[rows, cols], grad_scores)[:HEAD_DIM] * SCALE

    def body(u):
        if u > 0:
            back(u - 1, (u - 1) % 2)
        score(u, u % 2)

    grouped_units(units, body, hooks, beside)
    back(units - 1, (units - 1) % 2)


def forward_project(s, a, w, source, leading, cols):
    x = source[:, cols]
    if not leading:
        normed, inverse = norm(x)
        a.normed_attn[:, cols] = normed
        a.inverse_attn[:, cols] = inverse
        x = normed * wide(w.cols[3], cols) + wide(w.cols[4], cols)
    a.attn_low[:D, cols] = x.astype(BF)
    low = a.attn_low[:, cols]
    query = nn(w.qkv_t[0], low).astype(BF)
    a.query[:, cols] = query
    scaled = query.astype(F32) * (SCALE * LOG2E)
    high = scaled.astype(BF)
    s.high[:, cols] = high
    s.low[:, cols] = (scaled - high.astype(F32)).astype(BF)
    a.key[:, cols] = nn(w.qkv_t[1], low).astype(BF)
    a.value[:, cols] = nn(w.qkv_t[2], low).astype(BF)


def forward_feed(s, a, w, source, target, cols):
    a.mixed_low[:D, cols] = s.compact[0, :, cols].astype(BF)
    middle = source[:, cols] + nn(w.out_t[...], a.mixed_low[:, cols])
    normed, inverse = norm(middle)
    a.normed_ffn[:, cols] = normed
    a.inverse_ffn[:, cols] = inverse
    a.ffn_low[:D, cols] = (normed * wide(w.cols[1], cols) + wide(w.cols[2], cols)).astype(BF)
    low = a.ffn_low[:, cols]
    linear = nn(w.inner_t[:FF, :], low)
    gate = nn(w.inner_t[FF:, :], low)
    sigmoid = 1.0 / (1.0 + jnp.exp2(gate * (-LOG2E)))
    silu = gate * sigmoid
    a.silu[:, cols] = silu
    a.slope[:, cols] = linear * sigmoid * (1.0 + gate * (1.0 - sigmoid))
    hidden = (linear * silu).astype(BF)
    a.hidden[:FF, cols] = hidden
    target[:, cols] = middle + nn(w.outer_t[...], hidden) + wide(w.cols[0], cols)


def backward_feed(s, a, w, grad, cols):
    g = grad[:, cols]
    low = g.astype(BF)
    s.grad_branch[:, cols] = low
    grad_hidden = nn(w.outer[...], low)
    grad_linear = (grad_hidden * a.silu[:, cols]).astype(BF)
    grad_gate = (grad_hidden * a.slope[:, cols]).astype(BF)
    s.grad_inner[:FF, cols] = grad_linear
    s.grad_inner[FF:, cols] = grad_gate
    u = nn(w.inner[:, :FF], grad_linear) + nn(w.inner[:, FF:], grad_gate)
    normed = a.normed_ffn[:, cols]
    s.sums[0] += fold(u * normed)
    s.sums[1] += fold(u)
    middle = g + norm_back(u, normed, a.inverse_ffn[:, cols], wide(w.cols[1], cols))
    s.grad_middle[:, cols] = middle
    low = middle.astype(BF)
    s.grad_attn[:, cols] = low
    grad_mixed = nn(w.out_pad[...], low).astype(BF).astype(F32)
    for head in range(HEADS):
        rows = slice(head * PAD, (head + 1) * PAD)
        part = grad_mixed[rows]
        dot = jnp.sum(part * a.mixed[rows, cols], axis=0, keepdims=True)
        spare = lax.broadcasted_iota(jnp.int32, part.shape, 0) == HEAD_DIM
        part = jnp.where(spare, -dot, part) * a.total[head : head + 1, cols]
        high = part.astype(BF)
        s.high[rows, cols] = high
        s.low[rows, cols] = (part - high.astype(F32)).astype(BF)


def keep_vector(s, leading, name, value):
    row = vector_names(leading).index(name)
    s.vectors[row : row + 1, :] = value


def write_vectors(s, flat, leading, pair):
    count = len(vector_names(leading))
    last = MATS + count * 3 // 2
    keep = flat[last : last + 8, :]
    write_wide(flat, MATS, s.vectors[: count + 1, :], pair)
    flat[last : last + 8, :] = keep


def grads_feed(s, a, leading, flat, pair, tail):
    names = vector_names(leading)
    grads = nt(a.hidden[...], s.grad_branch[...])
    write_wide(tail, 8 + 772, grads[:FF], pair)
    tail[8 + 1156 : 8 + 1157, :] = grads[FF : FF + 1, :128]
    tail[8 + 1157 : 8 + 1158, :64] = grads[FF : FF + 1, 128:]
    tail[8 + 1157 : 8 + 1158, 64:] = jnp.zeros((1, 64), F32)
    tail[8 + 1158 :, :] = jnp.zeros_like(tail[8 + 1158 :, :])
    grads = nt(a.ffn_low[...], s.grad_inner[...])
    for j in range(4):
        cols = slice(128 * j, 128 * j + 128)
        tail[pl.ds(8 + j, D, stride=4), :] = grads[:D, cols]
        tail[8 + 768 + j : 8 + 769 + j, :] = grads[D : D + 1, cols]
    bias_ffn = sum_lanes(s.sums[1])
    keep_vector(s, leading, "gain_ffn", sum_lanes(s.sums[0]))
    keep_vector(s, leading, "bias_ffn", bias_ffn)
    tail[7:8, 64:] = bias_ffn[:, 128:]
    start = MATS + len(names) * 3 // 2
    count = 1160
    turned = half_turn(tail[pl.ds(0, count + 8), :])
    flat[pl.ds(start, count), :] = jnp.where(
        lanes_low(count), turned[7 : 7 + count], turned[8 : 8 + count]
    )
    grads = nt(a.mixed_low[...], s.grad_attn[...])
    write_wide(flat, 864, grads[:D], pair)
    keep_vector(s, leading, "b_output", grads[D : D + 1])
    write_vectors(s, flat, leading, pair)


def grads_attention(s, a, leading, flat, pair):
    for i, bias in enumerate(("b_query", None, "b_value")):
        grads = nt(a.attn_low[...], s.grad_qkv[i])
        write_wide(flat, 288 * i, grads[:D], pair)
        if bias:
            keep_vector(s, leading, bias, grads[D : D + 1])
    if not leading:
        keep_vector(s, leading, "gain_attn", sum_lanes(s.sums[2]))
        keep_vector(s, leading, "bias_attn", sum_lanes(s.sums[3]))
    write_vectors(s, flat, leading, pair)


def backward_begin(s):
    s.sums[...] = jnp.zeros_like(s.sums)
    s.vectors[...] = jnp.zeros_like(s.vectors)


def round_qkv(s, cols):
    for i in range(3):
        s.grad_qkv[i, :, cols] = s.compact[i, :, cols].astype(BF)


def backward_project(s, a, w, target, leading, cols):
    total = nn(w.qkv[0], s.grad_qkv[0, :, cols])
    total = total + nn(w.qkv[1], s.grad_qkv[1, :, cols])
    total = total + nn(w.qkv[2], s.grad_qkv[2, :, cols])
    if not leading:
        normed = a.normed_attn[:, cols]
        s.sums[2] += fold(total * normed)
        s.sums[3] += fold(total)
        total = norm_back(total, normed, a.inverse_attn[:, cols], wide(w.cols[3], cols))
    target[:, cols] = s.grad_middle[:, cols] + total


def fold(values):
    total = values[:, :128]
    for start in range(128, values.shape[1], 128):
        total = total + values[:, start : start + 128]
    return total


def sum_lanes(values):
    return jnp.sum(values.T, axis=0, keepdims=True)


def weight_shapes():
    return dict(
        qkv=((3, D, D), BF),
        qkv_t=((3, HEADS * PAD, AUG), BF),
        out_t=((D, AUG), BF),
        out_pad=((HEADS * PAD, D), BF),
        inner=((D, 2 * FF), BF),
        inner_t=((2 * FF, AUG), BF),
        outer=((FF, D), BF),
        outer_t=((D, FF), BF),
        cols=((5, D, 128), F32),
    )


def kept_shapes(tokens, seq, row_count):
    return dict(
        attn_low=((AUG, tokens), BF),
        query=((HEADS * PAD, tokens), BF),
        key=((HEADS * PAD, tokens), BF),
        value=((HEADS * PAD, tokens), BF),
        expo=((row_count * HEADS, seq, seq), BF),
        mixed=((HEADS * PAD, tokens), F32),
        total=((HEADS, tokens), F32),
        mixed_low=((AUG, tokens), BF),
        normed_ffn=((D, tokens), F32),
        inverse_ffn=((1, tokens), F32),
        ffn_low=((AUG, tokens), BF),
        silu=((FF, tokens), F32),
        slope=((FF, tokens), F32),
        hidden=((HID, tokens), BF),
    )


def norm_shapes(tokens):
    return dict(normed_attn=((D, tokens), F32), inverse_attn=((1, tokens), F32))


def shared_shapes(tokens, seq):
    return dict(
        scores=((SLOTS, seq, seq), F32),
        top=((SLOTS, 1, seq), F32),
        grad_scores=((2, seq, seq), BF),
        compact=((3, D, tokens), F32),
        high=((HEADS * PAD, tokens), BF),
        low=((HEADS * PAD, tokens), BF),
        grad_branch=((D, tokens), BF),
        grad_inner=((2 * FF, tokens), BF),
        grad_middle=((D, tokens), F32),
        grad_attn=((D, tokens), BF),
        grad_qkv=((3, D, tokens), BF),
        sums=((4, D, 128), F32),
        vectors=((8, D), F32),
        grad_next=((D, tokens), F32),
        input_one=((D, tokens), F32),
        input_two=((D, tokens), F32),
        pair=((2, FF, 128), F32),
        tail=((1176, 128), F32),
    )


def fill_spare(group, widths, seq, row_count):
    tokens = seq * row_count
    row = lax.broadcasted_iota(jnp.int32, (AUG - D, tokens), 0)
    ones = jnp.where(row == 0, 1.0, 0.0)
    slot = lax.broadcasted_iota(jnp.int32, (AUG - D, seq), 1)
    masks = [jnp.where(slot < widths[r], 0.0, MASK) for r in range(row_count)]
    mask = jnp.where(row == 1, jnp.concatenate(masks, axis=1), 0.0)
    group.attn_low[D:, :] = (ones + mask).astype(BF)
    group.mixed_low[D:, :] = ones.astype(BF)
    group.ffn_low[D:, :] = ones.astype(BF)
    group.hidden[FF:, :] = ones.astype(BF)
MESH_ID = pl.DeviceIdType.MESH


class Plan:
    def __init__(self, mesh_shape):
        self.dp, self.fs = mesh_shape["dp"], mesh_shape["fsdp"]
        self.line = 2 ** ((self.dp.bit_length()) // 2)
        self.low = self.dp // self.line
        self.peers = self.low * self.fs // 2
        self.count = self.dp * self.fs

    def here(self):
        dp, fs = lax.axis_index("dp"), lax.axis_index("fsdp")
        half = self.fs // 2
        return dp // self.low, (dp % self.low) * half + fs // 2, fs % 2

    def device(self, hi, q, c):
        half = self.fs // 2
        return (hi * self.low + q // half, (q % half) * 2 + c)

    def shard(self, hi, q, c):
        return (hi * self.peers + q) * 2 + c

    def partners(self):
        hi, q, c = self.here()
        return (
            [self.device((hi + d) % self.line, q, c) for d in range(1, self.line)]
            + [self.mate(d) for d in range(1, 2 * self.peers)]
        )

    def mate(self, d):
        hi, q, c = self.here()
        other = (q * 2 + c + d) % (2 * self.peers)
        return self.device(hi, other // 2, other % 2)

    def greet(self):
        barrier = pltpu.get_barrier_semaphore()
        for other in self.partners():
            pl.semaphore_signal(barrier, 1, device_id=other, device_id_type=MESH_ID)

    def meet(self):
        pl.semaphore_wait(pltpu.get_barrier_semaphore(), self.line + 2 * self.peers - 2)


def piece_rows(length):
    return -(-(length + 127) // 2048) * 16


def remote(source, target, sems, sent, received, device):
    return pltpu.make_async_remote_copy(
        source, target, sems.at[0, sent], sems.at[1, received], device_id=device, device_id_type=MESH_ID
    )


def send(source, target, sems, index, device):
    copy = remote(source, target, sems, index, index, device)
    copy.start()
    return copy


def place_shard(x, offset):
    turned = pltpu.roll(x, offset, 1)
    before = jnp.concatenate([jnp.zeros((1, 128), x.dtype), turned[:-1]], axis=0)
    lane = lax.broadcasted_iota(jnp.int32, x.shape, 1)
    return jnp.where(lane >= offset, turned, before)


def lift_shard(x, offset):
    turned = pltpu.roll(x, lax.rem(128 - offset, 128), 1)
    after = jnp.concatenate([turned[1:], turned[:1]], axis=0)
    lane = lax.broadcasted_iota(jnp.int32, x.shape, 1)
    return jnp.where(lane < 128 - offset, turned, after)


class Gather:
    def __init__(self, plan, sems, held, length, parts, direct=False):
        self.direct = direct
        self.plan, self.sems, self.held, self.length = plan, sems, held, length
        self.parts = parts
        self.across = [[] for _ in parts]
        self.pair = [[] for _ in parts]

    def steps(self, part):
        first, last = self.parts[part]
        if part > 0 or len(self.parts) == 1:
            return [(None, slice(first, last))]
        near = jnp.clip(self.plan.here()[0], first, last - 1)
        count = last - first
        indices = [first + lax.rem(near - first + count - k, count) for k in range(count)]
        return [(t, pl.ds(t, 1)) for t in indices]

    def base(self, part):
        p = self.plan
        return p.line + 2 * p.peers * (p.line if part else 0)

    def prepare(self, shard):
        p = self.plan
        hi, q, c = p.here()
        offset = lax.rem(p.shard(hi, q, c) * self.length, 128)
        self.held[c, q, hi] = place_shard(shard, offset).astype(BF)
        mine = self.held.at[c, q, hi]
        self.along = [
            remote(mine, mine, self.sems, d, hi, p.device((hi + d) % p.line, q, c)) for d in range(1, p.line)
        ]

    def begin(self, part):
        hi = self.plan.here()[0]
        first, last = self.parts[part]

        def start():
            for copy in self.along:
                copy.start()

        if (first, last) == (0, self.plan.line):
            start()
        else:
            pl.when((hi >= first) & (hi < last))(start)

    def await_line(self, t):
        p = self.plan
        hi, q, c = p.here()

        @pl.when(hi != t)
        def _():
            piece = self.held.at[c, q, t]
            remote(piece, piece, self.sems, 0, t, p.device(t, q, c)).wait_recv()

    def spread(self, part):
        p = self.plan
        hi, q, c = p.here()
        for k, (t, where) in enumerate(self.steps(part)):
            for index in range(*self.parts[part]) if t is None else [t]:
                self.await_line(index)
            mine = self.held.at[c, q, where]
            base = self.base(part) + 2 * p.peers * k
            if self.direct and part == 0:
                self.pair[part] += [
                    send(mine, mine, self.sems, base + d, p.mate(d)) for d in range(1, 2 * p.peers)
                ]
                continue
            self.across[part].append(
                [
                    send(mine, mine, self.sems, base + d, p.device(hi, (q + d) % p.peers, c))
                    for d in range(1, p.peers)
                ]
            )
            self.pair[part].append(send(mine, mine, self.sems, base, p.device(hi, q, 1 - c)))

    def mirror(self, part):
        p = self.plan
        hi, q, c = p.here()
        for k, (_, where) in enumerate(self.steps(part)):
            if self.direct and part == 0:
                continue
            base = self.base(part) + 2 * p.peers * k + p.peers
            for d, copy in enumerate(self.across[part][k], 1):
                copy.wait_recv()
                piece = self.held.at[c, (q - d + p.peers) % p.peers, where]
                self.pair[part].append(send(piece, piece, self.sems, base + d, p.device(hi, q, 1 - c)))

    def finish(self, part):
        for copy in self.pair[part]:
            copy.wait_recv()

    def drain(self):
        for copy in self.along:
            copy.wait_send()
        for copies in self.pair + [copies for part in self.across for copies in part]:
            for copy in copies:
                copy.wait_send()

    def flatten(self, part, flat):
        p = self.plan
        first, last = self.parts[part]
        per_line = p.peers * 2

        def piece(shard):
            hi, rest = divmod(shard, per_line)
            return self.held[rest % 2, rest // 2, hi].astype(F32)

        def start(shard):
            return shard * self.length // 128

        shard, end = first * per_line, last * per_line
        before = piece(shard - 1)[start(shard) - start(shard - 1) :][:1] if shard else None
        for shard in range(shard, end):
            rows = piece(shard)
            count = start(shard + 1) - start(shard)
            head = rows[:1] if before is None else rows[:1] + before
            flat[start(shard) : start(shard) + 1, :] = head
            flat[start(shard) + 1 : start(shard + 1), :] = rows[1:count]
            before = rows[count : count + 1]
        flat[start(end) : start(end) + 1, :] = before


def gather_sems(plan):
    return pltpu.SemaphoreType.DMA((2, plan.line + 2 * plan.peers * (plan.line + 1)))


class Reduce:
    def __init__(self, plan, sems, refs, length, part):
        self.plan, self.sems, self.r, self.length, self.part = plan, sems, refs, length, part

    def pack(self, flat):
        p, r = self.plan, self.r
        rows = r.mine.shape[3]
        first, last = self.part
        for hi in range(first, last):
            for q in range(p.peers):
                for c in range(2):
                    start = p.shard(hi, q, c) * self.length // 128
                    r.mine[c, q, hi - first] = flat[start : start + rows, :].astype(BF)

    def begin_direct(self, flat):
        self.pack(flat)
        p, r = self.plan, self.r
        hi, q, c = p.here()
        self.pair, self.peers = {}, []
        for d in range(1, 2 * p.peers):
            other = (q * 2 + c + d) % (2 * p.peers)
            piece = r.mine.at[other % 2, other // 2]
            self.peers.append(send(piece, r.peers.at[d], self.sems, d, p.mate(d)))
        r.own[...] = r.mine[c, q].astype(F32)

    def begin(self, flat):
        self.pack(flat)
        p, r = self.plan, self.r
        hi, q, c = p.here()
        self.pair = {}
        for d in list(range(1, p.peers)) + [0]:
            peer = (q + d) % p.peers
            self.pair[d] = send(
                r.mine.at[1 - c, peer], r.pair.at[peer], self.sems, d, p.device(hi, q, 1 - c)
            )

    def join(self, d):
        p, r = self.plan, self.r
        hi, q, c = p.here()
        peer = (q + d) % p.peers
        self.pair[d].wait_recv()
        return r.mine[c, peer].astype(F32) + r.pair[peer].astype(F32)

    def across(self):
        p, r = self.plan, self.r
        hi, q, c = p.here()
        self.peers = []
        for d in range(1, p.peers):
            peer = (q + d) % p.peers
            r.both[d] = self.join(d).astype(BF)
            self.peers.append(
                send(r.both.at[d], r.peers.at[d], self.sems, p.peers + d, p.device(hi, peer, c))
            )
        r.own[...] = self.join(0)

    def lines(self):
        p, r = self.plan, self.r
        hi, q, c = p.here()
        first, last = self.part
        for t in range(first, last):
            slot = lax.rem(hi - t + p.line, p.line)
            yield t, remote(
                r.plane.at[t - first],
                r.line.at[slot],
                self.sems,
                2 * p.peers + t,
                2 * p.peers + slot,
                p.device(t, q, c),
            )

    def along(self):
        p, r = self.plan, self.r
        hi, q, c = p.here()
        total = r.own[...]
        for d, copy in enumerate(self.peers, 1):
            copy.wait_recv()
            total = total + r.peers[d].astype(F32)
        r.plane[...] = total.astype(BF)
        for t, copy in self.lines():

            @pl.when(hi != t)
            def _():
                copy.start()

    def finish(self, out):
        p, r = self.plan, self.r
        hi, q, c = p.here()
        first, last = self.part

        def collect():
            total = r.plane[hi - first].astype(F32)
            for d in range(1, p.line):
                index = 2 * p.peers + d
                source = p.device((hi + d) % p.line, q, c)
                remote(r.line.at[d], r.line.at[d], self.sems, 0, index, source).wait_recv()
                total = total + r.line[d].astype(F32)
            offset = lax.rem(p.shard(hi, q, c) * self.length, 128)
            out[...] = lift_shard(total, offset)

        if (first, last) == (0, p.line):
            collect()
        else:
            pl.when((hi >= first) & (hi < last))(collect)
        for copy in self.pair.values():
            copy.wait_send()
        for copy in self.peers:
            copy.wait_send()
        for t, copy in self.lines():

            @pl.when(hi != t)
            def _():
                copy.wait_send()


def reduce_shapes(plan, rows, part):
    wide_part = part[1] - part[0]
    return dict(
        mine=((2, plan.peers, wide_part, rows, 128), BF),
        pair=((plan.peers, wide_part, rows, 128), BF),
        both=((plan.peers, wide_part, rows, 128), BF),
        peers=((2 * plan.peers, wide_part, rows, 128), BF),
        own=((wide_part, rows, 128), F32),
        plane=((wide_part, rows, 128), BF),
        line=((plan.line, rows, 128), BF),
    )


def reduce_sems(plan):
    return pltpu.SemaphoreType.DMA((2, 2 * plan.peers + plan.line))
def vmem():
    return pl.BlockSpec(memory_space=pltpu.VMEM)


def hbm():
    return pl.BlockSpec(memory_space=pl.ANY)


def scratch(*dicts):
    shapes, names = [], []
    for entry in dicts:
        names.append(list(entry))
        shapes += [pltpu.VMEM(*entry[name]) for name in entry]
    return shapes, names


def grouped(names, refs):
    it = iter(refs)
    return [Group(**{name: next(it) for name in entry}) for entry in names]


def shard_rows(ref, rows):
    fill = jnp.zeros((rows * 128 - ref.shape[0],), F32)
    return jnp.concatenate([ref[...], fill]).reshape(rows, 128)


def quarters(part):
    first, last = part
    middle = (first + last) // 2
    return [(first, middle), (middle, last)]


def call_all(works):
    for work in works:
        work()


def row_copies(source, target, sems, base, seq, row_count, out):
    copies = []
    for r in range(row_count):
        inside = target.at[:, pl.ds(r * seq, seq)]
        outside = source.at[r]
        pair = (inside, outside) if out else (outside, inside)
        copies.append(pltpu.make_async_copy(*pair, sems.at[base + r]))
    return copies


def whole_kernel(plan, lengths, names, halves, seq, row_count, *refs):
    widths, one, two, features, out_grad, activations, grad_features, out_one, out_two = refs[:9]
    sem_one, sem_two, red_early, red_first, red_second, red_two, io = refs[9:16]
    w_one, w_two, a_one, a_two, s, h, r_early, r_first, r_second, r_two = grouped(names, refs[16:])
    tokens = seq * row_count
    everything = (0, plan.line)
    plan.greet()
    loads = row_copies(features, s.input_one, io, 0, seq, row_count, False)
    loads_grad = row_copies(out_grad, s.grad_next, io, row_count, seq, row_count, False)
    for copy in loads:
        copy.start()
    live = [widths[r] for r in range(row_count)]
    for a in (a_one, a_two):
        fill_spare(a, live, seq, row_count)
    gather_one = Gather(plan, sem_one, h.one, lengths[0], halves, direct=True)
    gather_two = Gather(plan, sem_two, h.two, lengths[1], halves)
    gather_one.prepare(shard_rows(one, h.one.shape[3]))
    gather_two.prepare(shard_rows(two, h.two.shape[3]))
    plan.meet()
    gather_one.begin(0)
    gather_one.begin(1)
    gather_one.spread(0)
    for copy in loads:
        copy.wait()
    gather_one.finish(0)
    gather_one.spread(1)
    gather_two.begin(0)
    gather_two.begin(1)
    gather_one.flatten(0, h.flat)
    unpack_attention(h.flat, w_one, True, s.pair)
    rows = [pl.ds(r * seq, seq) for r in range(row_count)]
    half = HEADS // GROUP

    def project(a, w, source, leading, r):
        forward_project(s, a, w, source, leading, rows[r])

    def feed(a, w, source, target, r):
        forward_feed(s, a, w, source, target, rows[r])

    def beside(entries):
        table = {}
        for g, work in entries:
            table.setdefault(g, []).append(work)
        return {g: functools.partial(call_all, works) for g, works in table.items()}

    later = range(1, row_count)
    before = range(row_count - 1)
    job = functools.partial
    one = (a_one, w_one, s.input_one)
    two = (a_two, w_two, s.input_two)

    project(*one, True, 0)
    attend_forward(
        s,
        a_one,
        seq,
        row_count,
        {2: lambda: gather_two.spread(0), 3: lambda: gather_one.mirror(1)},
        beside([(half * r - 1, job(project, *one, True, r)) for r in later]),
    )
    gather_two.mirror(0)
    gather_one.finish(1)
    gather_two.spread(1)
    gather_one.flatten(1, h.flat)
    unpack_rest(h.flat, w_one, True, s.pair, s.tail)
    for r in range(row_count):
        feed(*one, s.input_two, r)
    gather_two.finish(0)
    gather_two.flatten(0, h.flat)
    unpack_attention(h.flat, w_two, False, s.pair)
    project(*two, False, 0)
    for copy in loads_grad:
        copy.start()

    def rest():
        gather_two.finish(1)
        gather_two.flatten(1, h.flat)
        unpack_rest(h.flat, w_two, False, s.pair, s.tail)

    attend_forward(
        s,
        a_two,
        seq,
        row_count,
        {1: lambda: gather_two.mirror(1), 2: rest},
        beside(
            [(half * r - 1, job(project, *two, False, r)) for r in later]
            + [(half * (r + 2) - 1, job(feed, *two, s.input_one, r)) for r in before]
        ),
    )
    feed(*two, s.input_one, row_count - 1)
    gather_one.drain()
    gather_two.drain()
    stores = row_copies(activations, s.input_one, io, 2 * row_count, seq, row_count, True)
    for copy in stores:
        copy.start()
    for copy in loads_grad:
        copy.wait()

    reduce_two = Reduce(plan, red_two, r_two, lengths[1], everything)
    reduce_early = Reduce(plan, red_early, r_early, lengths[0], halves[1])
    reduce_late = [
        Reduce(plan, sems, r, lengths[0], part)
        for sems, r, part in zip((red_first, red_second), (r_first, r_second), quarters(halves[0]))
    ]

    def back_feed(a, w, r):
        backward_feed(s, a, w, s.grad_next, rows[r])

    def back_project(a, w, target, leading, r):
        backward_project(s, a, w, target, leading, rows[r])

    def finish_row(a, w, target, leading, r):
        round_qkv(s, rows[r])
        back_project(a, w, target, leading, r)

    def grads(a, leading):
        grads_feed(s, a, leading, h.flat, s.pair, s.tail)

    backward_begin(s)
    back_feed(a_two, w_two, 0)
    attend_backward(
        s,
        a_two,
        seq,
        row_count,
        {},
        beside(
            [(half * r - 1, job(back_feed, a_two, w_two, r)) for r in later]
            + [(half * row_count - 2, job(grads, a_two, False))]
            + [(half * (r + 2) - 1, job(finish_row, a_two, w_two, s.grad_next, False, r)) for r in before]
        ),
    )
    finish_row(a_two, w_two, s.grad_next, False, row_count - 1)
    grads_attention(s, a_two, False, h.flat, s.pair)
    reduce_two.begin(h.flat)
    backward_begin(s)
    for r in range(row_count):
        back_feed(a_one, w_one, r)
    attend_backward(
        s,
        a_one,
        seq,
        row_count,
        {
            1: reduce_two.across,
            2: lambda: reduce_early.begin(h.flat),
            3: lambda: call_all([reduce_two.along, reduce_early.across]),
        },
        beside(
            [(1, job(grads, a_one, True))]
            + [(half * (r + 2) - 1, job(round_qkv, s, rows[r])) for r in before]
        ),
    )
    round_qkv(s, rows[-1])
    grads_attention(s, a_one, True, h.flat, s.pair)
    for late in reduce_late:
        late.begin_direct(h.flat)
    for r in range(row_count):
        back_project(a_one, w_one, s.input_two, True, r)
    last = row_copies(grad_features, s.input_two, io, 3 * row_count, seq, row_count, True)
    for copy in last:
        copy.start()
    for late in reduce_late:
        late.along()
    reduce_early.along()
    reduce_two.finish(out_two)
    for copy in stores + last:
        copy.wait()
    reduce_early.finish(out_one)
    for late in reduce_late:
        late.finish(out_one)


def deliver_kernel(count, *refs):
    sources, targets, sems = refs[:count], refs[count : 2 * count], refs[2 * count]
    copies = [pltpu.make_async_copy(a, b, sems.at[i]) for i, (a, b) in enumerate(zip(sources, targets))]
    for copy in copies:
        copy.start()
    for copy in copies:
        copy.wait()


def deliver(arrays):
    count = len(arrays)
    return pl.pallas_call(
        functools.partial(deliver_kernel, count),
        out_shape=[jax.ShapeDtypeStruct(x.shape, x.dtype) for x in arrays],
        in_specs=[vmem()] * count,
        out_specs=[hbm()] * count,
        scratch_shapes=[pltpu.SemaphoreType.DMA((count,))],
        compiler_params=pltpu.CompilerParams(vmem_limit_bytes=2**20),
        name="deliver",
    )(*[pltpu.with_memory_space_constraint(x, pltpu.VMEM) for x in arrays])


def on_device(plan, features, widths, params_one, params_two, out_grad):
    row_count, seq, _ = features.shape
    tokens = row_count * seq
    lengths = [params_one.shape[0], params_two.shape[0]]
    rows = [piece_rows(length) for length in lengths]
    flat_rows = [plan.count * length // 128 for length in lengths]
    room = max(2360, max(flat_rows) + max(rows) + 16) // 8 * 8
    halves = [(0, plan.line // 2), (plan.line // 2, plan.line)]
    everything = (0, plan.line)
    held = {
        name: ((2, plan.peers, plan.line, r, 128), BF) for name, r in zip(("one", "two"), rows)
    }
    kept = kept_shapes(tokens, seq, row_count)
    shapes, names = scratch(
        weight_shapes(),
        weight_shapes(),
        kept,
        {**kept, **norm_shapes(tokens)},
        shared_shapes(tokens, seq),
        {**held, "flat": ((room, 128), F32)},
        reduce_shapes(plan, rows[0], halves[1]),
        *[reduce_shapes(plan, rows[0], part) for part in quarters(halves[0])],
        reduce_shapes(plan, rows[1], everything),
    )
    sems = [gather_sems(plan)] * 2 + [reduce_sems(plan)] * 4
    sems.append(pltpu.SemaphoreType.DMA((4 * row_count,)))
    turned = pltpu.VMEM((row_count, D, seq), F32)
    results = pl.pallas_call(
        functools.partial(whole_kernel, plan, lengths, names, halves, seq, row_count),
        out_shape=[turned, turned] + [pltpu.VMEM((r, 128), F32) for r in rows],
        in_specs=[pl.BlockSpec(memory_space=pltpu.SMEM), vmem(), vmem(), hbm(), hbm()],
        out_specs=[hbm(), hbm(), vmem(), vmem()],
        scratch_shapes=sems + shapes,
        compiler_params=pltpu.CompilerParams(
            vmem_limit_bytes=62 * 2**20, collective_id=0, has_side_effects=True
        ),
        name="blocks",
    )(widths, params_one, params_two, jnp.swapaxes(features, 1, 2), jnp.swapaxes(out_grad, 1, 2))
    activations, grad_features, grad_one, grad_two = deliver(results)
    shards = [g.reshape(-1)[:length] for g, length in zip((grad_one, grad_two), lengths)]
    return (jnp.swapaxes(activations, 1, 2), jnp.swapaxes(grad_features, 1, 2), *shards)


def solution(mesh):
    plan = Plan(dict(mesh.shape))
    rows = P(("dp", "fsdp"), None, None)
    flat = P(("dp", "fsdp"))
    return jax.shard_map(
        functools.partial(on_device, plan),
        mesh=mesh,
        in_specs=(rows, flat, flat, flat, rows),
        out_specs=(rows, rows, flat, flat),
        check_vma=False,
    )
```

```python
import functools
import math

import jax
import jax.numpy as jnp
from jax import lax
from jax.experimental import pallas as pl
from jax.experimental.pallas import tpu as pltpu
from jax.sharding import PartitionSpec as P

D = 192
HEADS = 8
FF = 256
HEAD_DIM = 24
PAD = 32
AUG = 208
HID = 272
GROUP = 4
SLOTS = 3
LAG = 2
EPS = 1e-5
MASK = -4e30
SCALE = HEAD_DIM**-0.5
LOG2E = math.log2(math.e)
MATS = 1152
BF = jnp.bfloat16
F32 = jnp.float32


def nn(left, right):
    return lax.dot_general(left, right, (((1,), (0,)), ((), ())), preferred_element_type=F32)


def nt(left, right):
    return lax.dot_general(left, right, (((1,), (1,)), ((), ())), preferred_element_type=F32)


def tn(left, right):
    return lax.dot_general(left, right, (((0,), (0,)), ((), ())), preferred_element_type=F32)


def lanes_low(rows):
    return lax.broadcasted_iota(jnp.int32, (rows, 128), 1) < 64


def half_turn(values):
    return pltpu.roll(values, 64, 1)


def read_wide(flat, start, rows, pair):
    count = rows // 2
    first = flat[pl.ds(start, count, stride=3), :]
    second = flat[pl.ds(start + 1, count, stride=3), :]
    third = half_turn(flat[pl.ds(start + 2, count, stride=3), :])
    pair[0, pl.ds(0, count, stride=2), :] = first
    pair[1, pl.ds(0, count, stride=2), :] = second
    pair[0, pl.ds(1, count, stride=2), :] = jnp.where(lanes_low(count), half_turn(second), third)
    pair[1, pl.ds(1, count, stride=2), :] = third
    return jnp.concatenate([pair[0, :rows, :], pair[1, :rows, :64]], axis=1)


def write_wide(flat, start, values, pair):
    rows = values.shape[0]
    count = rows // 2
    pair[0, :rows, :] = values[:, :128]
    pair[1, :rows, :64] = values[:, 128:]
    low = lanes_low(count)
    even_low = pair[0, pl.ds(0, count, stride=2), :]
    even_high = pair[1, pl.ds(0, count, stride=2), :]
    odd_low = half_turn(pair[0, pl.ds(1, count, stride=2), :])
    odd_high = half_turn(pair[1, pl.ds(1, count, stride=2), :])
    flat[pl.ds(start, count, stride=3), :] = even_low
    flat[pl.ds(start + 1, count, stride=3), :] = jnp.where(low, even_high, odd_low)
    flat[pl.ds(start + 2, count, stride=3), :] = jnp.where(low, odd_low, odd_high)


def vector_names(leading):
    names = ["b_query", "b_value", "b_output"]
    if not leading:
        names = names + ["gain_attn", "bias_attn"]
    return names + ["gain_ffn", "bias_ffn"]


def spread():
    row = lax.broadcasted_iota(jnp.int32, (HEADS * PAD, D), 0)
    col = lax.broadcasted_iota(jnp.int32, (HEADS * PAD, D), 1)
    inside = (row & (PAD - 1)) < HEAD_DIM
    source = (row >> 5) * HEAD_DIM + (row & (PAD - 1))
    return jnp.where(inside & (source == col), 1.0, 0.0).astype(BF)


def identity(size):
    row = lax.broadcasted_iota(jnp.int32, (size, size), 0)
    col = lax.broadcasted_iota(jnp.int32, (size, size), 1)
    return jnp.where(row == col, 1.0, 0.0).astype(BF)


def unit_entry(column):
    row = lax.broadcasted_iota(jnp.int32, (HEADS * PAD, AUG), 0)
    col = lax.broadcasted_iota(jnp.int32, (HEADS * PAD, AUG), 1)
    return jnp.where(((row & (PAD - 1)) == HEAD_DIM) & (col == column), 1.0, 0.0)


def column(row_vec):
    return jnp.broadcast_to(row_vec, (128, D)).T


def augment(matrix, bias):
    width = matrix.shape[1]
    return jnp.concatenate([matrix, bias, jnp.zeros((AUG - D - 1, width), F32)], axis=0).astype(BF)


def unpack_vectors(flat, leading, pair):
    names = vector_names(leading)
    vecs = read_wide(flat, MATS, len(names) + 1, pair)
    return {name: vecs[i : i + 1, :] for i, name in enumerate(names)}


def unpack_attention(flat, w, leading, pair):
    vec = unpack_vectors(flat, leading, pair)
    put = spread()
    zero_row = jnp.zeros((1, D), F32)
    for i, (bias, spare) in enumerate((("b_query", D), (None, D + 1), ("b_value", D))):
        mat = read_wide(flat, 288 * i, D, pair)
        aug = augment(mat, vec[bias] if bias else zero_row)
        w.qkv[i] = aug[:D]
        w.qkv_t[i] = (nt(put, aug) + unit_entry(spare)).astype(BF)
    if not leading:
        w.cols[3] = column(vec["gain_attn"])
        w.cols[4] = column(vec["bias_attn"])


def unpack_rest(flat, w, leading, pair, tail):
    names = vector_names(leading)
    vec = unpack_vectors(flat, leading, pair)
    put = spread()
    aug = augment(read_wide(flat, 864, D, pair), vec["b_output"])
    w.out_t[...] = nt(identity(D), aug).astype(BF)
    w.out_pad[...] = nn(put, aug[:D]).astype(BF)
    start = MATS + len(names) * 3 // 2
    count = 1160
    turned = half_turn(flat[pl.ds(start, count + 8), :])
    tail[:count, :] = jnp.where(lanes_low(count), turned[:count], turned[1 : count + 1])
    aug = augment(
        jnp.concatenate([tail[pl.ds(j, D, stride=4), :] for j in range(4)], axis=1),
        jnp.concatenate([tail[768 + j : 769 + j, :] for j in range(4)], axis=1),
    )
    w.inner[...] = aug[:D]
    for half in range(2):
        cols = slice(half * FF, (half + 1) * FF)
        w.inner_t[cols, :] = nt(identity(FF), aug[:, cols]).astype(BF)
    outer = read_wide(tail, 772, FF, pair).astype(BF)
    w.outer[...] = outer
    w.outer_t[...] = nt(identity(D), outer).astype(BF)
    b_outer = jnp.concatenate([tail[1156:1157, :], tail[1157:1158, :64]], axis=1)
    w.cols[0] = column(b_outer)
    w.cols[1] = column(vec["gain_ffn"])
    w.cols[2] = column(vec["bias_ffn"])


class Group:
    def __init__(self, **refs):
        self.__dict__.update(refs)


def wide(col, cols):
    return jnp.concatenate([col] * (cols.size // 128), axis=1)


def norm(values):
    center = values - jnp.sum(values, axis=0, keepdims=True) * (1.0 / D)
    inverse = lax.rsqrt(jnp.sum(center * center, axis=0, keepdims=True) * (1.0 / D) + EPS)
    return center * inverse, inverse


def norm_back(grad, normed, inverse, gain):
    scaled = grad * gain
    mean = jnp.sum(scaled, axis=0, keepdims=True) * (1.0 / D)
    cross = jnp.sum(scaled * normed, axis=0, keepdims=True) * (1.0 / D)
    return inverse * (scaled - mean - normed * cross)


def place(u, seq):
    row, head = divmod(u, HEADS)
    return head, pl.ds(head * PAD, PAD), pl.ds(head * HEAD_DIM, HEAD_DIM), pl.ds(row * seq, seq)


def grouped_units(units, body, hooks, beside):
    always = lax.axis_index("dp") >= 0
    for g in range(units // GROUP):
        hooks.get(g, lambda: None)()

        @pl.when(always)
        def _():
            beside.get(g, lambda: None)()
            for j in range(GROUP):
                body(g * GROUP + j)


def attend_forward(s, a, seq, row_count, hooks, beside):
    units = row_count * HEADS

    def score(u, slot):
        _, rows, _, cols = place(u, seq)
        key = a.key[rows, cols]
        keys = jnp.concatenate([key, key], axis=0)
        query = jnp.concatenate([s.high[rows, cols], s.low[rows, cols]], axis=0)
        scores = tn(keys, query)
        s.scores[slot] = scores
        s.top[slot] = jnp.max(scores, axis=0, keepdims=True)

    def expo(u, slot):
        a.expo[u] = jnp.exp2(s.scores[slot] - s.top[slot]).astype(BF)

    def mix(u):
        head, rows, compact, cols = place(u, seq)
        total = nn(a.value[rows, cols], a.expo[u])
        inverse = 1.0 / total[HEAD_DIM : HEAD_DIM + 1]
        mixed = total * inverse
        a.mixed[rows, cols] = mixed
        a.total[head : head + 1, cols] = inverse
        s.compact[0, compact, cols] = mixed[:HEAD_DIM]

    def body(u):
        if u > LAG:
            mix(u - LAG - 1)
        if u >= LAG:
            expo(u - LAG, (u - LAG) % SLOTS)
        score(u, u % SLOTS)

    grouped_units(units, body, hooks, beside)
    for u in range(units - LAG - 1, units):
        mix(u)
        if u + 1 < units:
            expo(u + 1, (u + 1) % SLOTS)


def attend_backward(s, a, seq, row_count, hooks, beside):
    units = row_count * HEADS

    def score(u, slot):
        _, rows, compact, cols = place(u, seq)
        value = a.value[rows, cols]
        grad_hi = s.high[rows, cols]
        values = jnp.concatenate([value, value], axis=0)
        grads = jnp.concatenate([grad_hi, s.low[rows, cols]], axis=0)
        expo = a.expo[u]
        grad_soft = tn(values, grads)
        s.grad_scores[slot] = (grad_soft * expo.astype(F32)).astype(BF)
        s.compact[2, compact, cols] = nt(grad_hi, expo)[:HEAD_DIM]

    def back(u, slot):
        _, rows, compact, cols = place(u, seq)
        grad_scores = s.grad_scores[slot]
        s.compact[1, compact, cols] = nt(a.query[rows, cols], grad_scores)[:HEAD_DIM] * SCALE
        s.compact[0, compact, cols] = nn(a.key[rows, cols], grad_scores)[:HEAD_DIM] * SCALE

    def body(u):
        if u > 0:
            back(u - 1, (u - 1) % 2)
        score(u, u % 2)

    grouped_units(units, body, hooks, beside)
    back(units - 1, (units - 1) % 2)


def forward_project(s, a, w, source, leading, cols):
    x = source[:, cols]
    if not leading:
        normed, inverse = norm(x)
        a.normed_attn[:, cols] = normed
        a.inverse_attn[:, cols] = inverse
        x = normed * wide(w.cols[3], cols) + wide(w.cols[4], cols)
    a.attn_low[:D, cols] = x.astype(BF)
    low = a.attn_low[:, cols]
    query = nn(w.qkv_t[0], low).astype(BF)
    a.query[:, cols] = query
    scaled = query.astype(F32) * (SCALE * LOG2E)
    high = scaled.astype(BF)
    s.high[:, cols] = high
    s.low[:, cols] = (scaled - high.astype(F32)).astype(BF)
    a.key[:, cols] = nn(w.qkv_t[1], low).astype(BF)
    a.value[:, cols] = nn(w.qkv_t[2], low).astype(BF)


def forward_feed(s, a, w, source, target, cols):
    a.mixed_low[:D, cols] = s.compact[0, :, cols].astype(BF)
    middle = source[:, cols] + nn(w.out_t[...], a.mixed_low[:, cols])
    normed, inverse = norm(middle)
    a.normed_ffn[:, cols] = normed
    a.inverse_ffn[:, cols] = inverse
    a.ffn_low[:D, cols] = (normed * wide(w.cols[1], cols) + wide(w.cols[2], cols)).astype(BF)
    low = a.ffn_low[:, cols]
    linear = nn(w.inner_t[:FF, :], low)
    gate = nn(w.inner_t[FF:, :], low)
    sigmoid = 1.0 / (1.0 + jnp.exp2(gate * (-LOG2E)))
    silu = gate * sigmoid
    a.silu[:, cols] = silu
    a.slope[:, cols] = linear * sigmoid * (1.0 + gate * (1.0 - sigmoid))
    hidden = (linear * silu).astype(BF)
    a.hidden[:FF, cols] = hidden
    target[:, cols] = middle + nn(w.outer_t[...], hidden) + wide(w.cols[0], cols)


def backward_feed(s, a, w, grad, cols):
    g = grad[:, cols]
    low = g.astype(BF)
    s.grad_branch[:, cols] = low
    grad_hidden = nn(w.outer[...], low)
    grad_linear = (grad_hidden * a.silu[:, cols]).astype(BF)
    grad_gate = (grad_hidden * a.slope[:, cols]).astype(BF)
    s.grad_inner[:FF, cols] = grad_linear
    s.grad_inner[FF:, cols] = grad_gate
    u = nn(w.inner[:, :FF], grad_linear) + nn(w.inner[:, FF:], grad_gate)
    normed = a.normed_ffn[:, cols]
    s.sums[0] += fold(u * normed)
    s.sums[1] += fold(u)
    middle = g + norm_back(u, normed, a.inverse_ffn[:, cols], wide(w.cols[1], cols))
    s.grad_middle[:, cols] = middle
    low = middle.astype(BF)
    s.grad_attn[:, cols] = low
    grad_mixed = nn(w.out_pad[...], low).astype(BF).astype(F32)
    for head in range(HEADS):
        rows = slice(head * PAD, (head + 1) * PAD)
        part = grad_mixed[rows]
        dot = jnp.sum(part * a.mixed[rows, cols], axis=0, keepdims=True)
        spare = lax.broadcasted_iota(jnp.int32, part.shape, 0) == HEAD_DIM
        part = jnp.where(spare, -dot, part) * a.total[head : head + 1, cols]
        high = part.astype(BF)
        s.high[rows, cols] = high
        s.low[rows, cols] = (part - high.astype(F32)).astype(BF)


def keep_vector(s, leading, name, value):
    row = vector_names(leading).index(name)
    s.vectors[row : row + 1, :] = value


def write_vectors(s, flat, leading, pair):
    count = len(vector_names(leading))
    last = MATS + count * 3 // 2
    keep = flat[last : last + 8, :]
    write_wide(flat, MATS, s.vectors[: count + 1, :], pair)
    flat[last : last + 8, :] = keep


def grads_feed(s, a, leading, flat, pair, tail):
    names = vector_names(leading)
    grads = nt(a.hidden[...], s.grad_branch[...])
    write_wide(tail, 8 + 772, grads[:FF], pair)
    tail[8 + 1156 : 8 + 1157, :] = grads[FF : FF + 1, :128]
    tail[8 + 1157 : 8 + 1158, :64] = grads[FF : FF + 1, 128:]
    tail[8 + 1157 : 8 + 1158, 64:] = jnp.zeros((1, 64), F32)
    tail[8 + 1158 :, :] = jnp.zeros_like(tail[8 + 1158 :, :])
    grads = nt(a.ffn_low[...], s.grad_inner[...])
    for j in range(4):
        cols = slice(128 * j, 128 * j + 128)
        tail[pl.ds(8 + j, D, stride=4), :] = grads[:D, cols]
        tail[8 + 768 + j : 8 + 769 + j, :] = grads[D : D + 1, cols]
    bias_ffn = sum_lanes(s.sums[1])
    keep_vector(s, leading, "gain_ffn", sum_lanes(s.sums[0]))
    keep_vector(s, leading, "bias_ffn", bias_ffn)
    tail[7:8, 64:] = bias_ffn[:, 128:]
    start = MATS + len(names) * 3 // 2
    count = 1160
    turned = half_turn(tail[pl.ds(0, count + 8), :])
    flat[pl.ds(start, count), :] = jnp.where(
        lanes_low(count), turned[7 : 7 + count], turned[8 : 8 + count]
    )
    grads = nt(a.mixed_low[...], s.grad_attn[...])
    write_wide(flat, 864, grads[:D], pair)
    keep_vector(s, leading, "b_output", grads[D : D + 1])
    write_vectors(s, flat, leading, pair)


def grads_attention(s, a, leading, flat, pair):
    for i, bias in enumerate(("b_query", None, "b_value")):
        grads = nt(a.attn_low[...], s.grad_qkv[i])
        write_wide(flat, 288 * i, grads[:D], pair)
        if bias:
            keep_vector(s, leading, bias, grads[D : D + 1])
    if not leading:
        keep_vector(s, leading, "gain_attn", sum_lanes(s.sums[2]))
        keep_vector(s, leading, "bias_attn", sum_lanes(s.sums[3]))
    write_vectors(s, flat, leading, pair)


def backward_begin(s):
    s.sums[...] = jnp.zeros_like(s.sums)
    s.vectors[...] = jnp.zeros_like(s.vectors)


def round_qkv(s, cols):
    for i in range(3):
        s.grad_qkv[i, :, cols] = s.compact[i, :, cols].astype(BF)


def backward_project(s, a, w, target, leading, cols):
    total = nn(w.qkv[0], s.grad_qkv[0, :, cols])
    total = total + nn(w.qkv[1], s.grad_qkv[1, :, cols])
    total = total + nn(w.qkv[2], s.grad_qkv[2, :, cols])
    if not leading:
        normed = a.normed_attn[:, cols]
        s.sums[2] += fold(total * normed)
        s.sums[3] += fold(total)
        total = norm_back(total, normed, a.inverse_attn[:, cols], wide(w.cols[3], cols))
    target[:, cols] = s.grad_middle[:, cols] + total


def fold(values):
    total = values[:, :128]
    for start in range(128, values.shape[1], 128):
        total = total + values[:, start : start + 128]
    return total


def sum_lanes(values):
    return jnp.sum(values.T, axis=0, keepdims=True)


def weight_shapes():
    return dict(
        qkv=((3, D, D), BF),
        qkv_t=((3, HEADS * PAD, AUG), BF),
        out_t=((D, AUG), BF),
        out_pad=((HEADS * PAD, D), BF),
        inner=((D, 2 * FF), BF),
        inner_t=((2 * FF, AUG), BF),
        outer=((FF, D), BF),
        outer_t=((D, FF), BF),
        cols=((5, D, 128), F32),
    )


def kept_shapes(tokens, seq, row_count):
    return dict(
        attn_low=((AUG, tokens), BF),
        query=((HEADS * PAD, tokens), BF),
        key=((HEADS * PAD, tokens), BF),
        value=((HEADS * PAD, tokens), BF),
        expo=((row_count * HEADS, seq, seq), BF),
        mixed=((HEADS * PAD, tokens), F32),
        total=((HEADS, tokens), F32),
        mixed_low=((AUG, tokens), BF),
        normed_ffn=((D, tokens), F32),
        inverse_ffn=((1, tokens), F32),
        ffn_low=((AUG, tokens), BF),
        silu=((FF, tokens), F32),
        slope=((FF, tokens), F32),
        hidden=((HID, tokens), BF),
    )


def norm_shapes(tokens):
    return dict(normed_attn=((D, tokens), F32), inverse_attn=((1, tokens), F32))


def shared_shapes(tokens, seq):
    return dict(
        scores=((SLOTS, seq, seq), F32),
        top=((SLOTS, 1, seq), F32),
        grad_scores=((2, seq, seq), BF),
        compact=((3, D, tokens), F32),
        high=((HEADS * PAD, tokens), BF),
        low=((HEADS * PAD, tokens), BF),
        grad_branch=((D, tokens), BF),
        grad_inner=((2 * FF, tokens), BF),
        grad_middle=((D, tokens), F32),
        grad_attn=((D, tokens), BF),
        grad_qkv=((3, D, tokens), BF),
        sums=((4, D, 128), F32),
        vectors=((8, D), F32),
        grad_next=((D, tokens), F32),
        input_one=((D, tokens), F32),
        input_two=((D, tokens), F32),
        pair=((2, FF + 8, 128), F32),
        tail=((1176, 128), F32),
    )


def fill_spare(group, widths, seq, row_count):
    tokens = seq * row_count
    row = lax.broadcasted_iota(jnp.int32, (AUG - D, tokens), 0)
    ones = jnp.where(row == 0, 1.0, 0.0)
    slot = lax.broadcasted_iota(jnp.int32, (AUG - D, seq), 1)
    masks = [jnp.where(slot < widths[r], 0.0, MASK) for r in range(row_count)]
    mask = jnp.where(row == 1, jnp.concatenate(masks, axis=1), 0.0)
    group.attn_low[D:, :] = (ones + mask).astype(BF)
    group.mixed_low[D:, :] = ones.astype(BF)
    group.ffn_low[D:, :] = ones.astype(BF)
    group.hidden[FF:, :] = ones.astype(BF)
MESH_ID = pl.DeviceIdType.MESH


class Plan:
    def __init__(self, mesh_shape):
        self.dp, self.fs = mesh_shape["dp"], mesh_shape["fsdp"]
        self.line = 2 ** ((self.dp.bit_length()) // 2)
        self.low = self.dp // self.line
        self.peers = self.low * self.fs // 2
        self.count = self.dp * self.fs

    def here(self):
        dp, fs = lax.axis_index("dp"), lax.axis_index("fsdp")
        half = self.fs // 2
        return dp // self.low, (dp % self.low) * half + fs // 2, fs % 2

    def device(self, hi, q, c):
        half = self.fs // 2
        return (hi * self.low + q // half, (q % half) * 2 + c)

    def shard(self, hi, q, c):
        return (hi * self.peers + q) * 2 + c

    def partners(self):
        hi, q, c = self.here()
        return (
            [self.device((hi + d) % self.line, q, c) for d in range(1, self.line)]
            + [self.mate(d) for d in range(1, 2 * self.peers)]
        )

    def mate(self, d):
        hi, q, c = self.here()
        other = (q * 2 + c + d) % (2 * self.peers)
        return self.device(hi, other // 2, other % 2)

    def greet(self):
        barrier = pltpu.get_barrier_semaphore()
        for other in self.partners():
            pl.semaphore_signal(barrier, 1, device_id=other, device_id_type=MESH_ID)

    def meet(self):
        pl.semaphore_wait(pltpu.get_barrier_semaphore(), self.line + 2 * self.peers - 2)


def piece_rows(length):
    return -(-(length + 127) // 2048) * 16


def remote(source, target, sems, sent, received, device):
    return pltpu.make_async_remote_copy(
        source, target, sems.at[0, sent], sems.at[1, received], device_id=device, device_id_type=MESH_ID
    )


def send(source, target, sems, index, device):
    copy = remote(source, target, sems, index, index, device)
    copy.start()
    return copy


def place_shard(x, offset):
    turned = pltpu.roll(x, offset, 1)
    before = jnp.concatenate([jnp.zeros((1, 128), x.dtype), turned[:-1]], axis=0)
    lane = lax.broadcasted_iota(jnp.int32, x.shape, 1)
    return jnp.where(lane >= offset, turned, before)


def lift_shard(x, offset):
    turned = pltpu.roll(x, lax.rem(128 - offset, 128), 1)
    after = jnp.concatenate([turned[1:], turned[:1]], axis=0)
    lane = lax.broadcasted_iota(jnp.int32, x.shape, 1)
    return jnp.where(lane < 128 - offset, turned, after)


class Gather:
    def __init__(self, plan, sems, held, length, parts, direct=False):
        self.direct = direct
        self.plan, self.sems, self.held, self.length = plan, sems, held, length
        self.parts = parts
        self.across = [[] for _ in parts]
        self.pair = [[] for _ in parts]

    def steps(self, part):
        first, last = self.parts[part]
        if part > 0 or len(self.parts) == 1:
            return [(None, slice(first, last))]
        near = jnp.clip(self.plan.here()[0], first, last - 1)
        count = last - first
        indices = [first + lax.rem(near - first + count - k, count) for k in range(count)]
        return [(t, pl.ds(t, 1)) for t in indices]

    def base(self, part):
        p = self.plan
        return p.line + 2 * p.peers * (p.line if part else 0)

    def prepare(self, shard):
        p = self.plan
        hi, q, c = p.here()
        offset = lax.rem(p.shard(hi, q, c) * self.length, 128)
        self.held[c, q, hi] = place_shard(shard, offset).astype(BF)
        mine = self.held.at[c, q, hi]
        self.along = [
            remote(mine, mine, self.sems, d, hi, p.device((hi + d) % p.line, q, c)) for d in range(1, p.line)
        ]

    def begin(self, part):
        hi = self.plan.here()[0]
        first, last = self.parts[part]

        def start():
            for copy in self.along:
                copy.start()

        if (first, last) == (0, self.plan.line):
            start()
        else:
            pl.when((hi >= first) & (hi < last))(start)

    def await_line(self, t):
        p = self.plan
        hi, q, c = p.here()

        @pl.when(hi != t)
        def _():
            piece = self.held.at[c, q, t]
            remote(piece, piece, self.sems, 0, t, p.device(t, q, c)).wait_recv()

    def spread(self, part):
        p = self.plan
        hi, q, c = p.here()
        for k, (t, where) in enumerate(self.steps(part)):
            for index in range(*self.parts[part]) if t is None else [t]:
                self.await_line(index)
            mine = self.held.at[c, q, where]
            base = self.base(part) + 2 * p.peers * k
            if self.direct and part == 0:
                self.pair[part] += [
                    send(mine, mine, self.sems, base + d, p.mate(d)) for d in range(1, 2 * p.peers)
                ]
                continue
            self.across[part].append(
                [
                    send(mine, mine, self.sems, base + d, p.device(hi, (q + d) % p.peers, c))
                    for d in range(1, p.peers)
                ]
            )
            self.pair[part].append(send(mine, mine, self.sems, base, p.device(hi, q, 1 - c)))

    def mirror(self, part):
        p = self.plan
        hi, q, c = p.here()
        for k, (_, where) in enumerate(self.steps(part)):
            if self.direct and part == 0:
                continue
            base = self.base(part) + 2 * p.peers * k + p.peers
            for d, copy in enumerate(self.across[part][k], 1):
                copy.wait_recv()
                piece = self.held.at[c, (q - d + p.peers) % p.peers, where]
                self.pair[part].append(send(piece, piece, self.sems, base + d, p.device(hi, q, 1 - c)))

    def finish(self, part):
        for copy in self.pair[part]:
            copy.wait_recv()

    def drain(self):
        for copy in self.along:
            copy.wait_send()
        for copies in self.pair + [copies for part in self.across for copies in part]:
            for copy in copies:
                copy.wait_send()

    def flatten(self, part, flat):
        p = self.plan
        first, last = self.parts[part]
        per_line = p.peers * 2

        def piece(shard):
            hi, rest = divmod(shard, per_line)
            return self.held[rest % 2, rest // 2, hi].astype(F32)

        def start(shard):
            return shard * self.length // 128

        shard, end = first * per_line, last * per_line
        before = piece(shard - 1)[start(shard) - start(shard - 1) :][:1] if shard else None
        for shard in range(shard, end):
            rows = piece(shard)
            count = start(shard + 1) - start(shard)
            head = rows[:1] if before is None else rows[:1] + before
            flat[start(shard) : start(shard) + 1, :] = head
            flat[start(shard) + 1 : start(shard + 1), :] = rows[1:count]
            before = rows[count : count + 1]
        flat[start(end) : start(end) + 1, :] = before


def gather_sems(plan):
    return pltpu.SemaphoreType.DMA((2, plan.line + 2 * plan.peers * (plan.line + 1)))


class Reduce:
    def __init__(self, plan, sems, refs, length, part):
        self.plan, self.sems, self.r, self.length, self.part = plan, sems, refs, length, part

    def pack(self, flat):
        p, r = self.plan, self.r
        rows = r.mine.shape[3]
        first, last = self.part
        for hi in range(first, last):
            for q in range(p.peers):
                for c in range(2):
                    start = p.shard(hi, q, c) * self.length // 128
                    r.mine[c, q, hi - first] = flat[start : start + rows, :].astype(BF)

    def begin_direct(self, flat):
        self.pack(flat)
        p, r = self.plan, self.r
        hi, q, c = p.here()
        self.pair, self.peers = {}, []
        for d in range(1, 2 * p.peers):
            other = (q * 2 + c + d) % (2 * p.peers)
            piece = r.mine.at[other % 2, other // 2]
            self.peers.append(send(piece, r.peers.at[d], self.sems, d, p.mate(d)))
        r.own[...] = r.mine[c, q].astype(F32)

    def begin(self, flat):
        self.pack(flat)
        p, r = self.plan, self.r
        hi, q, c = p.here()
        self.pair = {}
        for d in list(range(1, p.peers)) + [0]:
            peer = (q + d) % p.peers
            self.pair[d] = send(
                r.mine.at[1 - c, peer], r.pair.at[peer], self.sems, d, p.device(hi, q, 1 - c)
            )

    def join(self, d):
        p, r = self.plan, self.r
        hi, q, c = p.here()
        peer = (q + d) % p.peers
        self.pair[d].wait_recv()
        return r.mine[c, peer].astype(F32) + r.pair[peer].astype(F32)

    def across(self):
        p, r = self.plan, self.r
        hi, q, c = p.here()
        self.peers = []
        for d in range(1, p.peers):
            peer = (q + d) % p.peers
            r.both[d] = self.join(d).astype(BF)
            self.peers.append(
                send(r.both.at[d], r.peers.at[d], self.sems, p.peers + d, p.device(hi, peer, c))
            )
        r.own[...] = self.join(0)

    def lines(self):
        p, r = self.plan, self.r
        hi, q, c = p.here()
        first, last = self.part
        for t in range(first, last):
            slot = lax.rem(hi - t + p.line, p.line)
            yield t, remote(
                r.plane.at[t - first],
                r.line.at[slot],
                self.sems,
                2 * p.peers + t,
                2 * p.peers + slot,
                p.device(t, q, c),
            )

    def along(self):
        p, r = self.plan, self.r
        hi, q, c = p.here()
        total = r.own[...]
        for d, copy in enumerate(self.peers, 1):
            copy.wait_recv()
            total = total + r.peers[d].astype(F32)
        r.plane[...] = total.astype(BF)
        for t, copy in self.lines():

            @pl.when(hi != t)
            def _():
                copy.start()

    def finish(self, out):
        p, r = self.plan, self.r
        hi, q, c = p.here()
        first, last = self.part

        def collect():
            total = r.plane[hi - first].astype(F32)
            for d in range(1, p.line):
                index = 2 * p.peers + d
                source = p.device((hi + d) % p.line, q, c)
                remote(r.line.at[d], r.line.at[d], self.sems, 0, index, source).wait_recv()
                total = total + r.line[d].astype(F32)
            offset = lax.rem(p.shard(hi, q, c) * self.length, 128)
            out[...] = lift_shard(total, offset)

        if (first, last) == (0, p.line):
            collect()
        else:
            pl.when((hi >= first) & (hi < last))(collect)
        for copy in self.pair.values():
            copy.wait_send()
        for copy in self.peers:
            copy.wait_send()
        for t, copy in self.lines():

            @pl.when(hi != t)
            def _():
                copy.wait_send()


def reduce_shapes(plan, rows, part):
    wide_part = part[1] - part[0]
    return dict(
        mine=((2, plan.peers, wide_part, rows, 128), BF),
        pair=((plan.peers, wide_part, rows, 128), BF),
        both=((plan.peers, wide_part, rows, 128), BF),
        peers=((2 * plan.peers, wide_part, rows, 128), BF),
        own=((wide_part, rows, 128), F32),
        plane=((wide_part, rows, 128), BF),
        line=((plan.line, rows, 128), BF),
    )


def reduce_sems(plan):
    return pltpu.SemaphoreType.DMA((2, 2 * plan.peers + plan.line))
def vmem():
    return pl.BlockSpec(memory_space=pltpu.VMEM)


def hbm():
    return pl.BlockSpec(memory_space=pl.ANY)


def scratch(*dicts):
    shapes, names = [], []
    for entry in dicts:
        names.append(list(entry))
        shapes += [pltpu.VMEM(*entry[name]) for name in entry]
    return shapes, names


def grouped(names, refs):
    it = iter(refs)
    return [Group(**{name: next(it) for name in entry}) for entry in names]


def shard_rows(ref, rows):
    fill = jnp.zeros((rows * 128 - ref.shape[0],), F32)
    return jnp.concatenate([ref[...], fill]).reshape(rows, 128)


def quarters(part):
    first, last = part
    middle = (first + last) // 2
    return [(first, middle), (middle, last)]


def call_all(works):
    for work in works:
        work()


def row_copies(source, target, sems, base, seq, row_count, out):
    copies = []
    for r in range(row_count):
        inside = target.at[:, pl.ds(r * seq, seq)]
        outside = source.at[r]
        pair = (inside, outside) if out else (outside, inside)
        copies.append(pltpu.make_async_copy(*pair, sems.at[base + r]))
    return copies


def whole_kernel(plan, lengths, names, halves, seq, row_count, *refs):
    widths, one, two, features, out_grad, activations, grad_features, out_one, out_two = refs[:9]
    sem_one, sem_two, red_early, red_first, red_second, red_two, io = refs[9:16]
    w_one, w_two, a_one, a_two, s, h, r_early, r_first, r_second, r_two = grouped(names, refs[16:])
    tokens = seq * row_count
    everything = (0, plan.line)
    plan.greet()
    loads = row_copies(features, s.input_one, io, 0, seq, row_count, False)
    loads_grad = row_copies(out_grad, s.grad_next, io, row_count, seq, row_count, False)
    for copy in loads:
        copy.start()
    live = [widths[r] for r in range(row_count)]
    for a in (a_one, a_two):
        fill_spare(a, live, seq, row_count)
    gather_one = Gather(plan, sem_one, h.one, lengths[0], halves, direct=True)
    gather_two = Gather(plan, sem_two, h.two, lengths[1], halves)
    gather_one.prepare(shard_rows(one, h.one.shape[3]))
    gather_two.prepare(shard_rows(two, h.two.shape[3]))
    plan.meet()
    gather_one.begin(0)
    gather_one.begin(1)
    gather_one.spread(0)
    for copy in loads:
        copy.wait()
    gather_one.finish(0)
    gather_one.spread(1)
    gather_two.begin(0)
    gather_two.begin(1)
    gather_one.flatten(0, h.flat)
    unpack_attention(h.flat, w_one, True, s.pair)
    rows = [pl.ds(r * seq, seq) for r in range(row_count)]
    half = HEADS // GROUP

    def project(a, w, source, leading, r):
        forward_project(s, a, w, source, leading, rows[r])

    def feed(a, w, source, target, r):
        forward_feed(s, a, w, source, target, rows[r])

    def beside(entries):
        table = {}
        for g, work in entries:
            table.setdefault(g, []).append(work)
        return {g: functools.partial(call_all, works) for g, works in table.items()}

    later = range(1, row_count)
    before = range(row_count - 1)
    job = functools.partial
    one = (a_one, w_one, s.input_one)
    two = (a_two, w_two, s.input_two)

    project(*one, True, 0)
    attend_forward(
        s,
        a_one,
        seq,
        row_count,
        {2: lambda: gather_two.spread(0), 3: lambda: gather_one.mirror(1)},
        beside([(half * r - 1, job(project, *one, True, r)) for r in later]),
    )
    gather_two.mirror(0)
    gather_one.finish(1)
    gather_two.spread(1)
    gather_one.flatten(1, h.flat)
    unpack_rest(h.flat, w_one, True, s.pair, s.tail)
    for r in range(row_count):
        feed(*one, s.input_two, r)
    gather_two.finish(0)
    gather_two.flatten(0, h.flat)
    unpack_attention(h.flat, w_two, False, s.pair)
    project(*two, False, 0)
    for copy in loads_grad:
        copy.start()

    def rest():
        gather_two.finish(1)
        gather_two.flatten(1, h.flat)
        unpack_rest(h.flat, w_two, False, s.pair, s.tail)

    attend_forward(
        s,
        a_two,
        seq,
        row_count,
        {1: lambda: gather_two.mirror(1), 2: rest},
        beside(
            [(half * r - 1, job(project, *two, False, r)) for r in later]
            + [(half * (r + 2) - 1, job(feed, *two, s.input_one, r)) for r in before]
        ),
    )
    feed(*two, s.input_one, row_count - 1)
    gather_one.drain()
    gather_two.drain()
    stores = row_copies(activations, s.input_one, io, 2 * row_count, seq, row_count, True)
    for copy in stores:
        copy.start()
    for copy in loads_grad:
        copy.wait()

    reduce_two = Reduce(plan, red_two, r_two, lengths[1], everything)
    reduce_early = Reduce(plan, red_early, r_early, lengths[0], halves[1])
    reduce_late = [
        Reduce(plan, sems, r, lengths[0], part)
        for sems, r, part in zip((red_first, red_second), (r_first, r_second), quarters(halves[0]))
    ]

    def back_feed(a, w, r):
        backward_feed(s, a, w, s.grad_next, rows[r])

    def back_project(a, w, target, leading, r):
        backward_project(s, a, w, target, leading, rows[r])

    def finish_row(a, w, target, leading, r):
        round_qkv(s, rows[r])
        back_project(a, w, target, leading, r)

    def grads(a, leading):
        grads_feed(s, a, leading, h.flat, s.pair, s.tail)

    backward_begin(s)
    back_feed(a_two, w_two, 0)
    attend_backward(
        s,
        a_two,
        seq,
        row_count,
        {},
        beside(
            [(half * r - 1, job(back_feed, a_two, w_two, r)) for r in later]
            + [(half * row_count - 2, job(grads, a_two, False))]
            + [(half * (r + 2) - 1, job(finish_row, a_two, w_two, s.grad_next, False, r)) for r in before]
        ),
    )
    finish_row(a_two, w_two, s.grad_next, False, row_count - 1)
    grads_attention(s, a_two, False, h.flat, s.pair)
    reduce_two.begin(h.flat)
    backward_begin(s)
    for r in range(row_count):
        back_feed(a_one, w_one, r)
    attend_backward(
        s,
        a_one,
        seq,
        row_count,
        {
            1: reduce_two.across,
            2: lambda: reduce_early.begin(h.flat),
            3: lambda: call_all([reduce_two.along, reduce_early.across]),
        },
        beside(
            [(1, job(grads, a_one, True))]
            + [(half * (r + 2) - 1, job(round_qkv, s, rows[r])) for r in before]
        ),
    )
    round_qkv(s, rows[-1])
    grads_attention(s, a_one, True, h.flat, s.pair)
    for late in reduce_late:
        late.begin_direct(h.flat)
    for r in range(row_count):
        back_project(a_one, w_one, s.input_two, True, r)
    last = row_copies(grad_features, s.input_two, io, 3 * row_count, seq, row_count, True)
    for copy in last:
        copy.start()
    for late in reduce_late:
        late.along()
    reduce_early.along()
    reduce_two.finish(out_two)
    for copy in stores + last:
        copy.wait()
    reduce_early.finish(out_one)
    for late in reduce_late:
        late.finish(out_one)


def deliver_kernel(count, *refs):
    sources, targets, sems = refs[:count], refs[count : 2 * count], refs[2 * count]
    copies = [pltpu.make_async_copy(a, b, sems.at[i]) for i, (a, b) in enumerate(zip(sources, targets))]
    for copy in copies:
        copy.start()
    for copy in copies:
        copy.wait()


def deliver(arrays):
    count = len(arrays)
    return pl.pallas_call(
        functools.partial(deliver_kernel, count),
        out_shape=[jax.ShapeDtypeStruct(x.shape, x.dtype) for x in arrays],
        in_specs=[vmem()] * count,
        out_specs=[hbm()] * count,
        scratch_shapes=[pltpu.SemaphoreType.DMA((count,))],
        compiler_params=pltpu.CompilerParams(vmem_limit_bytes=2**20),
        name="deliver",
    )(*[pltpu.with_memory_space_constraint(x, pltpu.VMEM) for x in arrays])


def on_device(plan, features, widths, params_one, params_two, out_grad):
    row_count, seq, _ = features.shape
    tokens = row_count * seq
    lengths = [params_one.shape[0], params_two.shape[0]]
    rows = [piece_rows(length) for length in lengths]
    flat_rows = [plan.count * length // 128 for length in lengths]
    room = max(2360, max(flat_rows) + max(rows) + 16) // 8 * 8
    halves = [(0, plan.line // 2), (plan.line // 2, plan.line)]
    everything = (0, plan.line)
    held = {
        name: ((2, plan.peers, plan.line, r, 128), BF) for name, r in zip(("one", "two"), rows)
    }
    kept = kept_shapes(tokens, seq, row_count)
    shapes, names = scratch(
        weight_shapes(),
        weight_shapes(),
        kept,
        {**kept, **norm_shapes(tokens)},
        shared_shapes(tokens, seq),
        {**held, "flat": ((room, 128), F32)},
        reduce_shapes(plan, rows[0], halves[1]),
        *[reduce_shapes(plan, rows[0], part) for part in quarters(halves[0])],
        reduce_shapes(plan, rows[1], everything),
    )
    sems = [gather_sems(plan)] * 2 + [reduce_sems(plan)] * 4
    sems.append(pltpu.SemaphoreType.DMA((4 * row_count,)))
    turned = pltpu.VMEM((row_count, D, seq), F32)
    results = pl.pallas_call(
        functools.partial(whole_kernel, plan, lengths, names, halves, seq, row_count),
        out_shape=[turned, turned] + [pltpu.VMEM((r, 128), F32) for r in rows],
        in_specs=[pl.BlockSpec(memory_space=pltpu.SMEM), vmem(), vmem(), hbm(), hbm()],
        out_specs=[hbm(), hbm(), vmem(), vmem()],
        scratch_shapes=sems + shapes,
        compiler_params=pltpu.CompilerParams(
            vmem_limit_bytes=62 * 2**20, collective_id=0, has_side_effects=True
        ),
        name="blocks",
    )(widths, params_one, params_two, jnp.swapaxes(features, 1, 2), jnp.swapaxes(out_grad, 1, 2))
    activations, grad_features, grad_one, grad_two = deliver(results)
    shards = [g.reshape(-1)[:length] for g, length in zip((grad_one, grad_two), lengths)]
    return (jnp.swapaxes(activations, 1, 2), jnp.swapaxes(grad_features, 1, 2), *shards)


def solution(mesh):
    plan = Plan(dict(mesh.shape))
    rows = P(("dp", "fsdp"), None, None)
    flat = P(("dp", "fsdp"))
    return jax.shard_map(
        functools.partial(on_device, plan),
        mesh=mesh,
        in_specs=(rows, flat, flat, flat, rows),
        out_specs=(rows, rows, flat, flat),
        check_vma=False,
    )
```
